32 devices in a mesh: pole: 2 (over x), row: 8 (over z, y), col: 2 (over core).
Axes of the slice: x: 2, y: 2, z: 4, core: 2. Of those that a mesh axis runs over, the one named last changes fastest.
Arguments:
- inverse_pairs: bfloat16 [4, 12288, 12288], P('pole', 'row', 'col'), parts along dimension 0, may hold values from -0.09375 to 0.09375
- factor_rows: bfloat16 [4, 2, 2048, 256], P('pole', None, 'row', 'col'), parts along dimension 0, may hold values from -1.1953125 to 1.1953125
- diag_blocks: bfloat16 [4, 2, 256, 256], P('pole', None, None, 'col'), parts along dimension 0, may hold values from -6 to 6
- row_lists: int32 [2, 16], replicated, may hold values from 0 to 95, as said below
- block_order: int32 [96], replicated, may hold values from 0 to 95, each once
Outputs:
- inv_cols: float32 [4, 2, 12288, 256], P('pole', None, 'row', 'col'), parts along dimension 0
- schur_blocks: float32 [4, 2, 256, 256], P('pole', None, None, 'col'), parts along dimension 0
The draws below stay inside these ranges and needn't reach their ends.
There are 2 independent parts, one for each index of `pole`. The reference program is written for one: setup_inputs(seed, part) draws one part's arguments, and reference() takes and returns one part's arrays. A program takes and returns all parts, laid end to end along the dimension named above; an argument that names none is the same for every part. Nothing has to cross between parts.
Inputs may be any that keep to these rules, and one draw needn't show every extreme that they name: `row_lists`: each of the 2 rows holds 16 different block numbers in increasing order, always including 0 and 95.
All inputs are finite; a program needn't handle non-finite values.
Results may differ from the reference program's by a relative error of at most 0.0003.
Values may be sent and summed in bfloat16 or wider, within the bound.
No kernel may reach another device: no remote copies, remote signals or barrier semaphores. Data moves between devices by JAX's collectives and lax.ppermute only.
A program may use at most 128 MiB of HBM per device.

```python
import jax
import jax.numpy as jnp
from jax import lax

NSN = 2
W = 256
MA = 12288
BLK = 128
R = 16
NB = 96
LROWS = 2048


def draw_row_lists(key, part):
    lists = []
    for supernode in range(NSN):
        inner = jax.random.permutation(jax.random.fold_in(key, 101 + supernode), NB - 2).astype(jnp.int32) + 1
        chosen = jnp.concatenate([jnp.zeros((1,), jnp.int32), inner[:R - 2], jnp.full((1,), NB - 1, jnp.int32)])
        lists.append(jnp.sort(chosen))
    return jnp.stack(lists).astype(jnp.int32)


def block_levels(rng, dims, cuts, least, high):
    factor_of = 1.0
    for axis_at, shards_of in cuts:
        steps = jax.random.uniform(jax.random.fold_in(jax.random.fold_in(rng, 6), axis_at), (shards_of,), jnp.float32, least / len(cuts), high / len(cuts))
        factor_of = factor_of * jnp.repeat(jnp.exp(steps), dims[axis_at] // shards_of).reshape((-1,) + (1,) * (len(dims) - 1 - axis_at))
    return factor_of


def normal_values(key, shape, deviation, bound, shards=(), held_as=jnp.bfloat16):
    result = deviation * jax.random.normal(key, shape, jnp.float32)
    if shards:
        result = result * block_levels(key, shape, shards, -0.22, 0.18)
    return jnp.clip(result, -bound, bound).astype(held_as)


def setup_inputs(seed: int = 0, part: int = 0) -> dict:
    splits = jax.random.split(jax.random.key(seed), 6)
    part_keys = jax.random.split(jax.random.fold_in(splits[5], part), 6)
    return {
        "inverse_pairs": normal_values(part_keys[0], (2, MA, MA), (2 * LROWS) ** -0.5, 0.09375, ((1, 8), (2, 2))),
        "factor_rows": normal_values(part_keys[1], (NSN, 2, LROWS, W), 0.2, 1.1953125, ((2, 8), (3, 2))),
        "diag_blocks": normal_values(part_keys[2], (NSN, 2, W, W), 1.0, 6.0, ((3, 2),)),
        "row_lists": draw_row_lists(jax.random.fold_in(splits[5], 71), part),
        "block_order": jax.random.permutation(splits[4], NB).astype(jnp.int32),
    }


def reference(inverse_pairs, factor_rows, diag_blocks, row_lists, block_order):
    columns = inverse_pairs.reshape(2, MA, NB, BLK)
    storage = jnp.arange(NB, dtype=jnp.int32)
    cols_list = []
    schur_list = []
    for supernode in range(NSN):
        hits = block_order[None, :] == row_lists[supernode][:, None]
        position = jnp.sum(jnp.where(hits, storage[None, :], 0), axis=1).astype(jnp.int32)
        chosen = jnp.take(columns, position, axis=2).reshape(2, MA, LROWS)
        factor = factor_rows[supernode]
        real_part = jnp.dot(chosen[0], factor[0], preferred_element_type=jnp.float32) - jnp.dot(chosen[1], factor[1], preferred_element_type=jnp.float32)
        imag_part = jnp.dot(chosen[0], factor[1], preferred_element_type=jnp.float32) + jnp.dot(chosen[1], factor[0], preferred_element_type=jnp.float32)
        values = -jnp.stack([real_part, imag_part])
        listed = jnp.take(values.reshape(2, NB, BLK, W), position, axis=1).reshape(2, LROWS, W)
        factor_wide = factor.astype(jnp.float32)
        highest = lax.Precision.HIGHEST
        gram_real = jnp.dot(factor_wide[0].T, listed[0], precision=highest) - jnp.dot(factor_wide[1].T, listed[1], precision=highest)
        gram_imag = jnp.dot(factor_wide[0].T, listed[1], precision=highest) + jnp.dot(factor_wide[1].T, listed[0], precision=highest)
        schur = diag_blocks[supernode].astype(jnp.float32) - jnp.stack([gram_real, gram_imag])
        cols_list.append(values)
        schur_list.append(schur)
    return jnp.stack(cols_list), jnp.stack(schur_list)
```

```python
import functools

import jax
import jax.numpy as jnp
from jax import lax
from jax.experimental import pallas as pl
from jax.experimental.pallas import tpu as pltpu
from jax.sharding import PartitionSpec as P

BLK = 128
CH = 2
MESH_AXES = ("row", "col")


def fetch(part, rows):
    ref, index = part
    return ref[index, rows, :]


def split_refs(refs, count, halves):
    chunks = [((refs[i], 0), (refs[i], 1)) for i in range(count)]
    if halves:
        chunks.append(((refs[count], 0), (refs[count + 1], 0)))
    return chunks, refs[count + 2 * halves :]


def build_weights(w_ref, slot, sub, offset, own, sib, rows):
    base = pl.multiple_of(slot * BLK, BLK)
    where = pl.ds(base, BLK)
    if sub < BLK:
        w_ref[0, where, :] = jnp.zeros((BLK, w_ref.shape[2]), w_ref.dtype)
        w_ref[1, where, :] = jnp.zeros((BLK, w_ref.shape[2]), w_ref.dtype)
        where = pl.ds(pl.multiple_of(base + offset, sub), sub)
    for at, chunk in enumerate((own, sib)):
        width = chunk[0][0].shape[2]
        real, imag = fetch(chunk[0], rows), fetch(chunk[1], rows)
        first, second = pl.ds(at * width, width), pl.ds((2 + at) * width, width)
        w_ref[0, where, first] = -real
        w_ref[0, where, second] = -imag
        w_ref[1, where, first] = imag
        w_ref[1, where, second] = -real


def values_kernel(count, halves, entries, sub, tile, tab_ref, a_ref, *refs):
    own, refs = split_refs(refs, count, halves)
    sib, refs = split_refs(refs, count, halves)
    mine_ref, theirs_ref, x_ref, w_ref, acc_ref, sems = refs
    step = pl.program_id(0)
    tiles = x_ref.shape[1] // tile
    width = mine_ref.shape[2]
    total = len(own) * entries

    def copy(at, slot, block):
        rows = pl.ds(pl.multiple_of(at * tile, tile), tile)
        return pltpu.make_async_copy(
            a_ref.at[:, rows, pl.ds(pl.multiple_of(block * BLK, BLK), BLK)],
            x_ref.at[:, rows, pl.ds(pl.multiple_of(slot * BLK, BLK), BLK)],
            sems.at[at, slot],
        )

    listed = jnp.int32(0)
    slots = []
    for i in range(total):
        slots.append(listed)
        listed = listed + (tab_ref[0, i] >= 0).astype(jnp.int32)

    @pl.when(step == 0)
    def _():
        for at in range(tiles):
            for i in range(total):

                @pl.when(tab_ref[0, i] >= 0)
                def _(at=at, i=i):
                    copy(at, slots[i], tab_ref[0, i]).start()

        for i in range(total):

            @pl.when(tab_ref[0, i] >= 0)
            def _(i=i):
                rows = pl.ds((i % entries) * sub, sub)
                build_weights(w_ref, slots[i], sub, tab_ref[2, i], own[i // entries], sib[i // entries], rows)

        @pl.when(lax.rem(listed, CH) != 0)
        def _():
            for extra in range(CH - 1):
                pad = pl.ds(pl.multiple_of((listed + extra) * BLK, BLK), BLK)
                w_ref[:, pad, :] = jnp.zeros((2, BLK, w_ref.shape[2]), w_ref.dtype)
                x_ref[:, :, pad] = jnp.zeros((2, x_ref.shape[1], BLK), x_ref.dtype)

    def arrived(slot, carry):
        copy(step, slot, 0).wait()
        return carry

    lax.fori_loop(0, listed, arrived, 0)
    acc_ref[...] = jnp.zeros_like(acc_ref)
    here = pl.ds(pl.multiple_of(step * tile, tile), tile)

    def multiply(at, carry):
        depth = pl.ds(pl.multiple_of(at * (CH * BLK), CH * BLK), CH * BLK)
        acc_ref[...] += jnp.dot(
            x_ref[0, here, depth], w_ref[0, depth, :], preferred_element_type=jnp.float32
        ) + jnp.dot(x_ref[1, here, depth], w_ref[1, depth, :], preferred_element_type=jnp.float32)
        return carry

    lax.fori_loop(0, lax.div(listed + (CH - 1), CH), multiply, 0)
    for q in range(2):
        mine_ref[q] = acc_ref[:, pl.ds(2 * q * width, width)]
        theirs_ref[q] = acc_ref[:, pl.ds((2 * q + 1) * width, width)]


def gram_kernel(count, halves, entries, sub, tab_ref, a_ref, *refs):
    own, refs = split_refs(refs, count, halves)
    sib, refs = split_refs(refs, count, halves)
    mine_ref, theirs_ref, x_ref, w_ref, l_ref, acc_ref, v_ref, sems = refs
    width = mine_ref.shape[2]
    total = len(own) * entries

    def copy(place, slot, row, block):
        return pltpu.make_async_copy(
            a_ref.at[
                :,
                pl.ds(pl.multiple_of(row * BLK, BLK), BLK),
                pl.ds(pl.multiple_of(block * BLK, BLK), BLK),
            ],
            x_ref.at[:, place, :, pl.ds(pl.multiple_of(slot * BLK, BLK), BLK)],
            sems.at[place, slot],
        )

    listed, placed = jnp.int32(0), jnp.int32(0)
    slots, places = [], []
    for i in range(total):
        slots.append(listed)
        places.append(placed)
        listed = listed + (tab_ref[0, i] >= 0).astype(jnp.int32)
        placed = placed + (tab_ref[1, i] >= 0).astype(jnp.int32)

    for r in range(total):

        @pl.when(tab_ref[1, r] >= 0)
        def _(r=r):
            for i in range(total):

                @pl.when(tab_ref[0, i] >= 0)
                def _(i=i):
                    copy(places[r], slots[i], tab_ref[1, r], tab_ref[0, i]).start()

    for i in range(total):
        rows = pl.ds((i % entries) * sub, sub)

        @pl.when(tab_ref[0, i] >= 0)
        def _(i=i, rows=rows):
            build_weights(w_ref, slots[i], sub, tab_ref[2, i], own[i // entries], sib[i // entries], rows)

        @pl.when(tab_ref[1, i] >= 0)
        def _(i=i, rows=rows):
            place = places[i]
            where = pl.ds(0, BLK)
            if sub < BLK:
                l_ref[place] = jnp.zeros(l_ref.shape[1:], l_ref.dtype)
                where = pl.ds(pl.multiple_of(tab_ref[2, i], sub), sub)
            for p in range(2):
                l_ref[place, 2 * p, where, :] = fetch(own[i // entries][p], rows)
                l_ref[place, 2 * p + 1, where, :] = fetch(sib[i // entries][p], rows)

    @pl.when(lax.rem(listed, CH) != 0)
    def _():
        for extra in range(CH - 1):
            pad = pl.ds(pl.multiple_of((listed + extra) * BLK, BLK), BLK)
            w_ref[:, pad, :] = jnp.zeros((2, BLK, w_ref.shape[2]), w_ref.dtype)
            x_ref[:, :, :, pad] = jnp.zeros((2, x_ref.shape[1], BLK, BLK), x_ref.dtype)

    acc_ref[...] = jnp.zeros_like(acc_ref)

    def one_place(place, carry):
        def arrived(slot, inner):
            copy(place, slot, 0, 0).wait()
            return inner

        lax.fori_loop(0, listed, arrived, 0)
        v_ref[...] = jnp.zeros_like(v_ref)

        def multiply(at, inner):
            depth = pl.ds(pl.multiple_of(at * (CH * BLK), CH * BLK), CH * BLK)
            v_ref[...] += jnp.dot(
                x_ref[0, place, :, depth], w_ref[0, depth, :], preferred_element_type=jnp.float32
            ) + jnp.dot(x_ref[1, place, :, depth], w_ref[1, depth, :], preferred_element_type=jnp.float32)
            return inner

        lax.fori_loop(0, lax.div(listed + (CH - 1), CH), multiply, 0)
        rest = v_ref[...]
        pieces = []
        for _ in range(3):
            piece = rest.astype(jnp.bfloat16)
            pieces.append(piece)
            rest = rest - piece.astype(jnp.float32)
        for half in range(2):
            real, imag = l_ref[place, half], l_ref[place, 2 + half]
            sums = [jnp.zeros((width, 4 * width), jnp.float32)] * 2
            for piece in reversed(pieces):
                for p, left in enumerate((real, imag)):
                    sums[p] = sums[p] + lax.dot_general(
                        left, piece, (((0,), (0,)), ((), ())), preferred_element_type=jnp.float32
                    )
            lo, hi = pl.ds(0, 2 * width), pl.ds(2 * width, 2 * width)
            acc_ref[half, :, lo] += sums[0][:, : 2 * width] - sums[1][:, 2 * width :]
            acc_ref[half, :, hi] += sums[0][:, 2 * width :] + sums[1][:, : 2 * width]
        return carry

    lax.fori_loop(0, placed, one_place, 0)
    core = tab_ref[3, 0]
    for half in range(2):
        at = core if half == 0 else 1 - core
        where = pl.ds(pl.multiple_of(at * width, width), width)
        for q in range(2):
            mine_ref[q, where, :] = acc_ref[half, :, pl.ds(2 * q * width, width)]
            theirs_ref[q, where, :] = acc_ref[half, :, pl.ds((2 * q + 1) * width, width)]


def kernel_operands(own, sib):
    return list(own) + list(sib)


def whole(x):
    rank = x.ndim
    return pl.BlockSpec(x.shape, lambda *_: (0,) * rank)


def make_values(tab, a, own, sib, halves, entries, sub, slots_max):
    rows = a.shape[1]
    width = own[0].shape[2]
    tile = max(t for t in range(BLK, min(rows, 512) + 1, BLK) if rows % t == 0)
    count = len(own) - 2 * halves
    operands = kernel_operands(own, sib)
    out = jax.ShapeDtypeStruct((2, rows, width), jnp.float32)
    out_spec = pl.BlockSpec((2, tile, width), lambda m, _: (0, m, 0))
    return pl.pallas_call(
        functools.partial(values_kernel, count, halves, entries, sub, tile),
        out_shape=(out, out),
        grid_spec=pltpu.PrefetchScalarGridSpec(
            num_scalar_prefetch=1,
            grid=(rows // tile,),
            in_specs=[pl.BlockSpec(memory_space=pl.ANY)] + [whole(x) for x in operands],
            out_specs=(out_spec, out_spec),
            scratch_shapes=[
                pltpu.VMEM((2, rows, slots_max * BLK), jnp.bfloat16),
                pltpu.VMEM((2, slots_max * BLK, 4 * width), jnp.bfloat16),
                pltpu.VMEM((tile, 4 * width), jnp.float32),
                pltpu.SemaphoreType.DMA((rows // tile, slots_max)),
            ],
        ),
        compiler_params=pltpu.CompilerParams(vmem_limit_bytes=40 * 2**20),
        cost_estimate=pl.CostEstimate(
            flops=2 * rows * slots_max * BLK * 4 * width, bytes_accessed=10 * 2**20, transcendentals=0
        ),
        name="values",
    )(tab, a, *operands)


def make_gram(tab, a, own, sib, halves, entries, sub, slots_max):
    rows = a.shape[1]
    width = own[0].shape[2]
    count = len(own) - 2 * halves
    operands = kernel_operands(own, sib)
    places_max = min(slots_max, (rows // BLK) * (BLK // sub))
    out = jax.ShapeDtypeStruct((2, 2 * width, width), jnp.float32)
    return pl.pallas_call(
        functools.partial(gram_kernel, count, halves, entries, sub),
        out_shape=(out, out),
        grid_spec=pltpu.PrefetchScalarGridSpec(
            num_scalar_prefetch=1,
            grid=(1,),
            in_specs=[pl.BlockSpec(memory_space=pl.ANY)] + [whole(x) for x in operands],
            out_specs=(whole(out), whole(out)),
            scratch_shapes=[
                pltpu.VMEM((2, places_max, BLK, slots_max * BLK), jnp.bfloat16),
                pltpu.VMEM((2, slots_max * BLK, 4 * width), jnp.bfloat16),
                pltpu.VMEM((places_max, 4, BLK, width), jnp.bfloat16),
                pltpu.VMEM((2, width, 4 * width), jnp.float32),
                pltpu.VMEM((BLK, 4 * width), jnp.float32),
                pltpu.SemaphoreType.DMA((places_max, slots_max)),
            ],
        ),
        compiler_params=pltpu.CompilerParams(vmem_limit_bytes=40 * 2**20),
        cost_estimate=pl.CostEstimate(
            flops=2 * 2 * BLK * slots_max * BLK * 4 * width, bytes_accessed=4 * 2**20, transcendentals=0
        ),
        name="gram",
    )(tab, a, *operands)


def local(n_row, inverse_pairs, factor_rows, diag_blocks, row_lists, block_order):
    supernodes = row_lists.shape[0]
    local_rows, local_cols = inverse_pairs.shape[1:]
    per_chip = factor_rows.shape[2]
    sub = min(BLK, per_chip)
    entries = per_chip // sub
    half = n_row // 2
    row, core = lax.axis_index("row"), lax.axis_index("col")
    cycle = list(range(0, n_row, 2)) + list(range(n_row - 1, 0, -2))
    ahead = [(cycle[i], cycle[(i + 1) % n_row]) for i in range(n_row)]
    behind = [(b, a) for a, b in ahead]
    swap = [(0, 1), (1, 0)]

    place = jnp.where(row % 2 == 0, row // 2, n_row - 1 - row // 2)
    offsets = [0]
    for d in range(1, half):
        offsets += [d, -d]
    offsets.append(half)
    source = (place - jnp.array(offsets, jnp.int32) + 2 * n_row) % n_row
    source = jnp.where(source < half, 2 * source, 2 * (n_row - 1 - source) + 1)
    start = (source[:, None] * per_chip + jnp.arange(entries, dtype=jnp.int32)[None, :] * sub).reshape(-1)
    wanted = start[:, None] // BLK == jnp.arange(row_lists.shape[1], dtype=jnp.int32)[None, :]
    listed = jnp.sum(jnp.where(wanted[None], row_lists[:, None, :], 0), axis=2)
    hits = listed[:, :, None] == block_order[None, None, :]
    storage = jnp.arange(block_order.shape[0], dtype=jnp.int32)
    position = jnp.sum(jnp.where(hits, storage[None, None, :], 0), axis=2)
    col_at = position - core * (local_cols // BLK)
    col_at = jnp.where((col_at >= 0) & (col_at < local_cols // BLK), col_at, -1)
    row_at = position - row * (local_rows // BLK)
    row_at = jnp.where((row_at >= 0) & (row_at < local_rows // BLK), row_at, -1)
    offset = jnp.broadcast_to((start % BLK)[None], position.shape)
    tab = jnp.stack([col_at, row_at, offset, jnp.broadcast_to(core, position.shape)], axis=1).astype(jnp.int32)

    own = [[factor_rows[k]] for k in range(supernodes)]
    up = [factor_rows[k] for k in range(supernodes)]
    down = list(up)
    for d in range(1, half):
        for k in range(supernodes):
            up[k] = lax.ppermute(up[k], "row", ahead)
            down[k] = lax.ppermute(down[k], "row", behind)
            own[k] += [up[k], down[k]]
    for k in range(supernodes):
        own[k].append(lax.ppermute(up[k][0:1], "row", ahead))
        own[k].append(lax.ppermute(down[k][1:2], "row", behind))
    sib = [[lax.ppermute(x, "col", swap) for x in own[k]] for k in range(supernodes)]

    slots_max = len(offsets) * entries
    args = [(tab[k], inverse_pairs, own[k], sib[k], True, entries, sub, slots_max) for k in range(supernodes)]

    odd, level = row % 2, row // 2
    pair = [(i, i ^ 1) for i in range(n_row)]
    shifts = [[(i, (i + 2 * d) % n_row) for i in range(n_row)] for d in range(half)]
    grams = []
    for k in range(supernodes):
        mine, theirs = make_gram(*args[k])
        total = mine + lax.ppermute(theirs, "col", swap)
        tall = total.shape[1] // 2
        sent = lax.dynamic_slice_in_dim(total, (1 - odd) * tall, tall, 1)
        kept = lax.dynamic_slice_in_dim(total, odd * tall, tall, 1)
        total = kept + lax.ppermute(sent, "row", pair)
        tall = tall // half
        kept = lax.dynamic_slice_in_dim(total, level * tall, tall, 1)
        for d in range(1, half):
            sent = lax.dynamic_slice_in_dim(total, (level + d) % half * tall, tall, 1)
            kept = kept + lax.ppermute(sent, "row", shifts[d])
        parts = [kept] + [lax.ppermute(kept, "row", shifts[half - d]) for d in range(1, half)]
        twice = jnp.concatenate(parts + parts, axis=1)
        same = lax.dynamic_slice_in_dim(twice, (half - level) % half * tall, half * tall, 1)
        other = lax.ppermute(same, "row", pair)
        grams.append(jnp.where(odd == 0, jnp.concatenate([same, other], 1), jnp.concatenate([other, same], 1)))
    schur = diag_blocks.astype(jnp.float32) - jnp.stack(grams)

    values = []
    for k in range(supernodes):
        mine, theirs = make_values(*args[k])
        values.append(mine + lax.ppermute(theirs, "col", swap))
    return (jnp.stack(values), schur)


def solution(mesh):
    in_specs = (
        P("pole", "row", "col"),
        P("pole", None, "row", "col"),
        P("pole", None, None, "col"),
        P(),
        P(),
    )
    out_specs = (P("pole", None, "row", "col"), P("pole", None, None, "col"))
    body = functools.partial(local, mesh.shape["row"])
    return jax.shard_map(body, mesh=mesh, in_specs=in_specs, out_specs=out_specs, check_vma=False)
```

```python
import functools

import jax
import jax.numpy as jnp
from jax import lax
from jax.experimental import pallas as pl
from jax.experimental.pallas import tpu as pltpu
from jax.sharding import PartitionSpec as P

BLK = 128
CH = 2
DEPTH = CH * 2 * BLK
COL_ENTRY, COL_BLOCK, ROW_ENTRY, ROW_BLOCK, OFFSET, COUNTS = range(6)


def pick(refs, early, chunk, p, rows):
    return refs[0 if early else 1][0, chunk, p, rows, :]


def on_entry(entry, entries, early_count, body):
    chunk, at = lax.div(entry, entries), lax.rem(entry, entries)

    @pl.when(chunk < early_count)
    def _():
        body(True, chunk, at)

    @pl.when(chunk >= early_count)
    def _():
        body(False, chunk - early_count, at)


def build_weights(w_ref, slot, sub, offset, own, sib, early, chunk, rows):
    base = pl.multiple_of(slot * 2 * BLK, 2 * BLK)
    if sub < BLK:
        w_ref[pl.ds(base, 2 * BLK), :] = jnp.zeros((2 * BLK, w_ref.shape[1]), w_ref.dtype)
        base = pl.multiple_of(base + offset, sub)
    with_real, with_imag = pl.ds(base, sub), pl.ds(base + BLK, sub)
    for at, refs in enumerate((own, sib)):
        width = refs[0].shape[4]
        real, imag = pick(refs, early, chunk, 0, rows), pick(refs, early, chunk, 1, rows)
        first, second = pl.ds(at * width, width), pl.ds((2 + at) * width, width)
        w_ref[with_real, first] = -real
        w_ref[with_real, second] = -imag
        w_ref[with_imag, first] = imag
        w_ref[with_imag, second] = -real


def rows_of(at, sub):
    return pl.ds(pl.multiple_of(at * sub, sub), sub)


def block_copies(a_ref, x_ref, sem, rows, to_rows, slot, block):
    base = pl.multiple_of(slot * 2 * BLK, 2 * BLK)
    cols = pl.ds(pl.multiple_of(block * BLK, BLK), BLK)
    return [
        pltpu.make_async_copy(a_ref.at[p, rows, cols], x_ref.at[to_rows, pl.ds(base + p * BLK, BLK)], sem)
        for p in range(2)
    ]


def block_wait(x_ref, sem, to_rows, slot):
    there = x_ref.at[to_rows, pl.ds(pl.multiple_of(slot * 2 * BLK, 2 * BLK), 2 * BLK)]
    pltpu.make_async_copy(there, there, sem).wait()


def values_kernel(entries, early_count, sub, tile, tab_ref, a_ref, own0, own1, sib0, sib1, *refs):
    mine_ref, theirs_ref, x_ref, w_ref, sems = refs
    k, step = pl.program_id(0), pl.program_id(1)
    own, sib = (own0, own1), (sib0, sib1)
    tiles = x_ref.shape[1] // tile
    width = mine_ref.shape[3]
    listed = tab_ref[k, COUNTS, 0]

    def tile_rows(at):
        return pl.ds(pl.multiple_of(at * tile, tile), tile)

    def start(which):
        for at in range(tiles):

            def one(slot, carry, at=at):
                block = tab_ref[which, COL_BLOCK, slot]
                for copy in block_copies(
                    a_ref, x_ref.at[which], sems.at[which, at, slot], tile_rows(at), tile_rows(at), slot, block
                ):
                    copy.start()
                return carry

            lax.fori_loop(0, tab_ref[which, COUNTS, 0], one, 0)

    @pl.when((k == 0) & (step == 0))
    def _():
        start(0)

    if tiles > 1:

        @pl.when((k == 0) & (step == 1))
        def _():
            for which in range(1, x_ref.shape[0]):
                start(which)

    else:

        @pl.when((k == 0) & (step == 0))
        def _():
            for which in range(1, x_ref.shape[0]):
                start(which)

    @pl.when(step == 0)
    def _():
        def one(slot, carry):
            entry = tab_ref[k, COL_ENTRY, slot]

            def body(early, chunk, at):
                build_weights(w_ref, slot, sub, tab_ref[k, OFFSET, entry], own, sib, early, chunk, rows_of(at, sub))

            on_entry(entry, entries, early_count, body)
            return carry

        lax.fori_loop(0, listed, one, 0)

        @pl.when(lax.rem(listed, CH) != 0)
        def _():
            pad = pl.ds(pl.multiple_of(listed * 2 * BLK, 2 * BLK), 2 * BLK)
            w_ref[pad, :] = jnp.zeros((2 * BLK, w_ref.shape[1]), w_ref.dtype)
            x_ref[k, :, pad] = jnp.zeros((x_ref.shape[1], 2 * BLK), x_ref.dtype)

    here = tile_rows(step)

    def arrived(slot, carry):
        block_wait(x_ref.at[k], sems.at[k, step, slot], here, slot)
        return carry

    lax.fori_loop(0, listed, arrived, 0)
    steps = lax.div(listed + (CH - 1), CH)

    def put(result):
        for q in range(2):
            mine_ref[0, q] = result[:, 2 * q * width : (2 * q + 1) * width]
            theirs_ref[0, q] = result[:, (2 * q + 1) * width : (2 * q + 2) * width]

    @pl.when(steps == 0)
    def _():
        put(jnp.zeros((tile, 4 * width), jnp.float32))

    for count in range(1, w_ref.shape[0] // DEPTH + 1):

        @pl.when(steps == count)
        def _(count=count):
            depth = pl.ds(0, count * DEPTH)
            put(jnp.dot(x_ref[k, here, depth], w_ref[depth, :], preferred_element_type=jnp.float32))


def gram_kernel(entries, early_count, sub, tab_ref, a_ref, own0, own1, sib0, sib1, *refs):
    mine_ref, theirs_ref, x_ref, w_ref, l_ref, v_ref, r_ref, acc_ref, sems = refs
    k = pl.program_id(0)
    own, sib = (own0, own1), (sib0, sib1)
    width = mine_ref.shape[4]
    chunk_rows = mine_ref.shape[3]
    listed, placed = tab_ref[k, COUNTS, 0], tab_ref[k, COUNTS, 1]

    def place_rows(place):
        return pl.ds(pl.multiple_of(place * BLK, BLK), BLK)

    def start(which):
        def one_place(place, carry):
            rows = place_rows(tab_ref[which, ROW_BLOCK, place])

            def one(slot, inner):
                block = tab_ref[which, COL_BLOCK, slot]
                for copy in block_copies(
                    a_ref, x_ref.at[which], sems.at[which, place, slot], rows, place_rows(place), slot, block
                ):
                    copy.start()
                return inner

            return lax.fori_loop(0, tab_ref[which, COUNTS, 0], one, carry)

        lax.fori_loop(0, tab_ref[which, COUNTS, 1], one_place, 0)

    @pl.when(k == 0)
    def _():
        for which in range(x_ref.shape[0]):
            start(which)

    @pl.when(placed > 0)
    def _():
        def one(slot, carry):
            entry = tab_ref[k, COL_ENTRY, slot]

            def body(early, chunk, at):
                build_weights(w_ref, slot, sub, tab_ref[k, OFFSET, entry], own, sib, early, chunk, rows_of(at, sub))

            on_entry(entry, entries, early_count, body)
            return carry

        lax.fori_loop(0, listed, one, 0)

        @pl.when(lax.rem(listed, CH) != 0)
        def _():
            pad = pl.ds(pl.multiple_of(listed * 2 * BLK, 2 * BLK), 2 * BLK)
            w_ref[pad, :] = jnp.zeros((2 * BLK, w_ref.shape[1]), w_ref.dtype)
            x_ref[k, :, pad] = jnp.zeros((x_ref.shape[1], 2 * BLK), x_ref.dtype)

    acc_ref[...] = jnp.zeros_like(acc_ref)
    steps = lax.div(listed + (CH - 1), CH)
    core = tab_ref[0, COUNTS, 2]

    def one_place(place, carry):
        def arrived(slot, inner):
            block_wait(x_ref.at[k], sems.at[k, place, slot], place_rows(place), slot)
            return inner

        lax.fori_loop(0, listed, arrived, 0)
        entry = tab_ref[k, ROW_ENTRY, place]

        def left(early, chunk, at):
            rows = rows_of(at, sub)
            for half, stack in enumerate((own, sib)):
                for p in range(2):
                    part = pick(stack, early, chunk, p, rows)
                    if sub < BLK:
                        l_ref[half, p] = jnp.zeros((BLK, width), l_ref.dtype)
                        l_ref[half, p, rows_of(lax.div(tab_ref[k, OFFSET, entry], sub), sub), :] = part
                    else:
                        l_ref[half, p] = part

        on_entry(entry, entries, early_count, left)
        for count in range(1, w_ref.shape[0] // DEPTH + 1):

            @pl.when(steps == count)
            def _(count=count):
                depth = pl.ds(0, count * DEPTH)
                v_ref[...] = jnp.dot(
                    x_ref[k, place_rows(place), depth], w_ref[depth, :], preferred_element_type=jnp.float32
                )

        rest = v_ref[...]
        for piece in range(3):
            kept = rest.astype(jnp.bfloat16)
            r_ref[piece, pl.ds(0, BLK), :] = kept
            r_ref[piece, pl.ds(BLK, BLK), pl.ds(0, 2 * width)] = -kept[:, 2 * width :]
            r_ref[piece, pl.ds(BLK, BLK), pl.ds(2 * width, 2 * width)] = kept[:, : 2 * width]
            rest = rest - kept.astype(jnp.float32)
        turned = jnp.concatenate(
            [jnp.concatenate([l_ref[half, p].T for p in range(2)], axis=1) for half in range(2)], axis=0
        )
        for piece in (2, 1, 0):
            acc_ref[...] += jnp.dot(turned, r_ref[piece], preferred_element_type=jnp.float32)
        return carry

    @pl.when(listed > 0)
    def _():
        lax.fori_loop(0, placed, one_place, 0)

    per_half = width // chunk_rows
    for half in range(2):
        first = (core if half == 0 else 1 - core) * per_half
        for i in range(per_half):
            rows = pl.ds(half * width + i * chunk_rows, chunk_rows)
            for q in range(2):
                mine_ref[first + i, 0, q] = acc_ref[rows, pl.ds(2 * q * width, width)]
                theirs_ref[first + i, 0, q] = acc_ref[rows, pl.ds((2 * q + 1) * width, width)]


def stack_spec(x):
    return pl.BlockSpec((1,) + x.shape[1:], lambda k, *_: (k, 0, 0, 0, 0))


def make_values(tab, a, stacks, entries, sub):
    supernodes, early_count = stacks[0].shape[:2]
    rows, width = a.shape[1], stacks[0].shape[4]
    slots = tab.shape[2]
    tile = max(t for t in range(BLK, min(rows, 512) + 1, BLK) if rows % t == 0)
    out = jax.ShapeDtypeStruct((supernodes, 2, rows, width), jnp.float32)
    out_spec = pl.BlockSpec((1, 2, tile, width), lambda k, m, _: (k, 0, m, 0))
    return pl.pallas_call(
        functools.partial(values_kernel, entries, early_count, sub, tile),
        out_shape=(out, out),
        grid_spec=pltpu.PrefetchScalarGridSpec(
            num_scalar_prefetch=1,
            grid=(supernodes, rows // tile),
            in_specs=[pl.BlockSpec(memory_space=pl.ANY)] + [stack_spec(x) for x in stacks],
            out_specs=(out_spec, out_spec),
            scratch_shapes=[
                pltpu.VMEM((supernodes, rows, slots * 2 * BLK), jnp.bfloat16),
                pltpu.VMEM((slots * 2 * BLK, 4 * width), jnp.bfloat16),
                pltpu.SemaphoreType.DMA((supernodes, rows // tile, slots)),
            ],
        ),
        compiler_params=pltpu.CompilerParams(vmem_limit_bytes=60 * 2**20),
        cost_estimate=pl.CostEstimate(
            flops=supernodes * rows * slots * 2 * BLK * 4 * width, bytes_accessed=20 * 2**20, transcendentals=0
        ),
        name="values",
    )(tab, a, *stacks)


def make_gram(tab, a, stacks, entries, sub, shares):
    supernodes, early_count = stacks[0].shape[:2]
    rows, width = a.shape[1], stacks[0].shape[4]
    slots = tab.shape[2]
    places = min(slots, (rows // BLK) * (BLK // sub))
    out = jax.ShapeDtypeStruct((shares, supernodes, 2, 2 * width // shares, width), jnp.float32)
    out_spec = pl.BlockSpec((shares, 1) + out.shape[2:], lambda k, _: (0, k, 0, 0, 0))
    return pl.pallas_call(
        functools.partial(gram_kernel, entries, early_count, sub),
        out_shape=(out, out),
        grid_spec=pltpu.PrefetchScalarGridSpec(
            num_scalar_prefetch=1,
            grid=(supernodes,),
            in_specs=[pl.BlockSpec(memory_space=pl.ANY)] + [stack_spec(x) for x in stacks],
            out_specs=(out_spec, out_spec),
            scratch_shapes=[
                pltpu.VMEM((supernodes, places * BLK, slots * 2 * BLK), jnp.bfloat16),
                pltpu.VMEM((slots * 2 * BLK, 4 * width), jnp.bfloat16),
                pltpu.VMEM((2, 2, BLK, width), jnp.bfloat16),
                pltpu.VMEM((BLK, 4 * width), jnp.float32),
                pltpu.VMEM((3, 2 * BLK, 4 * width), jnp.bfloat16),
                pltpu.VMEM((2 * width, 4 * width), jnp.float32),
                pltpu.SemaphoreType.DMA((supernodes, places, slots)),
            ],
        ),
        compiler_params=pltpu.CompilerParams(vmem_limit_bytes=60 * 2**20),
        cost_estimate=pl.CostEstimate(
            flops=supernodes * 2 * BLK * slots * 2 * BLK * 4 * width, bytes_accessed=8 * 2**20, transcendentals=0
        ),
        name="gram",
    )(tab, a, *stacks)


def compact(block, lo, count):
    inside = (block >= lo) & (block < lo + count)
    total = block.shape[1]
    number = jnp.arange(total, dtype=jnp.int32)
    before = jnp.sum(jnp.where(number[None, None, :] < number[None, :, None], inside[:, None, :], False), axis=2)
    goes = inside[:, None, :] & (before[:, None, :] == number[None, :, None])
    entry = jnp.sum(jnp.where(goes, number[None, None, :], 0), axis=2)
    local = jnp.sum(jnp.where(goes, block[:, None, :] - lo, 0), axis=2)
    return entry, local, jnp.sum(inside, axis=1)


def local(n_row, inverse_pairs, factor_rows, diag_blocks, row_lists, block_order):
    supernodes = row_lists.shape[0]
    local_rows, local_cols = inverse_pairs.shape[1:]
    per_chip = factor_rows.shape[2]
    sub = min(BLK, per_chip)
    entries = per_chip // sub
    half = n_row // 2
    row, core = lax.axis_index("row"), lax.axis_index("col")
    cycle = list(range(0, n_row, 2)) + list(range(n_row - 1, 0, -2))
    ahead = [(cycle[i], cycle[(i + 1) % n_row]) for i in range(n_row)]
    behind = [(b, a) for a, b in ahead]
    swap = [(0, 1), (1, 0)]

    place = jnp.where(row % 2 == 0, row // 2, n_row - 1 - row // 2)
    offsets = [0]
    for d in range(1, half):
        offsets += [d, -d]
    offsets.append(half)
    source = (place - jnp.array(offsets, jnp.int32) + 2 * n_row) % n_row
    source = jnp.where(source < half, 2 * source, 2 * (n_row - 1 - source) + 1)
    start = (source[:, None] * per_chip + jnp.arange(entries, dtype=jnp.int32)[None, :] * sub).reshape(-1)
    wanted = start[:, None] // BLK == jnp.arange(row_lists.shape[1], dtype=jnp.int32)[None, :]
    listed = jnp.sum(jnp.where(wanted[None], row_lists[:, None, :], 0), axis=2)
    hits = listed[:, :, None] == block_order[None, None, :]
    storage = jnp.arange(block_order.shape[0], dtype=jnp.int32)
    position = jnp.sum(jnp.where(hits, storage[None, None, :], 0), axis=2)
    col_entry, col_block, col_count = compact(position, core * (local_cols // BLK), local_cols // BLK)
    row_entry, row_block, row_count = compact(position, row * (local_rows // BLK), local_rows // BLK)
    number = jnp.arange(position.shape[1], dtype=jnp.int32)[None, :]
    counts = jnp.where(number == 0, col_count[:, None], jnp.where(number == 1, row_count[:, None], core))
    offset = jnp.broadcast_to((start % BLK)[None], position.shape)
    tab = jnp.stack([col_entry, col_block, row_entry, row_block, offset, counts], axis=1).astype(jnp.int32)

    chunks = [[factor_rows[k]] for k in range(supernodes)]
    up = [factor_rows[k] for k in range(supernodes)]
    down = list(up)
    for d in range(1, half):
        for k in range(supernodes):
            up[k] = lax.ppermute(up[k], "row", ahead)
            down[k] = lax.ppermute(down[k], "row", behind)
            chunks[k] += [up[k], down[k]]
    for k in range(supernodes):
        last = [lax.ppermute(up[k][0:1], "row", ahead), lax.ppermute(down[k][1:2], "row", behind)]
        chunks[k].append(jnp.concatenate(last, axis=0))
    early = max(1, len(offsets) - 3)
    own = [
        jnp.stack([jnp.stack(chunks[k][:early]) for k in range(supernodes)]),
        jnp.stack([jnp.stack(chunks[k][early:]) for k in range(supernodes)]),
    ]
    stacks = own + [lax.ppermute(x, "col", swap) for x in own]

    mine, theirs = make_gram(tab, inverse_pairs, stacks, entries, sub, n_row)
    total = mine + lax.ppermute(theirs, "col", swap)
    total, tab = lax.optimization_barrier((total, tab))
    share = jnp.sum(lax.all_to_all(total, "row", 0, 0, tiled=True), axis=0)
    shares = lax.all_to_all(jnp.broadcast_to(share[None], total.shape), "row", 0, 0, tiled=True)
    gram = jnp.moveaxis(shares, 0, 2).reshape(diag_blocks.shape)
    schur = diag_blocks.astype(jnp.float32) - gram

    mine, theirs = make_values(tab, inverse_pairs, stacks, entries, sub)
    return (mine + lax.ppermute(theirs, "col", swap), schur)


def solution(mesh):
    in_specs = (
        P("pole", "row", "col"),
        P("pole", None, "row", "col"),
        P("pole", None, None, "col"),
        P(),
        P(),
    )
    out_specs = (P("pole", None, "row", "col"), P("pole", None, None, "col"))
    body = functools.partial(local, mesh.shape["row"])
    return jax.shard_map(body, mesh=mesh, in_specs=in_specs, out_specs=out_specs, check_vma=False)
```

```python
import functools

import jax
import jax.numpy as jnp
from jax import lax
from jax.experimental import pallas as pl
from jax.experimental.pallas import tpu as pltpu
from jax.sharding import PartitionSpec as P

BLK = 128
CH = 2
DEPTH = CH * BLK
COL_ENTRY, COL_BLOCK, ROW_ENTRY, ROW_BLOCK, OFFSET, COUNTS = range(6)


def block_at(index, size=BLK):
    return pl.ds(pl.multiple_of(index * size, size), size)


def table_kernel(n_row, entries, sub, col_blocks, row_blocks, spot_ref, lists_ref, order_ref, tab_ref, where_ref):
    half = n_row // 2
    row, core = spot_ref[0], spot_ref[1]
    place = jnp.where(lax.rem(row, 2) == 0, lax.div(row, 2), n_row - 1 - lax.div(row, 2))

    def invert(g, carry):
        where_ref[order_ref[g]] = g
        return carry

    lax.fori_loop(0, order_ref.shape[0], invert, 0)
    for k in range(tab_ref.shape[0]):

        def one(i, counts, k=k):
            listed, placed = counts
            chunk, at = lax.div(i, entries), lax.rem(i, entries)
            step = lax.div(chunk + 1, 2)
            step = jnp.where((lax.rem(chunk, 2) == 1) | (chunk == n_row - 1), step, -step)
            source = lax.rem(place - step + 2 * n_row, n_row)
            source = jnp.where(source < half, 2 * source, 2 * (n_row - 1 - source) + 1)
            first = source * (entries * sub) + at * sub
            block = where_ref[lists_ref[k, lax.div(first, BLK)]]
            tab_ref[k, OFFSET, i] = lax.rem(first, BLK)
            col, line = block - core * col_blocks, block - row * row_blocks
            is_col = (col >= 0) & (col < col_blocks)
            is_row = (line >= 0) & (line < row_blocks)

            @pl.when(is_col)
            def _():
                tab_ref[k, COL_ENTRY, listed] = i
                tab_ref[k, COL_BLOCK, listed] = col

            @pl.when(is_row)
            def _():
                tab_ref[k, ROW_ENTRY, placed] = i
                tab_ref[k, ROW_BLOCK, placed] = line

            return listed + is_col.astype(jnp.int32), placed + is_row.astype(jnp.int32)

        listed, placed = lax.fori_loop(0, n_row * entries, one, (jnp.int32(0), jnp.int32(0)))
        tab_ref[k, COUNTS, 0] = listed
        tab_ref[k, COUNTS, 1] = placed
        tab_ref[k, COUNTS, 2] = core


def make_table(n_row, entries, sub, col_blocks, row_blocks, spot, row_lists, block_order):
    smem = pl.BlockSpec(memory_space=pltpu.SMEM)
    return pl.pallas_call(
        functools.partial(table_kernel, n_row, entries, sub, col_blocks, row_blocks),
        out_shape=jax.ShapeDtypeStruct((row_lists.shape[0], 6, max(n_row * entries, 3)), jnp.int32),
        in_specs=[smem] * 3,
        out_specs=smem,
        scratch_shapes=[pltpu.SMEM(block_order.shape, jnp.int32)],
        name="table",
    )(spot, row_lists, block_order)


def start_rows(tab_ref, kind, k, to_ref, sems, own, sib, entries, early_count, sub):
    def one(at, carry):
        entry = tab_ref[k, kind, at]
        chunk, part = lax.div(entry, entries), lax.rem(entry, entries)
        rows = pl.ds(at * BLK, BLK)
        if sub < BLK:
            to_ref[k, :, block_at(at), :] = jnp.zeros((2, BLK, to_ref.shape[3]), to_ref.dtype)
            rows = pl.ds(pl.multiple_of(at * BLK + tab_ref[k, OFFSET, entry], sub), sub)
        else:
            rows = block_at(at)
        for half, stacks in enumerate((own, sib)):
            width = stacks[0].shape[4]
            there = to_ref.at[k, :, rows, pl.ds(half * width, width)]

            @pl.when(chunk < early_count)
            def _(half=half, stacks=stacks, there=there):
                here = stacks[0].at[k, chunk, :, block_at(part, sub), :]
                pltpu.make_async_copy(here, there, sems.at[k, at, half]).start()

            @pl.when(chunk >= early_count)
            def _(half=half, stacks=stacks, there=there):
                here = stacks[1].at[k, chunk - early_count, :, block_at(part, sub), :]
                pltpu.make_async_copy(here, there, sems.at[k, at, half]).start()

        return carry

    return one


def wait_rows(k, to_ref, sems, width, sub):
    def one(at, carry):
        for half in range(2):
            there = to_ref.at[k, :, block_at(at) if sub == BLK else pl.ds(0, sub), pl.ds(half * width, width)]
            pltpu.make_async_copy(there, there, sems.at[k, at, half]).wait()
        return carry

    return one


def product(x, w, x_rows, depth):
    xr, xi = x[0, x_rows, depth], x[1, x_rows, depth]
    wr, wi = w[0, depth, :], w[1, depth, :]
    dot = functools.partial(jnp.dot, preferred_element_type=jnp.float32)
    return dot(xi, wi) - dot(xr, wr), -(dot(xr, wi) + dot(xi, wr))


def values_kernel(entries, early_count, sub, tile, tab_ref, a_ref, own0, own1, sib0, sib1, *refs):
    mine_ref, theirs_ref, x_ref, w_ref, x_sems, w_sems = refs
    k, step = pl.program_id(0), pl.program_id(1)
    own, sib = (own0, own1), (sib0, sib1)
    tiles = x_ref.shape[2] // tile
    width = mine_ref.shape[3]
    listed = tab_ref[k, COUNTS, 0]

    def start(which):
        rows = start_rows(tab_ref, COL_ENTRY, which, w_ref, w_sems, own, sib, entries, early_count, sub)
        lax.fori_loop(0, tab_ref[which, COUNTS, 0], rows, 0)
        for at in range(tiles):

            def one(slot, carry, at=at):
                pltpu.make_async_copy(
                    a_ref.at[:, block_at(at, tile), block_at(tab_ref[which, COL_BLOCK, slot])],
                    x_ref.at[which, :, block_at(at, tile), block_at(slot)],
                    x_sems.at[which, at, slot],
                ).start()
                return carry

            lax.fori_loop(0, tab_ref[which, COUNTS, 0], one, 0)

    @pl.when((k == 0) & (step == 0))
    def _():
        start(0)

    @pl.when((k == 0) & (step == min(1, tiles - 1)))
    def _():
        for which in range(1, x_ref.shape[0]):
            start(which)

    @pl.when(step == 0)
    def _():
        @pl.when(lax.rem(listed, CH) != 0)
        def _():
            w_ref[k, :, block_at(listed), :] = jnp.zeros((2, BLK, w_ref.shape[3]), w_ref.dtype)
            x_ref[k, :, :, block_at(listed)] = jnp.zeros((2, x_ref.shape[2], BLK), x_ref.dtype)

        lax.fori_loop(0, listed, wait_rows(k, w_ref, w_sems, width, sub), 0)

    def arrived(slot, carry):
        there = x_ref.at[k, :, block_at(step, tile), block_at(slot)]
        pltpu.make_async_copy(there, there, x_sems.at[k, step, slot]).wait()
        return carry

    lax.fori_loop(0, listed, arrived, 0)
    steps = lax.div(listed + (CH - 1), CH)

    @pl.when(steps == 0)
    def _():
        mine_ref[...] = jnp.zeros_like(mine_ref)
        theirs_ref[...] = jnp.zeros_like(theirs_ref)

    for count in range(1, w_ref.shape[2] // DEPTH + 1):

        @pl.when(steps == count)
        def _(count=count):
            parts = product(x_ref.at[k], w_ref.at[k], block_at(step, tile), pl.ds(0, count * DEPTH))
            for q, part in enumerate(parts):
                mine_ref[0, q] = part[:, :width]
                theirs_ref[0, q] = part[:, width:]


def gram_kernel(entries, early_count, sub, tab_ref, a_ref, own0, own1, sib0, sib1, *refs):
    mine_ref, theirs_ref, x_ref, w_ref, l_ref, v_ref, acc_ref, x_sems, w_sems, l_sems = refs
    k = pl.program_id(0)
    own, sib = (own0, own1), (sib0, sib1)
    width = mine_ref.shape[4]
    chunk_rows = mine_ref.shape[3]
    listed, placed = tab_ref[k, COUNTS, 0], tab_ref[k, COUNTS, 1]

    def start(which):
        stacks = (own, sib, entries, early_count, sub)
        there = tab_ref[which, COUNTS, 1]
        lax.fori_loop(0, there, start_rows(tab_ref, ROW_ENTRY, which, l_ref, l_sems, *stacks), 0)

        @pl.when(there > 0)
        def _():
            lax.fori_loop(
                0, tab_ref[which, COUNTS, 0], start_rows(tab_ref, COL_ENTRY, which, w_ref, w_sems, *stacks), 0
            )

        def one_place(place, carry):
            rows = block_at(tab_ref[which, ROW_BLOCK, place])

            def one(slot, inner):
                pltpu.make_async_copy(
                    a_ref.at[:, rows, block_at(tab_ref[which, COL_BLOCK, slot])],
                    x_ref.at[which, :, block_at(place), block_at(slot)],
                    x_sems.at[which, place, slot],
                ).start()
                return inner

            return lax.fori_loop(0, tab_ref[which, COUNTS, 0], one, carry)

        lax.fori_loop(0, there, one_place, 0)

    @pl.when(k == 0)
    def _():
        for which in range(x_ref.shape[0]):
            start(which)

    acc_ref[...] = jnp.zeros_like(acc_ref)
    steps = lax.div(listed + (CH - 1), CH)

    def one_pair(pair, carry):
        def one_place(place, inner):
            def arrived(slot, innermost):
                there = x_ref.at[k, :, block_at(place), block_at(slot)]
                pltpu.make_async_copy(there, there, x_sems.at[k, place, slot]).wait()
                return innermost

            lax.fori_loop(0, listed, arrived, 0)
            return wait_rows(k, l_ref, l_sems, width, sub)(place, inner)

        lax.fori_loop(2 * pair, jnp.minimum(2 * pair + 2, placed), one_place, 0)
        rows = block_at(pair, 2 * BLK)
        for count in range(1, w_ref.shape[2] // DEPTH + 1):

            @pl.when(steps == count)
            def _(count=count):
                parts = product(x_ref.at[k], w_ref.at[k], rows, pl.ds(0, count * DEPTH))
                v_ref[:, pl.ds(0, 2 * width)] = parts[0]
                v_ref[:, pl.ds(2 * width, 2 * width)] = parts[1]

        @pl.when(2 * pair + 1 >= placed)
        def _():
            v_ref[pl.ds(BLK, BLK), :] = jnp.zeros((BLK, v_ref.shape[1]), v_ref.dtype)
            l_ref[k, :, block_at(2 * pair + 1), :] = jnp.zeros((2, BLK, l_ref.shape[3]), l_ref.dtype)

        turned = [l_ref[k, p, rows, :].T for p in range(2)]
        rest = v_ref[...]
        pieces = []
        for _ in range(3):
            pieces.append(rest.astype(jnp.bfloat16))
            rest = rest - pieces[-1].astype(jnp.float32)
        for piece in reversed(pieces):
            for p in range(2):
                acc_ref[p] += jnp.dot(turned[p], piece, preferred_element_type=jnp.float32)
        return carry

    @pl.when((listed > 0) & (placed > 0))
    def _():
        @pl.when(lax.rem(listed, CH) != 0)
        def _():
            w_ref[k, :, block_at(listed), :] = jnp.zeros((2, BLK, w_ref.shape[3]), w_ref.dtype)
            x_ref[k, :, :, block_at(listed)] = jnp.zeros((2, x_ref.shape[2], BLK), x_ref.dtype)

        lax.fori_loop(0, listed, wait_rows(k, w_ref, w_sems, width, sub), 0)
        lax.fori_loop(0, lax.div(placed + 1, 2), one_pair, 0)

    @pl.when(listed == 0)
    def _():
        lax.fori_loop(0, placed, wait_rows(k, l_ref, l_sems, width, sub), 0)

    core = tab_ref[0, COUNTS, 2]
    per_half = width // chunk_rows
    for half in range(2):
        first = (core if half == 0 else 1 - core) * per_half
        for i in range(per_half):
            rows = pl.ds(half * width + i * chunk_rows, chunk_rows)
            for out_ref, at in ((mine_ref, 0), (theirs_ref, width)):
                real, imag = pl.ds(at, width), pl.ds(2 * width + at, width)
                out_ref[first + i, 0, 0] = acc_ref[0, rows, real] - acc_ref[1, rows, imag]
                out_ref[first + i, 0, 1] = acc_ref[0, rows, imag] + acc_ref[1, rows, real]


def make_values(tab, a, stacks, entries, sub):
    supernodes, early_count = stacks[0].shape[:2]
    rows, width = a.shape[1], stacks[0].shape[4]
    slots = tab.shape[2] + tab.shape[2] % CH
    tile = max(t for t in range(BLK, min(rows, 512) + 1, BLK) if rows % t == 0)
    out = jax.ShapeDtypeStruct((supernodes, 2, rows, width), jnp.float32)
    out_spec = pl.BlockSpec((1, 2, tile, width), lambda k, m, _: (k, 0, m, 0))
    return pl.pallas_call(
        functools.partial(values_kernel, entries, early_count, sub, tile),
        out_shape=(out, out),
        grid_spec=pltpu.PrefetchScalarGridSpec(
            num_scalar_prefetch=1,
            grid=(supernodes, rows // tile),
            in_specs=[pl.BlockSpec(memory_space=pl.ANY)] * 5,
            out_specs=(out_spec, out_spec),
            scratch_shapes=[
                pltpu.VMEM((supernodes, 2, rows, slots * BLK), jnp.bfloat16),
                pltpu.VMEM((supernodes, 2, slots * BLK, 2 * width), jnp.bfloat16),
                pltpu.SemaphoreType.DMA((supernodes, rows // tile, slots)),
                pltpu.SemaphoreType.DMA((supernodes, slots, 2)),
            ],
        ),
        compiler_params=pltpu.CompilerParams(vmem_limit_bytes=42 * 2**20),
        cost_estimate=pl.CostEstimate(
            flops=supernodes * rows * slots * 2 * BLK * 4 * width, bytes_accessed=20 * 2**20, transcendentals=0
        ),
        name="values",
    )(tab, a, *stacks)


def make_gram(tab, a, stacks, entries, sub, shares):
    supernodes, early_count = stacks[0].shape[:2]
    rows, width = a.shape[1], stacks[0].shape[4]
    slots = tab.shape[2] + tab.shape[2] % CH
    places = min(slots, (rows // BLK) * (BLK // sub))
    places += places % 2
    out = jax.ShapeDtypeStruct((shares, supernodes, 2, 2 * width // shares, width), jnp.float32)
    out_spec = pl.BlockSpec((shares, 1) + out.shape[2:], lambda k, _: (0, k, 0, 0, 0))
    return pl.pallas_call(
        functools.partial(gram_kernel, entries, early_count, sub),
        out_shape=(out, out),
        grid_spec=pltpu.PrefetchScalarGridSpec(
            num_scalar_prefetch=1,
            grid=(supernodes,),
            in_specs=[pl.BlockSpec(memory_space=pl.ANY)] * 5,
            out_specs=(out_spec, out_spec),
            scratch_shapes=[
                pltpu.VMEM((supernodes, 2, places * BLK, slots * BLK), jnp.bfloat16),
                pltpu.VMEM((supernodes, 2, slots * BLK, 2 * width), jnp.bfloat16),
                pltpu.VMEM((supernodes, 2, places * BLK, 2 * width), jnp.bfloat16),
                pltpu.VMEM((2 * BLK, 4 * width), jnp.float32),
                pltpu.VMEM((2, 2 * width, 4 * width), jnp.float32),
                pltpu.SemaphoreType.DMA((supernodes, places, slots)),
                pltpu.SemaphoreType.DMA((supernodes, slots, 2)),
                pltpu.SemaphoreType.DMA((supernodes, places, 2)),
            ],
        ),
        compiler_params=pltpu.CompilerParams(vmem_limit_bytes=42 * 2**20),
        cost_estimate=pl.CostEstimate(
            flops=supernodes * 2 * BLK * slots * 2 * BLK * 4 * width, bytes_accessed=8 * 2**20, transcendentals=0
        ),
        name="gram",
    )(tab, a, *stacks)


def sum_over_row(total, n_row, after):
    row = lax.axis_index("row")
    half = n_row // 2

    def moved(index, up, flip):
        level = (index // 2 + up + half) % half
        return 2 * level + (index % 2 if flip == 0 else 1 - index % 2)

    moves = [(up, flip) for up in range(1, half) for flip in range(2)]
    moves.sort(key=lambda m: -min(m[0], half - m[0]))
    moves.append((0, 1))
    routes = [[(i, moved(i, *m)) for i in range(n_row)] for m in moves]
    share = lax.dynamic_index_in_dim(total, row, 0, keepdims=False)
    came = [
        lax.ppermute(lax.dynamic_index_in_dim(total, moved(row, *m), 0, keepdims=False), "row", route)
        for m, route in zip(moves, routes)
    ]
    early = [i for i in range(len(came)) if i == 0 or i >= len(came) - 2]
    held = lax.optimization_barrier(tuple(came[i] for i in early) + (after,))
    for i, x in zip(early, held):
        came[i] = x
    for x in came:
        share = share + x
    came = [lax.ppermute(share, "row", route) for route in routes]
    whole = jnp.zeros(share.shape[:2] + (n_row,) + share.shape[2:], share.dtype)
    whole = lax.dynamic_update_index_in_dim(whole, share, row, 2)
    for (up, flip), x in zip(moves, came):
        whole = lax.dynamic_update_index_in_dim(whole, x, moved(row, -up, flip), 2)
    return whole, held[-1]


def local(n_row, inverse_pairs, factor_rows, diag_blocks, row_lists, block_order):
    supernodes = row_lists.shape[0]
    local_rows, local_cols = inverse_pairs.shape[1:]
    per_chip = factor_rows.shape[2]
    sub = min(BLK, per_chip)
    entries = per_chip // sub
    half = n_row // 2
    cycle = list(range(0, n_row, 2)) + list(range(n_row - 1, 0, -2))
    ahead = [(cycle[i], cycle[(i + 1) % n_row]) for i in range(n_row)]
    behind = [(b, a) for a, b in ahead]
    swap = [(0, 1), (1, 0)]

    chunks = [[factor_rows[k]] for k in range(supernodes)]
    up = [factor_rows[k] for k in range(supernodes)]
    down = list(up)
    for d in range(1, half):
        for k in range(supernodes):
            up[k] = lax.ppermute(up[k], "row", ahead)
            down[k] = lax.ppermute(down[k], "row", behind)
            chunks[k] += [up[k], down[k]]
    for k in range(supernodes):
        last = [lax.ppermute(up[k][0:1], "row", ahead), lax.ppermute(down[k][1:2], "row", behind)]
        chunks[k].append(jnp.concatenate(last, axis=0))
    early = max(1, n_row - 3)
    own = [
        jnp.stack([jnp.stack(chunks[k][:early]) for k in range(supernodes)]),
        jnp.stack([jnp.stack(chunks[k][early:]) for k in range(supernodes)]),
    ]
    stacks = own + [lax.ppermute(x, "col", swap) for x in own]

    spot = jnp.stack([lax.axis_index("row"), lax.axis_index("col")]).astype(jnp.int32)
    spot, _ = lax.optimization_barrier((spot, own[1]))
    tab = make_table(n_row, entries, sub, local_cols // BLK, local_rows // BLK, spot, row_lists, block_order)

    mine, theirs = make_gram(tab, inverse_pairs, stacks, entries, sub, n_row)
    total = mine + lax.ppermute(theirs, "col", swap)
    gram, tab = sum_over_row(total, n_row, tab)
    schur = diag_blocks.astype(jnp.float32) - gram.reshape(diag_blocks.shape)

    mine, theirs = make_values(tab, inverse_pairs, stacks, entries, sub)
    return (mine + lax.ppermute(theirs, "col", swap), schur)


def solution(mesh):
    in_specs = (
        P("pole", "row", "col"),
        P("pole", None, "row", "col"),
        P("pole", None, None, "col"),
        P(),
        P(),
    )
    out_specs = (P("pole", None, "row", "col"), P("pole", None, None, "col"))
    body = functools.partial(local, mesh.shape["row"])
    return jax.shard_map(body, mesh=mesh, in_specs=in_specs, out_specs=out_specs, check_vma=False)
```

```python
import functools

import jax
import jax.numpy as jnp
from jax import lax
from jax.experimental import pallas as pl
from jax.experimental.pallas import tpu as pltpu
from jax.sharding import PartitionSpec as P

BLK = 128
CH = 2
DEPTH = CH * BLK
COL_ENTRY, COL_BLOCK, ROW_ENTRY, ROW_BLOCK, OFFSET, COUNTS = range(6)


def block_at(index, size=BLK):
    return pl.ds(pl.multiple_of(index * size, size), size)


def table_kernel(n_row, entries, sub, col_blocks, row_blocks, spot_ref, lists_ref, order_ref, tab_ref, where_ref):
    half = n_row // 2
    row, core = spot_ref[0], spot_ref[1]
    place = jnp.where(lax.rem(row, 2) == 0, lax.div(row, 2), n_row - 1 - lax.div(row, 2))

    def invert(g, carry):
        where_ref[order_ref[g]] = g
        return carry

    lax.fori_loop(0, order_ref.shape[0], invert, 0, unroll=8)
    for k in range(tab_ref.shape[0]):

        def one(i, counts, k=k):
            listed, placed = counts
            chunk, at = lax.div(i, entries), lax.rem(i, entries)
            step = lax.div(chunk + 1, 2)
            step = jnp.where((lax.rem(chunk, 2) == 1) | (chunk == n_row - 1), step, -step)
            source = lax.rem(place - step + 2 * n_row, n_row)
            source = jnp.where(source < half, 2 * source, 2 * (n_row - 1 - source) + 1)
            first = source * (entries * sub) + at * sub
            block = where_ref[lists_ref[k, lax.div(first, BLK)]]
            tab_ref[k, OFFSET, i] = lax.rem(first, BLK)
            col, line = block - core * col_blocks, block - row * row_blocks
            is_col = (col >= 0) & (col < col_blocks)
            is_row = (line >= 0) & (line < row_blocks)

            @pl.when(is_col)
            def _():
                tab_ref[k, COL_ENTRY, listed] = i
                tab_ref[k, COL_BLOCK, listed] = col

            @pl.when(is_row)
            def _():
                tab_ref[k, ROW_ENTRY, placed] = i
                tab_ref[k, ROW_BLOCK, placed] = line

            return listed + is_col.astype(jnp.int32), placed + is_row.astype(jnp.int32)

        listed, placed = lax.fori_loop(0, n_row * entries, one, (jnp.int32(0), jnp.int32(0)), unroll=4)
        tab_ref[k, COUNTS, 0] = listed
        tab_ref[k, COUNTS, 1] = placed
        tab_ref[k, COUNTS, 2] = core


def make_table(n_row, entries, sub, col_blocks, row_blocks, spot, row_lists, block_order):
    smem = pl.BlockSpec(memory_space=pltpu.SMEM)
    return pl.pallas_call(
        functools.partial(table_kernel, n_row, entries, sub, col_blocks, row_blocks),
        out_shape=jax.ShapeDtypeStruct((row_lists.shape[0], 6, max(n_row * entries, 3)), jnp.int32),
        in_specs=[smem] * 3,
        out_specs=smem,
        scratch_shapes=[pltpu.SMEM(block_order.shape, jnp.int32)],
        name="table",
    )(spot, row_lists, block_order)


def start_rows(tab_ref, kind, k, to_ref, sems, halves, entries, early_count, sub):
    def one(at, carry):
        entry = tab_ref[k, kind, at]
        chunk, part = lax.div(entry, entries), lax.rem(entry, entries)
        rows = block_at(at)
        if sub < BLK:
            to_ref[k, rows, :] = jnp.zeros((BLK, to_ref.shape[2]), to_ref.dtype)
            rows = pl.ds(pl.multiple_of(at * BLK + tab_ref[k, OFFSET, entry], sub), sub)

        def copy(stack, chunk, there, p):
            here = stack.at[k, chunk, p, block_at(part, sub), :]
            pltpu.make_async_copy(here, there, sems.at[k]).start()

        for half, stacks in enumerate(halves):
            width = stacks[0].shape[4]
            for p in range(2):
                there = to_ref.at[k, rows, pl.ds((2 * half + p) * width, width)]

                @pl.when(chunk < early_count)
                def _(stacks=stacks, there=there, p=p):
                    copy(stacks[0], chunk, there, p)

                @pl.when(chunk >= early_count)
                def _(stacks=stacks, there=there, p=p):
                    copy(stacks[1], chunk - early_count, there, p)

        return carry

    return one


def wait_rows(k, to_ref, sems, width, sub, halves):
    def one(at, carry):
        there = to_ref.at[k, pl.ds(0, sub), pl.ds(0, 2 * halves * width)]
        pltpu.make_async_copy(there, there, sems.at[k]).wait()
        return carry

    return one


def product(x, w, x_rows, depth):
    width = w.shape[1] // 2
    real, imag = (
        jnp.dot(x[p, x_rows, depth], w[depth, :], preferred_element_type=jnp.float32) for p in range(2)
    )
    return imag[:, width:] - real[:, :width], -(real[:, width:] + imag[:, :width])


def values_kernel(entries, early_count, sub, tile, with_added, tab_ref, a_ref, first, second, *refs):
    added_ref = refs[0] if with_added else None
    out_ref, x_ref, w_ref, x_sems, w_sems = refs[with_added:]
    k, step = pl.program_id(0), pl.program_id(1)
    tiles = x_ref.shape[2] // tile
    width = out_ref.shape[3]
    listed = tab_ref[k, COUNTS, 0]

    def start(which):
        rows = start_rows(tab_ref, COL_ENTRY, which, w_ref, w_sems, ((first, second),), entries, early_count, sub)
        lax.fori_loop(0, tab_ref[which, COUNTS, 0], rows, 0)
        for at in range(tiles):

            def one(slot, carry, at=at):
                pltpu.make_async_copy(
                    a_ref.at[:, block_at(at, tile), block_at(tab_ref[which, COL_BLOCK, slot])],
                    x_ref.at[which, :, block_at(at, tile), block_at(slot)],
                    x_sems.at[which, at],
                ).start()
                return carry

            lax.fori_loop(0, tab_ref[which, COUNTS, 0], one, 0)

    @pl.when((k == 0) & (step == 0))
    def _():
        start(0)

    @pl.when((k == 0) & (step == min(1, tiles - 1)))
    def _():
        for which in range(1, x_ref.shape[0]):
            start(which)

    @pl.when(step == 0)
    def _():
        @pl.when(lax.rem(listed, CH) != 0)
        def _():
            w_ref[k, block_at(listed), :] = jnp.zeros((BLK, w_ref.shape[2]), w_ref.dtype)
            x_ref[k, :, :, block_at(listed)] = jnp.zeros((2, x_ref.shape[2], BLK), x_ref.dtype)

        lax.fori_loop(0, listed, wait_rows(k, w_ref, w_sems, width, sub, 1), 0)

    def arrived(slot, carry):
        there = x_ref.at[k, :, block_at(step, tile), block_at(slot)]
        pltpu.make_async_copy(there, there, x_sems.at[k, step]).wait()
        return carry

    lax.fori_loop(0, listed, arrived, 0)
    steps = lax.div(listed + (CH - 1), CH)

    def put(real, imag):
        for q, part in enumerate((real, imag)):
            out_ref[0, q] = part + added_ref[0, q] if with_added else part

    @pl.when(steps == 0)
    def _():
        zero = jnp.zeros((tile, width), jnp.float32)
        put(zero, zero)

    for count in range(1, w_ref.shape[1] // DEPTH + 1):

        @pl.when(steps == count)
        def _(count=count):
            put(*product(x_ref.at[k], w_ref.at[k], block_at(step, tile), pl.ds(0, count * DEPTH)))


def gram_kernel(entries, early_count, sub, tab_ref, a_ref, own0, own1, sib0, sib1, *refs):
    mine_ref, theirs_ref, x_ref, w_ref, l_ref, v_ref, acc_ref, x_sems, w_sems, l_sems = refs
    k = pl.program_id(0)
    own, sib = (own0, own1), (sib0, sib1)
    width = mine_ref.shape[4]
    chunk_rows = mine_ref.shape[3]
    listed, placed = tab_ref[k, COUNTS, 0], tab_ref[k, COUNTS, 1]

    def start(which):
        stacks = ((own, sib), entries, early_count, sub)
        there = tab_ref[which, COUNTS, 1]
        lax.fori_loop(0, there, start_rows(tab_ref, ROW_ENTRY, which, l_ref, l_sems, *stacks), 0)

        @pl.when(there > 0)
        def _():
            lax.fori_loop(
                0, tab_ref[which, COUNTS, 0], start_rows(tab_ref, COL_ENTRY, which, w_ref, w_sems, *stacks), 0
            )

        def one_place(place, carry):
            rows = block_at(tab_ref[which, ROW_BLOCK, place])

            def one(slot, inner):
                pltpu.make_async_copy(
                    a_ref.at[:, rows, block_at(tab_ref[which, COL_BLOCK, slot])],
                    x_ref.at[which, :, block_at(place), block_at(slot)],
                    x_sems.at[which, lax.div(place, 2)],
                ).start()
                return inner

            return lax.fori_loop(0, tab_ref[which, COUNTS, 0], one, carry)

        lax.fori_loop(0, there, one_place, 0)

    @pl.when(k == 0)
    def _():
        for which in range(x_ref.shape[0]):
            start(which)

    acc_ref[...] = jnp.zeros_like(acc_ref)
    lax.fori_loop(0, placed, wait_rows(k, l_ref, l_sems, width, sub, 2), 0)

    @pl.when(placed > 0)
    def _():
        lax.fori_loop(0, listed, wait_rows(k, w_ref, w_sems, width, sub, 2), 0)

    steps = lax.div(listed + (CH - 1), CH)

    def one_pair(pair, carry):
        def one_place(place, inner):
            def arrived(slot, innermost):
                there = x_ref.at[k, :, block_at(place), block_at(slot)]
                pltpu.make_async_copy(there, there, x_sems.at[k, pair]).wait()
                return innermost

            return lax.fori_loop(0, listed, arrived, inner)

        lax.fori_loop(2 * pair, jnp.minimum(2 * pair + 2, placed), one_place, 0)
        rows = block_at(pair, 2 * BLK)
        for count in range(1, w_ref.shape[1] // DEPTH + 1):

            @pl.when(steps == count)
            def _(count=count):
                for half in range(2):
                    columns = w_ref.at[k, :, pl.ds(2 * half * width, 2 * width)]
                    parts = product(x_ref.at[k], columns, rows, pl.ds(0, count * DEPTH))
                    for q in range(2):
                        v_ref[:, pl.ds((2 * half + q) * width, width)] = parts[q]

        @pl.when(2 * pair + 1 >= placed)
        def _():
            v_ref[pl.ds(BLK, BLK), :] = jnp.zeros((BLK, v_ref.shape[1]), v_ref.dtype)
            l_ref[k, block_at(2 * pair + 1), :] = jnp.zeros((BLK, l_ref.shape[2]), l_ref.dtype)

        left = l_ref[k, rows, :]
        turned = [
            jnp.concatenate([left[:, (2 * h + p) * width : (2 * h + p + 1) * width].T for h in range(2)], axis=0)
            for p in range(2)
        ]
        rest = v_ref[...]
        pieces = []
        for _ in range(3):
            pieces.append(rest.astype(jnp.bfloat16))
            rest = rest - pieces[-1].astype(jnp.float32)
        for piece in reversed(pieces):
            for p in range(2):
                acc_ref[p] += jnp.dot(turned[p], piece, preferred_element_type=jnp.float32)
        return carry

    @pl.when((listed > 0) & (placed > 0))
    def _():
        @pl.when(lax.rem(listed, CH) != 0)
        def _():
            w_ref[k, block_at(listed), :] = jnp.zeros((BLK, w_ref.shape[2]), w_ref.dtype)
            x_ref[k, :, :, block_at(listed)] = jnp.zeros((2, x_ref.shape[2], BLK), x_ref.dtype)

        lax.fori_loop(0, lax.div(placed + 1, 2), one_pair, 0)

    core = tab_ref[0, COUNTS, 2]
    per_half = width // chunk_rows
    for half in range(2):
        first = (core if half == 0 else 1 - core) * per_half
        for i in range(per_half):
            rows = pl.ds(half * width + i * chunk_rows, chunk_rows)
            for out_ref, at in ((mine_ref, 0), (theirs_ref, 2 * width)):
                real, imag = pl.ds(at, width), pl.ds(width + at, width)
                out_ref[first + i, 0, 0] = acc_ref[0, rows, real] - acc_ref[1, rows, imag]
                out_ref[first + i, 0, 1] = acc_ref[0, rows, imag] + acc_ref[1, rows, real]


def make_values(tab, a, stacks, entries, sub, added=None):
    supernodes, early_count = stacks[0].shape[:2]
    rows, width = a.shape[1], stacks[0].shape[4]
    slots = tab.shape[2] + tab.shape[2] % CH
    tile = max(t for t in range(BLK, min(rows, 512) + 1, BLK) if rows % t == 0)
    out_spec = pl.BlockSpec((1, 2, tile, width), lambda k, m, _: (k, 0, m, 0))
    extra = [] if added is None else [added]
    return pl.pallas_call(
        functools.partial(values_kernel, entries, early_count, sub, tile, len(extra)),
        out_shape=jax.ShapeDtypeStruct((supernodes, 2, rows, width), jnp.float32),
        grid_spec=pltpu.PrefetchScalarGridSpec(
            num_scalar_prefetch=1,
            grid=(supernodes, rows // tile),
            in_specs=[pl.BlockSpec(memory_space=pl.ANY)] * 3 + [out_spec] * len(extra),
            out_specs=out_spec,
            scratch_shapes=[
                pltpu.VMEM((supernodes, 2, rows, slots * BLK), jnp.bfloat16),
                pltpu.VMEM((supernodes, slots * BLK, 2 * width), jnp.bfloat16),
                pltpu.SemaphoreType.DMA((supernodes, rows // tile)),
                pltpu.SemaphoreType.DMA((supernodes,)),
            ],
        ),
        compiler_params=pltpu.CompilerParams(vmem_limit_bytes=42 * 2**20),
        cost_estimate=pl.CostEstimate(
            flops=supernodes * rows * slots * BLK * 4 * width, bytes_accessed=16 * 2**20, transcendentals=0
        ),
        name="values",
    )(tab, a, *stacks, *extra)


def make_gram(tab, a, stacks, entries, sub, shares):
    supernodes, early_count = stacks[0].shape[:2]
    rows, width = a.shape[1], stacks[0].shape[4]
    slots = tab.shape[2] + tab.shape[2] % CH
    places = min(slots, (rows // BLK) * (BLK // sub))
    places += places % 2
    out = jax.ShapeDtypeStruct((shares, supernodes, 2, 2 * width // shares, width), jnp.float32)
    out_spec = pl.BlockSpec((shares, 1) + out.shape[2:], lambda k, _: (0, k, 0, 0, 0))
    return pl.pallas_call(
        functools.partial(gram_kernel, entries, early_count, sub),
        out_shape=(out, out),
        grid_spec=pltpu.PrefetchScalarGridSpec(
            num_scalar_prefetch=1,
            grid=(supernodes,),
            in_specs=[pl.BlockSpec(memory_space=pl.ANY)] * 5,
            out_specs=(out_spec, out_spec),
            scratch_shapes=[
                pltpu.VMEM((supernodes, 2, places * BLK, slots * BLK), jnp.bfloat16),
                pltpu.VMEM((supernodes, slots * BLK, 4 * width), jnp.bfloat16),
                pltpu.VMEM((supernodes, places * BLK, 4 * width), jnp.bfloat16),
                pltpu.VMEM((2 * BLK, 4 * width), jnp.float32),
                pltpu.VMEM((2, 2 * width, 4 * width), jnp.float32),
                pltpu.SemaphoreType.DMA((supernodes, places // 2)),
                pltpu.SemaphoreType.DMA((supernodes,)),
                pltpu.SemaphoreType.DMA((supernodes,)),
            ],
        ),
        compiler_params=pltpu.CompilerParams(vmem_limit_bytes=42 * 2**20),
        cost_estimate=pl.CostEstimate(
            flops=supernodes * 2 * BLK * slots * 2 * BLK * 4 * width, bytes_accessed=8 * 2**20, transcendentals=0
        ),
        name="gram",
    )(tab, a, *stacks)


def local(n_row, inverse_pairs, factor_rows, diag_blocks, row_lists, block_order):
    supernodes = row_lists.shape[0]
    local_rows, local_cols = inverse_pairs.shape[1:]
    per_chip = factor_rows.shape[2]
    sub = min(BLK, per_chip)
    entries = per_chip // sub
    half = n_row // 2
    cycle = list(range(0, n_row, 2)) + list(range(n_row - 1, 0, -2))
    ahead = [(cycle[i], cycle[(i + 1) % n_row]) for i in range(n_row)]
    behind = [(b, a) for a, b in ahead]
    swap = [(0, 1), (1, 0)]

    chunks = [[factor_rows[k]] for k in range(supernodes)]
    up = [factor_rows[k] for k in range(supernodes)]
    down = list(up)
    for d in range(1, half):
        for k in range(supernodes):
            up[k] = lax.ppermute(up[k], "row", ahead)
            down[k] = lax.ppermute(down[k], "row", behind)
            chunks[k] += [up[k], down[k]]
    for k in range(supernodes):
        last = [lax.ppermute(up[k][0:1], "row", ahead), lax.ppermute(down[k][1:2], "row", behind)]
        chunks[k].append(jnp.concatenate(last, axis=0))
    early = max(1, n_row - 3)
    own = [
        jnp.stack([jnp.stack(chunks[k][:early]) for k in range(supernodes)]),
        jnp.stack([jnp.stack(chunks[k][early:]) for k in range(supernodes)]),
    ]
    stacks = own + [lax.ppermute(x, "col", swap) for x in own]

    spot = jnp.stack([lax.axis_index("row"), lax.axis_index("col")]).astype(jnp.int32)
    tab = make_table(n_row, entries, sub, local_cols // BLK, local_rows // BLK, spot, row_lists, block_order)

    mine, theirs = make_gram(tab, inverse_pairs, stacks, entries, sub, n_row)
    total = mine + lax.ppermute(theirs, "col", swap)
    total, tab = lax.optimization_barrier((total, tab))
    share = jnp.sum(lax.all_to_all(total, "row", 0, 0, tiled=True), axis=0)
    shares = lax.all_to_all(jnp.broadcast_to(share[None], total.shape), "row", 0, 0, tiled=True)
    gram = jnp.moveaxis(shares, 0, 2).reshape(diag_blocks.shape)
    schur = diag_blocks.astype(jnp.float32) - gram

    theirs = make_values(tab, inverse_pairs, stacks[2:], entries, sub)
    values = make_values(tab, inverse_pairs, stacks[:2], entries, sub, lax.ppermute(theirs, "col", swap))
    return (values, schur)


def solution(mesh):
    in_specs = (
        P("pole", "row", "col"),
        P("pole", None, "row", "col"),
        P("pole", None, None, "col"),
        P(),
        P(),
    )
    out_specs = (P("pole", None, "row", "col"), P("pole", None, None, "col"))
    body = functools.partial(local, mesh.shape["row"])
    return jax.shard_map(body, mesh=mesh, in_specs=in_specs, out_specs=out_specs, check_vma=False)
```

```python
import functools

import jax
import jax.numpy as jnp
from jax import lax
from jax.experimental import pallas as pl
from jax.experimental.pallas import tpu as pltpu
from jax.sharding import PartitionSpec as P

BLK = 128
CH = 2
DEPTH = CH * BLK
COL_ENTRY, COL_BLOCK, ROW_ENTRY, ROW_BLOCK, OFFSET, COUNTS = range(6)


def block_at(index, size=BLK):
    return pl.ds(pl.multiple_of(index * size, size), size)


def table_kernel(n_row, entries, sub, col_blocks, row_blocks, spot_ref, lists_ref, order_ref, tab_ref, where_ref):
    half = n_row // 2
    row, core = spot_ref[0], spot_ref[1]
    place = jnp.where(lax.rem(row, 2) == 0, lax.div(row, 2), n_row - 1 - lax.div(row, 2))

    def invert(g, carry):
        where_ref[order_ref[g]] = g
        return carry

    lax.fori_loop(0, order_ref.shape[0], invert, 0, unroll=8)
    for k in range(tab_ref.shape[0]):

        def one(i, counts, k=k):
            listed, placed = counts
            chunk, at = lax.div(i, entries), lax.rem(i, entries)
            step = lax.div(chunk + 1, 2)
            step = jnp.where((lax.rem(chunk, 2) == 1) | (chunk == n_row - 1), step, -step)
            source = lax.rem(place - step + 2 * n_row, n_row)
            source = jnp.where(source < half, 2 * source, 2 * (n_row - 1 - source) + 1)
            first = source * (entries * sub) + at * sub
            block = where_ref[lists_ref[k, lax.div(first, BLK)]]
            tab_ref[k, OFFSET, i] = lax.rem(first, BLK)
            col, line = block - core * col_blocks, block - row * row_blocks
            is_col = (col >= 0) & (col < col_blocks)
            is_row = (line >= 0) & (line < row_blocks)

            @pl.when(is_col)
            def _():
                tab_ref[k, COL_ENTRY, listed] = i
                tab_ref[k, COL_BLOCK, listed] = col

            @pl.when(is_row)
            def _():
                tab_ref[k, ROW_ENTRY, placed] = i
                tab_ref[k, ROW_BLOCK, placed] = line

            return listed + is_col.astype(jnp.int32), placed + is_row.astype(jnp.int32)

        listed, placed = lax.fori_loop(0, n_row * entries, one, (jnp.int32(0), jnp.int32(0)), unroll=4)
        tab_ref[k, COUNTS, 0] = listed
        tab_ref[k, COUNTS, 1] = placed
        tab_ref[k, COUNTS, 2] = core


def make_table(n_row, entries, sub, col_blocks, row_blocks, spot, row_lists, block_order):
    smem = pl.BlockSpec(memory_space=pltpu.SMEM)
    return pl.pallas_call(
        functools.partial(table_kernel, n_row, entries, sub, col_blocks, row_blocks),
        out_shape=jax.ShapeDtypeStruct((row_lists.shape[0], 6, max(n_row * entries, 3)), jnp.int32),
        in_specs=[smem] * 3,
        out_specs=smem,
        scratch_shapes=[pltpu.SMEM(block_order.shape, jnp.int32)],
        name="table",
    )(spot, row_lists, block_order)


def start_rows(tab_ref, kind, k, to_ref, sems, halves, entries, early_count, sub):
    def one(at, carry):
        entry = tab_ref[k, kind, at]
        chunk, part = lax.div(entry, entries), lax.rem(entry, entries)
        rows = block_at(at)
        if sub < BLK:
            to_ref[k, rows, :] = jnp.zeros((BLK, to_ref.shape[2]), to_ref.dtype)
            rows = pl.ds(pl.multiple_of(at * BLK + tab_ref[k, OFFSET, entry], sub), sub)

        def copy(stack, chunk, there, p):
            here = stack.at[k, chunk, p, block_at(part, sub), :]
            pltpu.make_async_copy(here, there, sems.at[k]).start()

        for half, stacks in enumerate(halves):
            width = stacks[0].shape[4]
            for p in range(2):
                there = to_ref.at[k, rows, pl.ds((2 * half + p) * width, width)]

                @pl.when(chunk < early_count)
                def _(stacks=stacks, there=there, p=p):
                    copy(stacks[0], chunk, there, p)

                @pl.when(chunk >= early_count)
                def _(stacks=stacks, there=there, p=p):
                    copy(stacks[1], chunk - early_count, there, p)

        return carry

    return one


def wait_rows(k, to_ref, sems, width, sub, halves):
    def one(at, carry):
        there = to_ref.at[k, pl.ds(0, sub), pl.ds(0, 2 * halves * width)]
        pltpu.make_async_copy(there, there, sems.at[k]).wait()
        return carry

    return one


def product(x, w, x_rows, depth):
    width = w.shape[1] // 2
    real, imag = (
        jnp.dot(x[p, x_rows, depth], w[depth, :], preferred_element_type=jnp.float32) for p in range(2)
    )
    return imag[:, width:] - real[:, :width], -(real[:, width:] + imag[:, :width])


def values_kernel(entries, early_count, sub, tile, with_added, tab_ref, a_ref, first, second, *refs):
    added_ref = refs[0] if with_added else None
    out_ref, x_ref, w_ref, x_sems, w_sems = refs[with_added:]
    k, step = pl.program_id(0), pl.program_id(1)
    tiles = x_ref.shape[2] // tile
    width = out_ref.shape[3]
    listed = tab_ref[k, COUNTS, 0]

    def start(which):
        rows = start_rows(tab_ref, COL_ENTRY, which, w_ref, w_sems, ((first, second),), entries, early_count, sub)
        lax.fori_loop(0, tab_ref[which, COUNTS, 0], rows, 0)
        for at in range(tiles):

            def one(slot, carry, at=at):
                pltpu.make_async_copy(
                    a_ref.at[:, block_at(at, tile), block_at(tab_ref[which, COL_BLOCK, slot])],
                    x_ref.at[which, :, block_at(at, tile), block_at(slot)],
                    x_sems.at[which, at],
                ).start()
                return carry

            lax.fori_loop(0, tab_ref[which, COUNTS, 0], one, 0)

    @pl.when((k == 0) & (step == 0))
    def _():
        start(0)

    @pl.when((k == 0) & (step == min(1, tiles - 1)))
    def _():
        for which in range(1, x_ref.shape[0]):
            start(which)

    @pl.when(step == 0)
    def _():
        @pl.when(lax.rem(listed, CH) != 0)
        def _():
            w_ref[k, block_at(listed), :] = jnp.zeros((BLK, w_ref.shape[2]), w_ref.dtype)
            x_ref[k, :, :, block_at(listed)] = jnp.zeros((2, x_ref.shape[2], BLK), x_ref.dtype)

        lax.fori_loop(0, listed, wait_rows(k, w_ref, w_sems, width, sub, 1), 0)

    def arrived(slot, carry):
        there = x_ref.at[k, :, block_at(step, tile), block_at(slot)]
        pltpu.make_async_copy(there, there, x_sems.at[k, step]).wait()
        return carry

    lax.fori_loop(0, listed, arrived, 0)
    steps = lax.div(listed + (CH - 1), CH)

    def put(real, imag):
        for q, part in enumerate((real, imag)):
            out_ref[0, q] = part + added_ref[0, q] if with_added else part

    @pl.when(steps == 0)
    def _():
        zero = jnp.zeros((tile, width), jnp.float32)
        put(zero, zero)

    for count in range(1, w_ref.shape[1] // DEPTH + 1):

        @pl.when(steps == count)
        def _(count=count):
            put(*product(x_ref.at[k], w_ref.at[k], block_at(step, tile), pl.ds(0, count * DEPTH)))


def gram_kernel(entries, early_count, sub, tab_ref, a_ref, own0, own1, sib0, sib1, *refs):
    mine_ref, theirs_ref, x_ref, w_ref, l_ref, v_ref, acc_ref, x_sems, w_sems, l_sems = refs
    k = pl.program_id(0)
    own, sib = (own0, own1), (sib0, sib1)
    width = mine_ref.shape[4]
    chunk_rows = mine_ref.shape[3]
    listed, placed = tab_ref[k, COUNTS, 0], tab_ref[k, COUNTS, 1]

    def start(which):
        stacks = ((own, sib), entries, early_count, sub)
        there = tab_ref[which, COUNTS, 1]
        lax.fori_loop(0, there, start_rows(tab_ref, ROW_ENTRY, which, l_ref, l_sems, *stacks), 0)

        @pl.when(there > 0)
        def _():
            lax.fori_loop(
                0, tab_ref[which, COUNTS, 0], start_rows(tab_ref, COL_ENTRY, which, w_ref, w_sems, *stacks), 0
            )

        def one_place(place, carry):
            rows = block_at(tab_ref[which, ROW_BLOCK, place])

            def one(slot, inner):
                pltpu.make_async_copy(
                    a_ref.at[:, rows, block_at(tab_ref[which, COL_BLOCK, slot])],
                    x_ref.at[which, :, block_at(place), block_at(slot)],
                    x_sems.at[which, lax.div(place, 2)],
                ).start()
                return inner

            return lax.fori_loop(0, tab_ref[which, COUNTS, 0], one, carry)

        lax.fori_loop(0, there, one_place, 0)

    @pl.when(k == 0)
    def _():
        for which in range(x_ref.shape[0]):
            start(which)

    acc_ref[...] = jnp.zeros_like(acc_ref)
    lax.fori_loop(0, placed, wait_rows(k, l_ref, l_sems, width, sub, 2), 0)

    @pl.when(placed > 0)
    def _():
        lax.fori_loop(0, listed, wait_rows(k, w_ref, w_sems, width, sub, 2), 0)

    steps = lax.div(listed + (CH - 1), CH)

    def one_pair(pair, carry):
        def one_place(place, inner):
            def arrived(slot, innermost):
                there = x_ref.at[k, :, block_at(place), block_at(slot)]
                pltpu.make_async_copy(there, there, x_sems.at[k, pair]).wait()
                return innermost

            return lax.fori_loop(0, listed, arrived, inner)

        lax.fori_loop(2 * pair, jnp.minimum(2 * pair + 2, placed), one_place, 0)
        rows = block_at(pair, 2 * BLK)
        for count in range(1, w_ref.shape[1] // DEPTH + 1):

            @pl.when(steps == count)
            def _(count=count):
                for half in range(2):
                    columns = w_ref.at[k, :, pl.ds(2 * half * width, 2 * width)]
                    parts = product(x_ref.at[k], columns, rows, pl.ds(0, count * DEPTH))
                    for q in range(2):
                        v_ref[:, pl.ds((2 * half + q) * width, width)] = parts[q]

        @pl.when(2 * pair + 1 >= placed)
        def _():
            v_ref[pl.ds(BLK, BLK), :] = jnp.zeros((BLK, v_ref.shape[1]), v_ref.dtype)
            l_ref[k, block_at(2 * pair + 1), :] = jnp.zeros((BLK, l_ref.shape[2]), l_ref.dtype)

        left = l_ref[k, rows, :]
        turned = [
            jnp.concatenate([left[:, (2 * h + p) * width : (2 * h + p + 1) * width].T for h in range(2)], axis=0)
            for p in range(2)
        ]
        rest = v_ref[...]
        pieces = []
        for _ in range(3):
            pieces.append(rest.astype(jnp.bfloat16))
            rest = rest - pieces[-1].astype(jnp.float32)
        for piece in reversed(pieces):
            for p in range(2):
                acc_ref[p] += jnp.dot(turned[p], piece, preferred_element_type=jnp.float32)
        return carry

    @pl.when((listed > 0) & (placed > 0))
    def _():
        @pl.when(lax.rem(listed, CH) != 0)
        def _():
            w_ref[k, block_at(listed), :] = jnp.zeros((BLK, w_ref.shape[2]), w_ref.dtype)
            x_ref[k, :, :, block_at(listed)] = jnp.zeros((2, x_ref.shape[2], BLK), x_ref.dtype)

        lax.fori_loop(0, lax.div(placed + 1, 2), one_pair, 0)

    core = tab_ref[0, COUNTS, 2]
    per_half = width // chunk_rows
    for half in range(2):
        first = (core if half == 0 else 1 - core) * per_half
        for i in range(per_half):
            rows = pl.ds(half * width + i * chunk_rows, chunk_rows)
            for out_ref, at in ((mine_ref, 0), (theirs_ref, 2 * width)):
                real, imag = pl.ds(at, width), pl.ds(width + at, width)
                out_ref[first + i, 0, 0] = acc_ref[0, rows, real] - acc_ref[1, rows, imag]
                out_ref[first + i, 0, 1] = acc_ref[0, rows, imag] + acc_ref[1, rows, real]


def make_values(tab, a, stacks, entries, sub, added=None):
    supernodes, early_count = stacks[0].shape[:2]
    rows, width = a.shape[1], stacks[0].shape[4]
    slots = tab.shape[2] + tab.shape[2] % CH
    tile = max(t for t in range(BLK, min(rows, 512) + 1, BLK) if rows % t == 0)
    out_spec = pl.BlockSpec((1, 2, tile, width), lambda k, m, _: (k, 0, m, 0))
    extra = [] if added is None else [added]
    return pl.pallas_call(
        functools.partial(values_kernel, entries, early_count, sub, tile, len(extra)),
        out_shape=jax.ShapeDtypeStruct((supernodes, 2, rows, width), jnp.float32),
        grid_spec=pltpu.PrefetchScalarGridSpec(
            num_scalar_prefetch=1,
            grid=(supernodes, rows // tile),
            in_specs=[pl.BlockSpec(memory_space=pl.ANY)] * 3 + [out_spec] * len(extra),
            out_specs=out_spec,
            scratch_shapes=[
                pltpu.VMEM((supernodes, 2, rows, slots * BLK), jnp.bfloat16),
                pltpu.VMEM((supernodes, slots * BLK, 2 * width), jnp.bfloat16),
                pltpu.SemaphoreType.DMA((supernodes, rows // tile)),
                pltpu.SemaphoreType.DMA((supernodes,)),
            ],
        ),
        compiler_params=pltpu.CompilerParams(vmem_limit_bytes=42 * 2**20),
        cost_estimate=pl.CostEstimate(
            flops=supernodes * rows * slots * BLK * 4 * width, bytes_accessed=16 * 2**20, transcendentals=0
        ),
        name="values",
    )(tab, a, *stacks, *extra)


def make_gram(tab, a, stacks, entries, sub, shares):
    supernodes, early_count = stacks[0].shape[:2]
    rows, width = a.shape[1], stacks[0].shape[4]
    slots = tab.shape[2] + tab.shape[2] % CH
    places = min(slots, (rows // BLK) * (BLK // sub))
    places += places % 2
    out = jax.ShapeDtypeStruct((shares, supernodes, 2, 2 * width // shares, width), jnp.float32)
    out_spec = pl.BlockSpec((shares, 1) + out.shape[2:], lambda k, _: (0, k, 0, 0, 0))
    return pl.pallas_call(
        functools.partial(gram_kernel, entries, early_count, sub),
        out_shape=(out, out),
        grid_spec=pltpu.PrefetchScalarGridSpec(
            num_scalar_prefetch=1,
            grid=(supernodes,),
            in_specs=[pl.BlockSpec(memory_space=pl.ANY)] * 5,
            out_specs=(out_spec, out_spec),
            scratch_shapes=[
                pltpu.VMEM((supernodes, 2, places * BLK, slots * BLK), jnp.bfloat16),
                pltpu.VMEM((supernodes, slots * BLK, 4 * width), jnp.bfloat16),
                pltpu.VMEM((supernodes, places * BLK, 4 * width), jnp.bfloat16),
                pltpu.VMEM((2 * BLK, 4 * width), jnp.float32),
                pltpu.VMEM((2, 2 * width, 4 * width), jnp.float32),
                pltpu.SemaphoreType.DMA((supernodes, places // 2)),
                pltpu.SemaphoreType.DMA((supernodes,)),
                pltpu.SemaphoreType.DMA((supernodes,)),
            ],
        ),
        compiler_params=pltpu.CompilerParams(vmem_limit_bytes=42 * 2**20),
        cost_estimate=pl.CostEstimate(
            flops=supernodes * 2 * BLK * slots * 2 * BLK * 4 * width, bytes_accessed=8 * 2**20, transcendentals=0
        ),
        name="gram",
    )(tab, a, *stacks)


def local(n_row, inverse_pairs, factor_rows, diag_blocks, row_lists, block_order):
    supernodes = row_lists.shape[0]
    local_rows, local_cols = inverse_pairs.shape[1:]
    per_chip = factor_rows.shape[2]
    sub = min(BLK, per_chip)
    entries = per_chip // sub
    half = n_row // 2
    cycle = list(range(0, n_row, 2)) + list(range(n_row - 1, 0, -2))
    ahead = [(cycle[i], cycle[(i + 1) % n_row]) for i in range(n_row)]
    behind = [(b, a) for a, b in ahead]
    swap = [(0, 1), (1, 0)]

    chunks = [[factor_rows[k]] for k in range(supernodes)]
    up = [factor_rows[k] for k in range(supernodes)]
    down = list(up)
    for d in range(1, half):
        for k in range(supernodes):
            up[k] = lax.ppermute(up[k], "row", ahead)
            down[k] = lax.ppermute(down[k], "row", behind)
            chunks[k] += [up[k], down[k]]
    for k in range(supernodes):
        last = [lax.ppermute(up[k][0:1], "row", ahead), lax.ppermute(down[k][1:2], "row", behind)]
        chunks[k].append(jnp.concatenate(last, axis=0))
    early = max(1, n_row - 3)
    own = [
        jnp.stack([jnp.stack(chunks[k][:early]) for k in range(supernodes)]),
        jnp.stack([jnp.stack(chunks[k][early:]) for k in range(supernodes)]),
    ]
    stacks = own + [lax.ppermute(x, "col", swap) for x in own]

    spot = jnp.stack([lax.axis_index("row"), lax.axis_index("col")]).astype(jnp.int32)
    tab = make_table(n_row, entries, sub, local_cols // BLK, local_rows // BLK, spot, row_lists, block_order)

    mine, theirs = make_gram(tab, inverse_pairs, stacks, entries, sub, n_row)
    total = mine + lax.ppermute(theirs, "col", swap)
    total, tab = lax.optimization_barrier((total, tab))
    share = jnp.sum(lax.all_to_all(total, "row", 0, 0, tiled=True), axis=0)
    gram = lax.all_gather(share, "row", axis=2, tiled=True)
    theirs = make_values(tab, inverse_pairs, stacks[2:], entries, sub)
    values = make_values(tab, inverse_pairs, stacks[:2], entries, sub, lax.ppermute(theirs, "col", swap))
    gram, values = lax.optimization_barrier((gram, values))
    return (values, diag_blocks.astype(jnp.float32) - gram)


def solution(mesh):
    in_specs = (
        P("pole", "row", "col"),
        P("pole", None, "row", "col"),
        P("pole", None, None, "col"),
        P(),
        P(),
    )
    out_specs = (P("pole", None, "row", "col"), P("pole", None, None, "col"))
    body = functools.partial(local, mesh.shape["row"])
    return jax.shard_map(body, mesh=mesh, in_specs=in_specs, out_specs=out_specs, check_vma=False)
```

```python
import functools

import jax
import jax.numpy as jnp
from jax import lax
from jax.experimental import pallas as pl
from jax.experimental.pallas import tpu as pltpu
from jax.sharding import PartitionSpec as P

BLK = 128
CH = 2
DEPTH = CH * BLK
COL_ENTRY, COL_BLOCK, ROW_ENTRY, ROW_BLOCK, OFFSET, COUNTS = range(6)


def block_at(index, size=BLK):
    return pl.ds(pl.multiple_of(index * size, size), size)


def table_kernel(n_row, entries, sub, col_blocks, row_blocks, lists_ref, order_ref, tab_ref, where_ref):
    half = n_row // 2
    row, core = lax.axis_index("row"), lax.axis_index("col")
    place = jnp.where(lax.rem(row, 2) == 0, lax.div(row, 2), n_row - 1 - lax.div(row, 2))

    def invert(g, carry):
        where_ref[order_ref[g]] = g
        return carry

    lax.fori_loop(0, order_ref.shape[0], invert, 0, unroll=8)
    for k in range(tab_ref.shape[0]):

        def one(i, counts, k=k):
            listed, placed = counts
            chunk, at = lax.div(i, entries), lax.rem(i, entries)
            step = lax.div(chunk + 1, 2)
            step = jnp.where((lax.rem(chunk, 2) == 1) | (chunk == n_row - 1), step, -step)
            source = lax.rem(place - step + 2 * n_row, n_row)
            source = jnp.where(source < half, 2 * source, 2 * (n_row - 1 - source) + 1)
            first = source * (entries * sub) + at * sub
            block = where_ref[lists_ref[k, lax.div(first, BLK)]]
            tab_ref[k, OFFSET, i] = lax.rem(first, BLK)
            col, line = block - core * col_blocks, block - row * row_blocks
            is_col = (col >= 0) & (col < col_blocks)
            is_row = (line >= 0) & (line < row_blocks)

            @pl.when(is_col)
            def _():
                tab_ref[k, COL_ENTRY, listed] = i
                tab_ref[k, COL_BLOCK, listed] = col

            @pl.when(is_row)
            def _():
                tab_ref[k, ROW_ENTRY, placed] = i
                tab_ref[k, ROW_BLOCK, placed] = line

            return listed + is_col.astype(jnp.int32), placed + is_row.astype(jnp.int32)

        listed, placed = lax.fori_loop(0, n_row * entries, one, (jnp.int32(0), jnp.int32(0)), unroll=4)
        tab_ref[k, COUNTS, 0] = listed
        tab_ref[k, COUNTS, 1] = placed
        tab_ref[k, COUNTS, 2] = core


def make_table(n_row, entries, sub, col_blocks, row_blocks, row_lists, block_order):
    smem = pl.BlockSpec(memory_space=pltpu.SMEM)
    return pl.pallas_call(
        functools.partial(table_kernel, n_row, entries, sub, col_blocks, row_blocks),
        out_shape=jax.ShapeDtypeStruct((row_lists.shape[0], 6, max(n_row * entries, 3)), jnp.int32),
        in_specs=[smem] * 2,
        out_specs=smem,
        scratch_shapes=[pltpu.SMEM(block_order.shape, jnp.int32)],
        name="table",
    )(row_lists, block_order)


def start_rows(tab_ref, kind, k, to_ref, sems, halves, entries, early_count, sub):
    def one(at, carry):
        entry = tab_ref[k, kind, at]
        chunk, part = lax.div(entry, entries), lax.rem(entry, entries)
        rows = block_at(at)
        if sub < BLK:
            to_ref[k, rows, :] = jnp.zeros((BLK, to_ref.shape[2]), to_ref.dtype)
            rows = pl.ds(pl.multiple_of(at * BLK + tab_ref[k, OFFSET, entry], sub), sub)

        def copy(stack, chunk, there, p):
            here = stack.at[k, chunk, p, block_at(part, sub), :]
            pltpu.make_async_copy(here, there, sems.at[k]).start()

        for half, stacks in enumerate(halves):
            width = stacks[0].shape[4]
            for p in range(2):
                there = to_ref.at[k, rows, pl.ds((2 * half + p) * width, width)]

                @pl.when(chunk < early_count)
                def _(stacks=stacks, there=there, p=p):
                    copy(stacks[0], chunk, there, p)

                @pl.when(chunk >= early_count)
                def _(stacks=stacks, there=there, p=p):
                    copy(stacks[1], chunk - early_count, there, p)

        return carry

    return one


def wait_rows(k, to_ref, sems, width, sub, halves):
    def one(at, carry):
        there = to_ref.at[k, pl.ds(0, sub), pl.ds(0, 2 * halves * width)]
        pltpu.make_async_copy(there, there, sems.at[k]).wait()
        return carry

    return one


def product(x, w, x_rows, depth):
    width = w.shape[1] // 2
    real, imag = (
        jnp.dot(x[p, x_rows, depth], w[depth, :], preferred_element_type=jnp.float32) for p in range(2)
    )
    return imag[:, width:] - real[:, :width], -(real[:, width:] + imag[:, :width])


def values_kernel(entries, early_count, sub, tile, tab_ref, a_ref, own0, own1, sib0, sib1, *refs):
    mine_ref, theirs_ref, x_ref, w_ref, x_sems, w_sems = refs
    k, step = pl.program_id(0), pl.program_id(1)
    tiles = x_ref.shape[2] // tile
    width = mine_ref.shape[3]
    listed = tab_ref[k, COUNTS, 0]

    def start(which):
        rows = start_rows(tab_ref, COL_ENTRY, which, w_ref, w_sems, ((own0, own1), (sib0, sib1)), entries, early_count, sub)
        lax.fori_loop(0, tab_ref[which, COUNTS, 0], rows, 0)
        for at in range(tiles):

            def one(slot, carry, at=at):
                pltpu.make_async_copy(
                    a_ref.at[:, block_at(at, tile), block_at(tab_ref[which, COL_BLOCK, slot])],
                    x_ref.at[which, :, block_at(at, tile), block_at(slot)],
                    x_sems.at[which, at],
                ).start()
                return carry

            lax.fori_loop(0, tab_ref[which, COUNTS, 0], one, 0)

    @pl.when((k == 0) & (step == 0))
    def _():
        start(0)

    @pl.when((k == 0) & (step == min(1, tiles - 1)))
    def _():
        for which in range(1, x_ref.shape[0]):
            start(which)

    @pl.when(step == 0)
    def _():
        @pl.when(lax.rem(listed, CH) != 0)
        def _():
            w_ref[k, block_at(listed), :] = jnp.zeros((BLK, w_ref.shape[2]), w_ref.dtype)
            x_ref[k, :, :, block_at(listed)] = jnp.zeros((2, x_ref.shape[2], BLK), x_ref.dtype)

        lax.fori_loop(0, listed, wait_rows(k, w_ref, w_sems, width, sub, 2), 0)

    def arrived(slot, carry):
        there = x_ref.at[k, :, block_at(step, tile), block_at(slot)]
        pltpu.make_async_copy(there, there, x_sems.at[k, step]).wait()
        return carry

    lax.fori_loop(0, listed, arrived, 0)
    steps = lax.div(listed + (CH - 1), CH)


    @pl.when(steps == 0)
    def _():
        mine_ref[...] = jnp.zeros_like(mine_ref)
        theirs_ref[...] = jnp.zeros_like(theirs_ref)

    for count in range(1, w_ref.shape[1] // DEPTH + 1):

        @pl.when(steps == count)
        def _(count=count):
            for half, out_ref in enumerate((mine_ref, theirs_ref)):
                columns = w_ref.at[k, :, pl.ds(2 * half * width, 2 * width)]
                parts = product(x_ref.at[k], columns, block_at(step, tile), pl.ds(0, count * DEPTH))
                for q in range(2):
                    out_ref[0, q] = parts[q]


def gram_kernel(entries, early_count, sub, tab_ref, a_ref, own0, own1, sib0, sib1, *refs):
    mine_ref, theirs_ref, x_ref, w_ref, l_ref, v_ref, r_ref, acc_ref, x_sems, w_sems, l_sems = refs
    k = pl.program_id(0)
    own, sib = (own0, own1), (sib0, sib1)
    width = mine_ref.shape[4]
    chunk_rows = mine_ref.shape[3]
    listed, placed = tab_ref[k, COUNTS, 0], tab_ref[k, COUNTS, 1]

    def start(which):
        stacks = ((own, sib), entries, early_count, sub)
        there = tab_ref[which, COUNTS, 1]
        lax.fori_loop(0, there, start_rows(tab_ref, ROW_ENTRY, which, l_ref, l_sems, *stacks), 0)

        @pl.when(there > 0)
        def _():
            lax.fori_loop(
                0, tab_ref[which, COUNTS, 0], start_rows(tab_ref, COL_ENTRY, which, w_ref, w_sems, *stacks), 0
            )

        def one_place(place, carry):
            rows = block_at(tab_ref[which, ROW_BLOCK, place])

            def one(slot, inner):
                pltpu.make_async_copy(
                    a_ref.at[:, rows, block_at(tab_ref[which, COL_BLOCK, slot])],
                    x_ref.at[which, :, block_at(place), block_at(slot)],
                    x_sems.at[which, lax.div(place, 2)],
                ).start()
                return inner

            return lax.fori_loop(0, tab_ref[which, COUNTS, 0], one, carry)

        lax.fori_loop(0, there, one_place, 0)

    @pl.when(k == 0)
    def _():
        for which in range(x_ref.shape[0]):
            start(which)

    acc_ref[...] = jnp.zeros_like(acc_ref)
    lax.fori_loop(0, placed, wait_rows(k, l_ref, l_sems, width, sub, 2), 0)

    @pl.when(placed > 0)
    def _():
        lax.fori_loop(0, listed, wait_rows(k, w_ref, w_sems, width, sub, 2), 0)

    steps = lax.div(listed + (CH - 1), CH)

    def one_pair(pair, carry):
        def one_place(place, inner):
            def arrived(slot, innermost):
                there = x_ref.at[k, :, block_at(place), block_at(slot)]
                pltpu.make_async_copy(there, there, x_sems.at[k, pair]).wait()
                return innermost

            return lax.fori_loop(0, listed, arrived, inner)

        lax.fori_loop(2 * pair, jnp.minimum(2 * pair + 2, placed), one_place, 0)
        rows = block_at(pair, 2 * BLK)
        for count in range(1, w_ref.shape[1] // DEPTH + 1):

            @pl.when(steps == count)
            def _(count=count):
                for half in range(2):
                    columns = w_ref.at[k, :, pl.ds(2 * half * width, 2 * width)]
                    parts = product(x_ref.at[k], columns, rows, pl.ds(0, count * DEPTH))
                    for q in range(2):
                        v_ref[:, pl.ds((2 * half + q) * width, width)] = parts[q]

        @pl.when(2 * pair + 1 >= placed)
        def _():
            v_ref[pl.ds(BLK, BLK), :] = jnp.zeros((BLK, v_ref.shape[1]), v_ref.dtype)
            l_ref[k, block_at(2 * pair + 1), :] = jnp.zeros((BLK, l_ref.shape[2]), l_ref.dtype)

        left = l_ref[k, rows, :]
        rest = v_ref[...]
        for piece in range(3):
            kept = rest.astype(jnp.bfloat16)
            r_ref[pl.ds(piece * 2 * BLK, 2 * BLK), :] = kept
            rest = rest - kept.astype(jnp.float32)
        for p in range(2):
            turned = jnp.concatenate(
                [left[:, (2 * h + p) * width : (2 * h + p + 1) * width].T for h in range(2)], axis=0
            )
            turned = jnp.concatenate([turned] * 3, axis=1)
            acc_ref[p] += jnp.dot(turned, r_ref[...], preferred_element_type=jnp.float32)
        return carry

    @pl.when((listed > 0) & (placed > 0))
    def _():
        @pl.when(lax.rem(listed, CH) != 0)
        def _():
            w_ref[k, block_at(listed), :] = jnp.zeros((BLK, w_ref.shape[2]), w_ref.dtype)
            x_ref[k, :, :, block_at(listed)] = jnp.zeros((2, x_ref.shape[2], BLK), x_ref.dtype)

        lax.fori_loop(0, lax.div(placed + 1, 2), one_pair, 0)

    core = tab_ref[0, COUNTS, 2]
    per_half = width // chunk_rows
    for half in range(2):
        first = (core if half == 0 else 1 - core) * per_half
        for i in range(per_half):
            rows = pl.ds(half * width + i * chunk_rows, chunk_rows)
            for out_ref, at in ((mine_ref, 0), (theirs_ref, 2 * width)):
                real, imag = pl.ds(at, width), pl.ds(width + at, width)
                out_ref[first + i, 0, 0] = acc_ref[0, rows, real] - acc_ref[1, rows, imag]
                out_ref[first + i, 0, 1] = acc_ref[0, rows, imag] + acc_ref[1, rows, real]


def make_values(tab, a, stacks, entries, sub):
    supernodes, early_count = stacks[0].shape[:2]
    rows, width = a.shape[1], stacks[0].shape[4]
    slots = tab.shape[2] + tab.shape[2] % CH
    tile = max(t for t in range(BLK, min(rows, 512) + 1, BLK) if rows % t == 0)
    out_spec = pl.BlockSpec((1, 2, tile, width), lambda k, m, _: (k, 0, m, 0))
    out = jax.ShapeDtypeStruct((supernodes, 2, rows, width), jnp.float32)
    return pl.pallas_call(
        functools.partial(values_kernel, entries, early_count, sub, tile),
        out_shape=(out, out),
        grid_spec=pltpu.PrefetchScalarGridSpec(
            num_scalar_prefetch=1,
            grid=(supernodes, rows // tile),
            in_specs=[pl.BlockSpec(memory_space=pl.ANY)] * 5,
            out_specs=(out_spec, out_spec),
            scratch_shapes=[
                pltpu.VMEM((supernodes, 2, rows, slots * BLK), jnp.bfloat16),
                pltpu.VMEM((supernodes, slots * BLK, 4 * width), jnp.bfloat16),
                pltpu.SemaphoreType.DMA((supernodes, rows // tile)),
                pltpu.SemaphoreType.DMA((supernodes,)),
            ],
        ),
        compiler_params=pltpu.CompilerParams(vmem_limit_bytes=42 * 2**20),
        cost_estimate=pl.CostEstimate(
            flops=2 * supernodes * rows * slots * BLK * 4 * width, bytes_accessed=16 * 2**20, transcendentals=0
        ),
        name="values",
    )(tab, a, *stacks)


def make_gram(tab, a, stacks, entries, sub, shares):
    supernodes, early_count = stacks[0].shape[:2]
    rows, width = a.shape[1], stacks[0].shape[4]
    slots = tab.shape[2] + tab.shape[2] % CH
    places = min(slots, (rows // BLK) * (BLK // sub))
    places += places % 2
    out = jax.ShapeDtypeStruct((shares, supernodes, 2, 2 * width // shares, width), jnp.float32)
    out_spec = pl.BlockSpec((shares, 1) + out.shape[2:], lambda k, _: (0, k, 0, 0, 0))
    return pl.pallas_call(
        functools.partial(gram_kernel, entries, early_count, sub),
        out_shape=(out, out),
        grid_spec=pltpu.PrefetchScalarGridSpec(
            num_scalar_prefetch=1,
            grid=(supernodes,),
            in_specs=[pl.BlockSpec(memory_space=pl.ANY)] * 5,
            out_specs=(out_spec, out_spec),
            scratch_shapes=[
                pltpu.VMEM((supernodes, 2, places * BLK, slots * BLK), jnp.bfloat16),
                pltpu.VMEM((supernodes, slots * BLK, 4 * width), jnp.bfloat16),
                pltpu.VMEM((supernodes, places * BLK, 4 * width), jnp.bfloat16),
                pltpu.VMEM((2 * BLK, 4 * width), jnp.float32),
                pltpu.VMEM((3 * 2 * BLK, 4 * width), jnp.bfloat16),
                pltpu.VMEM((2, 2 * width, 4 * width), jnp.float32),
                pltpu.SemaphoreType.DMA((supernodes, places // 2)),
                pltpu.SemaphoreType.DMA((supernodes,)),
                pltpu.SemaphoreType.DMA((supernodes,)),
            ],
        ),
        compiler_params=pltpu.CompilerParams(vmem_limit_bytes=42 * 2**20),
        cost_estimate=pl.CostEstimate(
            flops=supernodes * 2 * BLK * slots * 2 * BLK * 4 * width, bytes_accessed=8 * 2**20, transcendentals=0
        ),
        name="gram",
    )(tab, a, *stacks)


def scatter_sum(total, n_row, beside):
    if n_row & (n_row - 1):
        return jnp.sum(lax.all_to_all(total, "row", 0, 0, tiled=True), axis=0, keepdims=True), beside
    row, bit = lax.axis_index("row"), 1
    while bit < n_row:
        mine = row // bit % 2
        pairs = total.reshape((total.shape[0] // 2, 2) + total.shape[1:])
        route = [(i, i ^ bit) for i in range(n_row)]
        came = lax.ppermute(lax.dynamic_index_in_dim(pairs, 1 - mine, 1, keepdims=False), "row", route)
        if bit == 1:
            came, beside = lax.optimization_barrier((came, beside))
        total = lax.dynamic_index_in_dim(pairs, mine, 1, keepdims=False) + came
        bit *= 2
    return total, beside


def local(n_row, inverse_pairs, factor_rows, diag_blocks, row_lists, block_order):
    supernodes = row_lists.shape[0]
    local_rows, local_cols = inverse_pairs.shape[1:]
    per_chip = factor_rows.shape[2]
    sub = min(BLK, per_chip)
    entries = per_chip // sub
    half = n_row // 2
    cycle = list(range(0, n_row, 2)) + list(range(n_row - 1, 0, -2))
    ahead = [(cycle[i], cycle[(i + 1) % n_row]) for i in range(n_row)]
    behind = [(b, a) for a, b in ahead]
    swap = [(0, 1), (1, 0)]

    tab = make_table(n_row, entries, sub, local_cols // BLK, local_rows // BLK, row_lists, block_order)

    chunks = [[factor_rows[k]] for k in range(supernodes)]
    up = [factor_rows[k] for k in range(supernodes)]
    down = list(up)
    for d in range(1, half):
        for k in range(supernodes):
            up[k] = lax.ppermute(up[k], "row", ahead)
            down[k] = lax.ppermute(down[k], "row", behind)
            chunks[k] += [up[k], down[k]]
        if d == 1:
            up[0], tab = lax.optimization_barrier((up[0], tab))
    for k in range(supernodes):
        last = [lax.ppermute(up[k][0:1], "row", ahead), lax.ppermute(down[k][1:2], "row", behind)]
        chunks[k].append(jnp.concatenate(last, axis=0))
    early = max(1, n_row - 3)
    own = [
        jnp.stack([jnp.stack(chunks[k][:early]) for k in range(supernodes)]),
        jnp.stack([jnp.stack(chunks[k][early:]) for k in range(supernodes)]),
    ]
    stacks = own + [lax.ppermute(x, "col", swap) for x in own]

    mine, theirs = make_gram(tab, inverse_pairs, stacks, entries, sub, n_row)
    total = mine + lax.ppermute(theirs, "col", swap)
    total, tab = lax.optimization_barrier((total, tab))
    mine, theirs = make_values(tab, inverse_pairs, stacks, entries, sub)
    share, theirs = scatter_sum(total, n_row, theirs)
    values = mine + lax.ppermute(theirs, "col", swap)
    shares = lax.all_to_all(jnp.broadcast_to(share, total.shape), "row", 0, 0, tiled=True)
    gram = jnp.moveaxis(shares, 0, 2).reshape(diag_blocks.shape)
    return (values, diag_blocks.astype(jnp.float32) - gram)


def solution(mesh):
    in_specs = (
        P("pole", "row", "col"),
        P("pole", None, "row", "col"),
        P("pole", None, None, "col"),
        P(),
        P(),
    )
    out_specs = (P("pole", None, "row", "col"), P("pole", None, None, "col"))
    body = functools.partial(local, mesh.shape["row"])
    return jax.shard_map(body, mesh=mesh, in_specs=in_specs, out_specs=out_specs, check_vma=False)
```

```python
import functools
import math

import jax
import jax.numpy as jnp
from jax import lax
from jax.experimental import pallas as pl
from jax.experimental.pallas import tpu as pltpu
from jax.sharding import PartitionSpec as P

BLK = 128
CH = 2
DEPTH = CH * BLK
COL_ENTRY, COL_BLOCK, ROW_ENTRY, ROW_BLOCK, OFFSET, COUNTS = range(6)


def block_at(index, size=BLK):
    return pl.ds(pl.multiple_of(index * size, size), size)


def table_kernel(n_row, entries, sub, col_blocks, row_blocks, lists_ref, order_ref, tab_ref, where_ref):
    half = n_row // 2
    row, core = lax.axis_index("row"), lax.axis_index("col")
    place = jnp.where(lax.rem(row, 2) == 0, lax.div(row, 2), n_row - 1 - lax.div(row, 2))

    def invert(g, carry):
        where_ref[order_ref[g]] = g
        return carry

    lax.fori_loop(0, order_ref.shape[0], invert, 0, unroll=8)
    for k in range(tab_ref.shape[0]):

        def one(i, counts, k=k):
            listed, placed = counts
            chunk, at = lax.div(i, entries), lax.rem(i, entries)
            step = lax.div(chunk + 1, 2)
            step = jnp.where((lax.rem(chunk, 2) == 1) | (chunk == n_row - 1), step, -step)
            source = lax.rem(place - step + 2 * n_row, n_row)
            source = jnp.where(source < half, 2 * source, 2 * (n_row - 1 - source) + 1)
            first = source * (entries * sub) + at * sub
            block = where_ref[lists_ref[k, lax.div(first, BLK)]]
            tab_ref[k, OFFSET, i] = lax.rem(first, BLK)
            col, line = block - core * col_blocks, block - row * row_blocks
            is_col = (col >= 0) & (col < col_blocks)
            is_row = (line >= 0) & (line < row_blocks)

            @pl.when(is_col)
            def _():
                tab_ref[k, COL_ENTRY, listed] = i
                tab_ref[k, COL_BLOCK, listed] = col

            @pl.when(is_row)
            def _():
                tab_ref[k, ROW_ENTRY, placed] = i
                tab_ref[k, ROW_BLOCK, placed] = line

            return listed + is_col.astype(jnp.int32), placed + is_row.astype(jnp.int32)

        listed, placed = lax.fori_loop(0, n_row * entries, one, (jnp.int32(0), jnp.int32(0)), unroll=4)
        tab_ref[k, COUNTS, 0] = listed
        tab_ref[k, COUNTS, 1] = placed
        tab_ref[k, COUNTS, 2] = core


def make_table(n_row, entries, sub, col_blocks, row_blocks, row_lists, block_order):
    smem = pl.BlockSpec(memory_space=pltpu.SMEM)
    return pl.pallas_call(
        functools.partial(table_kernel, n_row, entries, sub, col_blocks, row_blocks),
        out_shape=jax.ShapeDtypeStruct((row_lists.shape[0], 6, max(n_row * entries, 3)), jnp.int32),
        in_specs=[smem] * 2,
        out_specs=smem,
        scratch_shapes=[pltpu.SMEM(block_order.shape, jnp.int32)],
        name="table",
    )(row_lists, block_order)


def start_rows(tab_ref, kind, k, to_ref, sems, halves, entries, early_count, sub):
    def one(at, carry):
        entry = tab_ref[k, kind, at]
        chunk, part = lax.div(entry, entries), lax.rem(entry, entries)
        rows = block_at(at)
        if sub < BLK:
            to_ref[k, rows, :] = jnp.zeros((BLK, to_ref.shape[2]), to_ref.dtype)
            rows = pl.ds(pl.multiple_of(at * BLK + tab_ref[k, OFFSET, entry], sub), sub)

        def copy(stack, chunk, there, p):
            here = stack.at[k, chunk, p, block_at(part, sub), :]
            pltpu.make_async_copy(here, there, sems.at[k]).start()

        for half, stacks in enumerate(halves):
            width = stacks[0].shape[4]
            for p in range(2):
                there = to_ref.at[k, rows, pl.ds((2 * half + p) * width, width)]

                @pl.when(chunk < early_count)
                def _(stacks=stacks, there=there, p=p):
                    copy(stacks[0], chunk, there, p)

                @pl.when(chunk >= early_count)
                def _(stacks=stacks, there=there, p=p):
                    copy(stacks[1], chunk - early_count, there, p)

        return carry

    return one


def wait_rows(k, to_ref, sems, width, sub, halves):
    def one(at, carry):
        there = to_ref.at[k, pl.ds(0, sub), pl.ds(0, 2 * halves * width)]
        pltpu.make_async_copy(there, there, sems.at[k]).wait()
        return carry

    return one


def product(x, w, x_rows, depth):
    width = w.shape[1] // 2
    real, imag = (
        jnp.dot(x[p, x_rows, depth], w[depth, :], preferred_element_type=jnp.float32) for p in range(2)
    )
    return imag[:, width:] - real[:, :width], -(real[:, width:] + imag[:, :width])


def values_kernel(entries, early_count, sub, tile, tab_ref, a_ref, own0, own1, sib0, sib1, *refs):
    mine_ref, theirs_ref, x_ref, w_ref, x_sems, w_sems = refs
    k, step = pl.program_id(0), pl.program_id(1)
    supernodes, tiles = pl.num_programs(0), pl.num_programs(1)
    width = mine_ref.shape[3]
    listed = tab_ref[k, COUNTS, 0]
    now = k * tiles + step

    def start(at):
        which, rows, buffer = lax.div(at, tiles), lax.rem(at, tiles), lax.rem(at, 2)

        def one(slot, carry):
            pltpu.make_async_copy(
                a_ref.at[:, block_at(rows, tile), block_at(tab_ref[which, COL_BLOCK, slot])],
                x_ref.at[buffer, :, :, block_at(slot)],
                x_sems.at[buffer],
            ).start()
            return carry

        lax.fori_loop(0, tab_ref[which, COUNTS, 0], one, 0)

    @pl.when(now == 0)
    def _():
        for which in range(w_ref.shape[0]):
            rows = start_rows(
                tab_ref, COL_ENTRY, which, w_ref, w_sems, ((own0, own1), (sib0, sib1)), entries, early_count, sub
            )
            lax.fori_loop(0, tab_ref[which, COUNTS, 0], rows, 0)
            if which == 0:
                start(now)

    @pl.when(now + 1 < supernodes * tiles)
    def _():
        start(now + 1)

    @pl.when(step == 0)
    def _():
        @pl.when(lax.rem(listed, CH) != 0)
        def _():
            w_ref[k, block_at(listed), :] = jnp.zeros((BLK, w_ref.shape[2]), w_ref.dtype)

        lax.fori_loop(0, listed, wait_rows(k, w_ref, w_sems, width, sub, 2), 0)

    buffer = lax.rem(now, 2)

    @pl.when(lax.rem(listed, CH) != 0)
    def _():
        x_ref[buffer, :, :, block_at(listed)] = jnp.zeros((2, tile, BLK), x_ref.dtype)

    def arrived(slot, carry):
        there = x_ref.at[buffer, :, :, block_at(slot)]
        pltpu.make_async_copy(there, there, x_sems.at[buffer]).wait()
        return carry

    lax.fori_loop(0, listed, arrived, 0)
    steps = lax.div(listed + (CH - 1), CH)

    @pl.when(steps == 0)
    def _():
        mine_ref[...] = jnp.zeros_like(mine_ref)
        theirs_ref[...] = jnp.zeros_like(theirs_ref)

    for count in range(1, w_ref.shape[1] // DEPTH + 1):

        @pl.when(steps == count)
        def _(count=count):
            for half, out_ref in enumerate((mine_ref, theirs_ref)):
                columns = w_ref.at[k, :, pl.ds(2 * half * width, 2 * width)]
                parts = product(x_ref.at[buffer], columns, pl.ds(0, tile), pl.ds(0, count * DEPTH))
                for q in range(2):
                    out_ref[0, q] = parts[q]


def gram_kernel(entries, early_count, sub, tab_ref, a_ref, own0, own1, sib0, sib1, *refs):
    mine_ref, theirs_ref, x_ref, w_ref, l_ref, v_ref, r_ref, acc_ref, x_sems, w_sems, l_sems = refs
    k = pl.program_id(0)
    own, sib = (own0, own1), (sib0, sib1)
    width = mine_ref.shape[4]
    chunk_rows = mine_ref.shape[3]
    listed, placed = tab_ref[k, COUNTS, 0], tab_ref[k, COUNTS, 1]

    def start_pair(which, pair):
        def one_place(place, carry):
            rows = block_at(tab_ref[which, ROW_BLOCK, place])

            def one(slot, inner):
                pltpu.make_async_copy(
                    a_ref.at[:, rows, block_at(tab_ref[which, COL_BLOCK, slot])],
                    x_ref.at[which, lax.rem(pair, 2), :, block_at(place - 2 * pair), block_at(slot)],
                    x_sems.at[which, lax.rem(pair, 2)],
                ).start()
                return inner

            return lax.fori_loop(0, tab_ref[which, COUNTS, 0], one, carry)

        lax.fori_loop(2 * pair, jnp.minimum(2 * pair + 2, tab_ref[which, COUNTS, 1]), one_place, 0)

    @pl.when(k == 0)
    def _():
        for which in range(x_ref.shape[0]):
            stacks = ((own, sib), entries, early_count, sub)
            there = tab_ref[which, COUNTS, 1]
            lax.fori_loop(0, there, start_rows(tab_ref, ROW_ENTRY, which, l_ref, l_sems, *stacks), 0)

            @pl.when(there > 0)
            def _(which=which, stacks=stacks):
                lax.fori_loop(
                    0, tab_ref[which, COUNTS, 0], start_rows(tab_ref, COL_ENTRY, which, w_ref, w_sems, *stacks), 0
                )

            start_pair(which, 0)

    acc_ref[...] = jnp.zeros_like(acc_ref)
    odd = lax.rem(listed, CH) != 0
    steps = lax.div(listed + (CH - 1), CH)
    lax.fori_loop(0, placed, wait_rows(k, l_ref, l_sems, width, sub, 2), 0)

    @pl.when(placed > 0)
    def _():
        lax.fori_loop(0, listed, wait_rows(k, w_ref, w_sems, width, sub, 2), 0)

    def one_pair(pair, carry):
        start_pair(k, pair + 1)
        buffer = lax.rem(pair, 2)

        @pl.when(odd)
        def _():
            x_ref[k, buffer, :, :, block_at(listed)] = jnp.zeros((2, 2 * BLK, BLK), x_ref.dtype)

        def one_place(place, inner):
            def arrived(slot, innermost):
                there = x_ref.at[k, buffer, :, block_at(place - 2 * pair), block_at(slot)]
                pltpu.make_async_copy(there, there, x_sems.at[k, buffer]).wait()
                return innermost

            return lax.fori_loop(0, listed, arrived, inner)

        lax.fori_loop(2 * pair, jnp.minimum(2 * pair + 2, placed), one_place, 0)
        for count in range(1, w_ref.shape[1] // DEPTH + 1):

            @pl.when(steps == count)
            def _(count=count):
                for half in range(2):
                    columns = w_ref.at[k, :, pl.ds(2 * half * width, 2 * width)]
                    parts = product(x_ref.at[k, buffer], columns, pl.ds(0, 2 * BLK), pl.ds(0, count * DEPTH))
                    for q in range(2):
                        v_ref[:, pl.ds((2 * half + q) * width, width)] = parts[q]

        @pl.when(2 * pair + 1 >= placed)
        def _():
            v_ref[pl.ds(BLK, BLK), :] = jnp.zeros((BLK, v_ref.shape[1]), v_ref.dtype)
            l_ref[k, block_at(2 * pair + 1), :] = jnp.zeros((BLK, l_ref.shape[2]), l_ref.dtype)

        left = l_ref[k, block_at(pair, 2 * BLK), :]
        rest = v_ref[...]
        for piece in range(3):
            kept = rest.astype(jnp.bfloat16)
            r_ref[pl.ds(piece * 2 * BLK, 2 * BLK), :] = kept
            rest = rest - kept.astype(jnp.float32)
        for p in range(2):
            turned = jnp.concatenate(
                [left[:, (2 * h + p) * width : (2 * h + p + 1) * width].T for h in range(2)], axis=0
            )
            turned = jnp.concatenate([turned] * 3, axis=1)
            acc_ref[p] += jnp.dot(turned, r_ref[...], preferred_element_type=jnp.float32)
        return carry

    @pl.when((listed > 0) & (placed > 0))
    def _():
        @pl.when(odd)
        def _():
            w_ref[k, block_at(listed), :] = jnp.zeros((BLK, w_ref.shape[2]), w_ref.dtype)

        lax.fori_loop(0, lax.div(placed + 1, 2), one_pair, 0)

    core = tab_ref[0, COUNTS, 2]
    per_half = width // chunk_rows
    for half in range(2):
        first = (core if half == 0 else 1 - core) * per_half
        for i in range(per_half):
            rows = pl.ds(half * width + i * chunk_rows, chunk_rows)
            for out_ref, at in ((mine_ref, 0), (theirs_ref, 2 * width)):
                real, imag = pl.ds(at, width), pl.ds(width + at, width)
                out_ref[first + i, 0, 0] = acc_ref[0, rows, real] - acc_ref[1, rows, imag]
                out_ref[first + i, 0, 1] = acc_ref[0, rows, imag] + acc_ref[1, rows, real]


def vmem_limit(scratch, blocks):
    held = [x for x in scratch if x.dtype in (jnp.bfloat16, jnp.float32)]
    size = sum(math.prod(x.shape) * jnp.dtype(x.dtype).itemsize for x in held)
    return size + 2 * sum(math.prod(shape) * 4 for shape in blocks) + 8 * 2**20


def make_values(tab, a, stacks, entries, sub):
    supernodes, early_count = stacks[0].shape[:2]
    rows, width = a.shape[1], stacks[0].shape[4]
    slots = tab.shape[2] + tab.shape[2] % CH
    tile = max(t for t in range(BLK, min(rows, 256) + 1, BLK) if rows % t == 0)
    out_spec = pl.BlockSpec((1, 2, tile, width), lambda k, m, _: (k, 0, m, 0))
    out = jax.ShapeDtypeStruct((supernodes, 2, rows, width), jnp.float32)
    scratch = [
        pltpu.VMEM((2, 2, tile, slots * BLK), jnp.bfloat16),
        pltpu.VMEM((supernodes, slots * BLK, 4 * width), jnp.bfloat16),
        pltpu.SemaphoreType.DMA((2,)),
        pltpu.SemaphoreType.DMA((supernodes,)),
    ]
    return pl.pallas_call(
        functools.partial(values_kernel, entries, early_count, sub, tile),
        out_shape=(out, out),
        grid_spec=pltpu.PrefetchScalarGridSpec(
            num_scalar_prefetch=1,
            grid=(supernodes, rows // tile),
            in_specs=[pl.BlockSpec(memory_space=pl.ANY)] * 5,
            out_specs=(out_spec, out_spec),
            scratch_shapes=scratch,
        ),
        compiler_params=pltpu.CompilerParams(vmem_limit_bytes=vmem_limit(scratch, [(2, tile, width)] * 2)),
        cost_estimate=pl.CostEstimate(
            flops=2 * supernodes * rows * slots * BLK * 4 * width, bytes_accessed=16 * 2**20, transcendentals=0
        ),
        name="values",
    )(tab, a, *stacks)


def make_gram(tab, a, stacks, entries, sub, shares):
    supernodes, early_count = stacks[0].shape[:2]
    rows, width = a.shape[1], stacks[0].shape[4]
    slots = tab.shape[2] + tab.shape[2] % CH
    places = min(slots, (rows // BLK) * (BLK // sub))
    places += places % 2
    out = jax.ShapeDtypeStruct((shares, supernodes, 2, 2 * width // shares, width), jnp.float32)
    out_spec = pl.BlockSpec((shares, 1) + out.shape[2:], lambda k, _: (0, k, 0, 0, 0))
    scratch = [
        pltpu.VMEM((supernodes, 2, 2, 2 * BLK, slots * BLK), jnp.bfloat16),
        pltpu.VMEM((supernodes, slots * BLK, 4 * width), jnp.bfloat16),
        pltpu.VMEM((supernodes, places * BLK, 4 * width), jnp.bfloat16),
        pltpu.VMEM((2 * BLK, 4 * width), jnp.float32),
        pltpu.VMEM((3 * 2 * BLK, 4 * width), jnp.bfloat16),
        pltpu.VMEM((2, 2 * width, 4 * width), jnp.float32),
        pltpu.SemaphoreType.DMA((supernodes, 2)),
        pltpu.SemaphoreType.DMA((supernodes,)),
        pltpu.SemaphoreType.DMA((supernodes,)),
    ]
    return pl.pallas_call(
        functools.partial(gram_kernel, entries, early_count, sub),
        out_shape=(out, out),
        grid_spec=pltpu.PrefetchScalarGridSpec(
            num_scalar_prefetch=1,
            grid=(supernodes,),
            in_specs=[pl.BlockSpec(memory_space=pl.ANY)] * 5,
            out_specs=(out_spec, out_spec),
            scratch_shapes=scratch,
        ),
        compiler_params=pltpu.CompilerParams(vmem_limit_bytes=vmem_limit(scratch, [out.shape] * 2)),
        cost_estimate=pl.CostEstimate(
            flops=supernodes * 2 * BLK * slots * 2 * BLK * 4 * width, bytes_accessed=8 * 2**20, transcendentals=0
        ),
        name="gram",
    )(tab, a, *stacks)


def local(n_row, inverse_pairs, factor_rows, diag_blocks, row_lists, block_order):
    supernodes = row_lists.shape[0]
    local_rows, local_cols = inverse_pairs.shape[1:]
    per_chip = factor_rows.shape[2]
    sub = min(BLK, per_chip)
    entries = per_chip // sub
    half = n_row // 2
    cycle = list(range(0, n_row, 2)) + list(range(n_row - 1, 0, -2))
    ahead = [(cycle[i], cycle[(i + 1) % n_row]) for i in range(n_row)]
    behind = [(b, a) for a, b in ahead]
    swap = [(0, 1), (1, 0)]

    tab = make_table(n_row, entries, sub, local_cols // BLK, local_rows // BLK, row_lists, block_order)

    chunks = [[factor_rows[k]] for k in range(supernodes)]
    up = [factor_rows[k] for k in range(supernodes)]
    down = list(up)
    for d in range(1, half):
        for k in range(supernodes):
            up[k] = lax.ppermute(up[k], "row", ahead)
            down[k] = lax.ppermute(down[k], "row", behind)
            chunks[k] += [up[k], down[k]]
        if d == 1:
            up[0], tab = lax.optimization_barrier((up[0], tab))
    for k in range(supernodes):
        last = [lax.ppermute(up[k][0:1], "row", ahead), lax.ppermute(down[k][1:2], "row", behind)]
        chunks[k].append(jnp.concatenate(last, axis=0))
    early = max(1, n_row - 3)
    own = [
        jnp.stack([jnp.stack(chunks[k][:early]) for k in range(supernodes)]),
        jnp.stack([jnp.stack(chunks[k][early:]) for k in range(supernodes)]),
    ]
    stacks = own + [lax.ppermute(x, "col", swap) for x in own]

    mine, theirs = make_gram(tab, inverse_pairs, stacks, entries, sub, n_row)
    total = mine + lax.ppermute(theirs, "col", swap)
    total, tab = lax.optimization_barrier((total, tab))
    share = jnp.sum(lax.all_to_all(total, "row", 0, 0, tiled=True), axis=0)
    shares = lax.all_to_all(jnp.broadcast_to(share[None], total.shape), "row", 0, 0, tiled=True)
    gram = jnp.moveaxis(shares, 0, 2).reshape(diag_blocks.shape)
    schur = diag_blocks.astype(jnp.float32) - gram

    mine, theirs = make_values(tab, inverse_pairs, stacks, entries, sub)
    return (mine + lax.ppermute(theirs, "col", swap), schur)


def solution(mesh):
    in_specs = (
        P("pole", "row", "col"),
        P("pole", None, "row", "col"),
        P("pole", None, None, "col"),
        P(),
        P(),
    )
    out_specs = (P("pole", None, "row", "col"), P("pole", None, None, "col"))
    body = functools.partial(local, mesh.shape["row"])
    return jax.shard_map(body, mesh=mesh, in_specs=in_specs, out_specs=out_specs, check_vma=False)
```

```python
import functools
import math

import jax
import jax.numpy as jnp
from jax import lax
from jax.experimental import pallas as pl
from jax.experimental.pallas import tpu as pltpu
from jax.sharding import PartitionSpec as P

BLK = 128
CH = 2
DEPTH = CH * BLK
COL_ENTRY, COL_BLOCK, ROW_ENTRY, ROW_BLOCK, OFFSET, COUNTS = range(6)


def block_at(index, size=BLK):
    return pl.ds(pl.multiple_of(index * size, size), size)


def table_kernel(n_row, entries, sub, col_blocks, row_blocks, lists_ref, order_ref, tab_ref, where_ref):
    half = n_row // 2
    row, core = lax.axis_index("row"), lax.axis_index("col")
    place = jnp.where(lax.rem(row, 2) == 0, lax.div(row, 2), n_row - 1 - lax.div(row, 2))

    def invert(g, carry):
        where_ref[order_ref[g]] = g
        return carry

    lax.fori_loop(0, order_ref.shape[0], invert, 0, unroll=8)
    for k in range(tab_ref.shape[0]):

        def one(i, counts, k=k):
            listed, placed = counts
            chunk, at = lax.div(i, entries), lax.rem(i, entries)
            step = lax.div(chunk + 1, 2)
            step = jnp.where((lax.rem(chunk, 2) == 1) | (chunk == n_row - 1), step, -step)
            source = lax.rem(place - step + 2 * n_row, n_row)
            source = jnp.where(source < half, 2 * source, 2 * (n_row - 1 - source) + 1)
            first = source * (entries * sub) + at * sub
            block = where_ref[lists_ref[k, lax.div(first, BLK)]]
            tab_ref[k, OFFSET, i] = lax.rem(first, BLK)
            col, line = block - core * col_blocks, block - row * row_blocks
            is_col = (col >= 0) & (col < col_blocks)
            is_row = (line >= 0) & (line < row_blocks)

            @pl.when(is_col)
            def _():
                tab_ref[k, COL_ENTRY, listed] = i
                tab_ref[k, COL_BLOCK, listed] = col

            @pl.when(is_row)
            def _():
                tab_ref[k, ROW_ENTRY, placed] = i
                tab_ref[k, ROW_BLOCK, placed] = line

            return listed + is_col.astype(jnp.int32), placed + is_row.astype(jnp.int32)

        listed, placed = lax.fori_loop(0, n_row * entries, one, (jnp.int32(0), jnp.int32(0)), unroll=4)
        tab_ref[k, COUNTS, 0] = listed
        tab_ref[k, COUNTS, 1] = placed
        tab_ref[k, COUNTS, 2] = core


def make_table(n_row, entries, sub, col_blocks, row_blocks, row_lists, block_order):
    smem = pl.BlockSpec(memory_space=pltpu.SMEM)
    return pl.pallas_call(
        functools.partial(table_kernel, n_row, entries, sub, col_blocks, row_blocks),
        out_shape=jax.ShapeDtypeStruct((row_lists.shape[0], 6, max(n_row * entries, 3)), jnp.int32),
        in_specs=[smem] * 2,
        out_specs=smem,
        scratch_shapes=[pltpu.SMEM(block_order.shape, jnp.int32)],
        name="table",
    )(row_lists, block_order)


def start_rows(tab_ref, kind, k, to_ref, sems, halves, entries, early_count, sub):
    def one(at, carry):
        entry = tab_ref[k, kind, at]
        chunk, part = lax.div(entry, entries), lax.rem(entry, entries)
        rows = block_at(at)
        if sub < BLK:
            to_ref[k, rows, :] = jnp.zeros((BLK, to_ref.shape[2]), to_ref.dtype)
            rows = pl.ds(pl.multiple_of(at * BLK + tab_ref[k, OFFSET, entry], sub), sub)

        def copy(stack, chunk, there, p):
            here = stack.at[k, chunk, p, block_at(part, sub), :]
            pltpu.make_async_copy(here, there, sems.at[k]).start()

        for half, stacks in enumerate(halves):
            width = stacks[0].shape[4]
            for p in range(2):
                there = to_ref.at[k, rows, pl.ds((2 * half + p) * width, width)]

                @pl.when(chunk < early_count)
                def _(stacks=stacks, there=there, p=p):
                    copy(stacks[0], chunk, there, p)

                @pl.when(chunk >= early_count)
                def _(stacks=stacks, there=there, p=p):
                    copy(stacks[1], chunk - early_count, there, p)

        return carry

    return one


def wait_rows(k, to_ref, sems, width, sub, halves):
    def one(at, carry):
        there = to_ref.at[k, pl.ds(0, sub), pl.ds(0, 2 * halves * width)]
        pltpu.make_async_copy(there, there, sems.at[k]).wait()
        return carry

    return one


def product(x, w, x_rows, depth):
    width = w.shape[1] // 2
    real, imag = (
        jnp.dot(x[p, x_rows, depth], w[depth, :], preferred_element_type=jnp.float32) for p in range(2)
    )
    return imag[:, width:] - real[:, :width], -(real[:, width:] + imag[:, :width])


def values_kernel(entries, early_count, sub, tile, tab_ref, a_ref, own0, own1, sib0, sib1, *refs):
    mine_ref, theirs_ref, x_ref, w_ref, x_sems, w_sems = refs
    k, step = pl.program_id(0), pl.program_id(1)
    supernodes, tiles = pl.num_programs(0), pl.num_programs(1)
    width = mine_ref.shape[3]
    listed = tab_ref[k, COUNTS, 0]
    now = k * tiles + step

    def start(at):
        which, rows, buffer = lax.div(at, tiles), lax.rem(at, tiles), lax.rem(at, 2)

        def one(slot, carry):
            pltpu.make_async_copy(
                a_ref.at[:, block_at(rows, tile), block_at(tab_ref[which, COL_BLOCK, slot])],
                x_ref.at[buffer, :, :, block_at(slot)],
                x_sems.at[buffer],
            ).start()
            return carry

        lax.fori_loop(0, tab_ref[which, COUNTS, 0], one, 0)

    @pl.when(now == 0)
    def _():
        for which in range(w_ref.shape[0]):
            rows = start_rows(
                tab_ref, COL_ENTRY, which, w_ref, w_sems, ((own0, own1), (sib0, sib1)), entries, early_count, sub
            )
            lax.fori_loop(0, tab_ref[which, COUNTS, 0], rows, 0)
            if which == 0:
                start(now)

    @pl.when(now + 1 < supernodes * tiles)
    def _():
        start(now + 1)

    @pl.when(step == 0)
    def _():
        @pl.when(lax.rem(listed, CH) != 0)
        def _():
            w_ref[k, block_at(listed), :] = jnp.zeros((BLK, w_ref.shape[2]), w_ref.dtype)

        lax.fori_loop(0, listed, wait_rows(k, w_ref, w_sems, width, sub, 2), 0)

    buffer = lax.rem(now, 2)

    @pl.when(lax.rem(listed, CH) != 0)
    def _():
        x_ref[buffer, :, :, block_at(listed)] = jnp.zeros((2, tile, BLK), x_ref.dtype)

    def arrived(slot, carry):
        there = x_ref.at[buffer, :, :, block_at(slot)]
        pltpu.make_async_copy(there, there, x_sems.at[buffer]).wait()
        return carry

    lax.fori_loop(0, listed, arrived, 0)
    steps = lax.div(listed + (CH - 1), CH)

    @pl.when(steps == 0)
    def _():
        mine_ref[...] = jnp.zeros_like(mine_ref)
        theirs_ref[...] = jnp.zeros_like(theirs_ref)

    for count in range(1, w_ref.shape[1] // DEPTH + 1):

        @pl.when(steps == count)
        def _(count=count):
            for half, out_ref in enumerate((mine_ref, theirs_ref)):
                columns = w_ref.at[k, :, pl.ds(2 * half * width, 2 * width)]
                parts = product(x_ref.at[buffer], columns, pl.ds(0, tile), pl.ds(0, count * DEPTH))
                for q in range(2):
                    out_ref[0, q] = parts[q]


def gram_kernel(entries, early_count, sub, tab_ref, a_ref, own0, own1, sib0, sib1, *refs):
    mine_ref, theirs_ref, x_ref, w_ref, l_ref, v_ref, r_ref, acc_ref, x_sems, w_sems, l_sems = refs
    k = pl.program_id(0)
    own, sib = (own0, own1), (sib0, sib1)
    width = mine_ref.shape[4]
    chunk_rows = mine_ref.shape[3]
    listed, placed = tab_ref[k, COUNTS, 0], tab_ref[k, COUNTS, 1]

    def start_pair(which, pair):
        def one_place(place, carry):
            rows = block_at(tab_ref[which, ROW_BLOCK, place])

            def one(slot, inner):
                pltpu.make_async_copy(
                    a_ref.at[:, rows, block_at(tab_ref[which, COL_BLOCK, slot])],
                    x_ref.at[which, lax.rem(pair, 2), :, block_at(place - 2 * pair), block_at(slot)],
                    x_sems.at[which, lax.rem(pair, 2)],
                ).start()
                return inner

            return lax.fori_loop(0, tab_ref[which, COUNTS, 0], one, carry)

        lax.fori_loop(2 * pair, jnp.minimum(2 * pair + 2, tab_ref[which, COUNTS, 1]), one_place, 0)

    @pl.when(k == 0)
    def _():
        for which in range(x_ref.shape[0]):
            stacks = ((own, sib), entries, early_count, sub)
            there = tab_ref[which, COUNTS, 1]
            lax.fori_loop(0, there, start_rows(tab_ref, ROW_ENTRY, which, l_ref, l_sems, *stacks), 0)

            @pl.when(there > 0)
            def _(which=which, stacks=stacks):
                lax.fori_loop(
                    0, tab_ref[which, COUNTS, 0], start_rows(tab_ref, COL_ENTRY, which, w_ref, w_sems, *stacks), 0
                )

            start_pair(which, 0)

    acc_ref[...] = jnp.zeros_like(acc_ref)
    odd = lax.rem(listed, CH) != 0
    steps = lax.div(listed + (CH - 1), CH)
    lax.fori_loop(0, placed, wait_rows(k, l_ref, l_sems, width, sub, 2), 0)

    @pl.when(placed > 0)
    def _():
        lax.fori_loop(0, listed, wait_rows(k, w_ref, w_sems, width, sub, 2), 0)

    def one_pair(pair, carry):
        start_pair(k, pair + 1)
        buffer = lax.rem(pair, 2)

        @pl.when(odd)
        def _():
            x_ref[k, buffer, :, :, block_at(listed)] = jnp.zeros((2, 2 * BLK, BLK), x_ref.dtype)

        def one_place(place, inner):
            def arrived(slot, innermost):
                there = x_ref.at[k, buffer, :, block_at(place - 2 * pair), block_at(slot)]
                pltpu.make_async_copy(there, there, x_sems.at[k, buffer]).wait()
                return innermost

            return lax.fori_loop(0, listed, arrived, inner)

        lax.fori_loop(2 * pair, jnp.minimum(2 * pair + 2, placed), one_place, 0)
        for count in range(1, w_ref.shape[1] // DEPTH + 1):

            @pl.when(steps == count)
            def _(count=count):
                for half in range(2):
                    columns = w_ref.at[k, :, pl.ds(2 * half * width, 2 * width)]
                    parts = product(x_ref.at[k, buffer], columns, pl.ds(0, 2 * BLK), pl.ds(0, count * DEPTH))
                    for q in range(2):
                        v_ref[:, pl.ds((2 * half + q) * width, width)] = parts[q]

        @pl.when(2 * pair + 1 >= placed)
        def _():
            v_ref[pl.ds(BLK, BLK), :] = jnp.zeros((BLK, v_ref.shape[1]), v_ref.dtype)
            l_ref[k, block_at(2 * pair + 1), :] = jnp.zeros((BLK, l_ref.shape[2]), l_ref.dtype)

        left = l_ref[k, block_at(pair, 2 * BLK), :]
        rest = v_ref[...]
        for piece in range(3):
            kept = rest.astype(jnp.bfloat16)
            r_ref[pl.ds(piece * 2 * BLK, 2 * BLK), :] = kept
            rest = rest - kept.astype(jnp.float32)
        for p in range(2):
            turned = jnp.concatenate(
                [left[:, (2 * h + p) * width : (2 * h + p + 1) * width].T for h in range(2)], axis=0
            )
            turned = jnp.concatenate([turned] * 3, axis=1)
            acc_ref[p] += jnp.dot(turned, r_ref[...], preferred_element_type=jnp.float32)
        return carry

    @pl.when((listed > 0) & (placed > 0))
    def _():
        @pl.when(odd)
        def _():
            w_ref[k, block_at(listed), :] = jnp.zeros((BLK, w_ref.shape[2]), w_ref.dtype)

        lax.fori_loop(0, lax.div(placed + 1, 2), one_pair, 0)

    core = tab_ref[0, COUNTS, 2]
    per_half = width // chunk_rows
    for half in range(2):
        first = (core if half == 0 else 1 - core) * per_half
        for i in range(per_half):
            rows = pl.ds(half * width + i * chunk_rows, chunk_rows)
            for out_ref, at in ((mine_ref, 0), (theirs_ref, 2 * width)):
                real, imag = pl.ds(at, width), pl.ds(width + at, width)
                out_ref[first + i, 0, 0] = acc_ref[0, rows, real] - acc_ref[1, rows, imag]
                out_ref[first + i, 0, 1] = acc_ref[0, rows, imag] + acc_ref[1, rows, real]


def vmem_limit(scratch, blocks):
    held = [x for x in scratch if x.dtype in (jnp.bfloat16, jnp.float32)]
    size = sum(math.prod(x.shape) * jnp.dtype(x.dtype).itemsize for x in held)
    return size + 2 * sum(math.prod(shape) * 4 for shape in blocks) + 8 * 2**20


def make_values(tab, a, stacks, entries, sub):
    supernodes, early_count = stacks[0].shape[:2]
    rows, width = a.shape[1], stacks[0].shape[4]
    slots = tab.shape[2] + tab.shape[2] % CH
    tile = max(t for t in range(BLK, min(rows, 768) + 1, BLK) if rows % t == 0)
    out_spec = pl.BlockSpec((1, 2, tile, width), lambda k, m, _: (k, 0, m, 0))
    out = jax.ShapeDtypeStruct((supernodes, 2, rows, width), jnp.float32)
    scratch = [
        pltpu.VMEM((2, 2, tile, slots * BLK), jnp.bfloat16),
        pltpu.VMEM((supernodes, slots * BLK, 4 * width), jnp.bfloat16),
        pltpu.SemaphoreType.DMA((2,)),
        pltpu.SemaphoreType.DMA((supernodes,)),
    ]
    return pl.pallas_call(
        functools.partial(values_kernel, entries, early_count, sub, tile),
        out_shape=(out, out),
        grid_spec=pltpu.PrefetchScalarGridSpec(
            num_scalar_prefetch=1,
            grid=(supernodes, rows // tile),
            in_specs=[pl.BlockSpec(memory_space=pl.ANY)] * 5,
            out_specs=(out_spec, out_spec),
            scratch_shapes=scratch,
        ),
        compiler_params=pltpu.CompilerParams(vmem_limit_bytes=vmem_limit(scratch, [(2, tile, width)] * 2)),
        cost_estimate=pl.CostEstimate(
            flops=2 * supernodes * rows * slots * BLK * 4 * width, bytes_accessed=16 * 2**20, transcendentals=0
        ),
        name="values",
    )(tab, a, *stacks)


def make_gram(tab, a, stacks, entries, sub, shares):
    supernodes, early_count = stacks[0].shape[:2]
    rows, width = a.shape[1], stacks[0].shape[4]
    slots = tab.shape[2] + tab.shape[2] % CH
    places = min(slots, (rows // BLK) * (BLK // sub))
    places += places % 2
    out = jax.ShapeDtypeStruct((shares, supernodes, 2, 2 * width // shares, width), jnp.float32)
    out_spec = pl.BlockSpec((shares, 1) + out.shape[2:], lambda k, _: (0, k, 0, 0, 0))
    scratch = [
        pltpu.VMEM((supernodes, 2, 2, 2 * BLK, slots * BLK), jnp.bfloat16),
        pltpu.VMEM((supernodes, slots * BLK, 4 * width), jnp.bfloat16),
        pltpu.VMEM((supernodes, places * BLK, 4 * width), jnp.bfloat16),
        pltpu.VMEM((2 * BLK, 4 * width), jnp.float32),
        pltpu.VMEM((3 * 2 * BLK, 4 * width), jnp.bfloat16),
        pltpu.VMEM((2, 2 * width, 4 * width), jnp.float32),
        pltpu.SemaphoreType.DMA((supernodes, 2)),
        pltpu.SemaphoreType.DMA((supernodes,)),
        pltpu.SemaphoreType.DMA((supernodes,)),
    ]
    return pl.pallas_call(
        functools.partial(gram_kernel, entries, early_count, sub),
        out_shape=(out, out),
        grid_spec=pltpu.PrefetchScalarGridSpec(
            num_scalar_prefetch=1,
            grid=(supernodes,),
            in_specs=[pl.BlockSpec(memory_space=pl.ANY)] * 5,
            out_specs=(out_spec, out_spec),
            scratch_shapes=scratch,
        ),
        compiler_params=pltpu.CompilerParams(vmem_limit_bytes=vmem_limit(scratch, [out.shape] * 2)),
        cost_estimate=pl.CostEstimate(
            flops=supernodes * 2 * BLK * slots * 2 * BLK * 4 * width, bytes_accessed=8 * 2**20, transcendentals=0
        ),
        name="gram",
    )(tab, a, *stacks)


def scatter_sum(total, n_row, beside):
    half = n_row // 2
    row = lax.axis_index("row")
    level, odd = row // 2, row % 2
    pairs = total.reshape((half, 2) + total.shape[1:])
    came = []
    for d in range(1, half):
        route = [(i, (i + 2 * d) % n_row) for i in range(n_row)]
        sent = lax.dynamic_index_in_dim(pairs, (level + d) % half, 0, keepdims=False)
        came.append(lax.ppermute(sent, "row", route))
    *came, beside = lax.optimization_barrier((*came, beside))
    kept = lax.dynamic_index_in_dim(pairs, level, 0, keepdims=False)
    for x in came:
        kept = kept + x
    route = [(i, i ^ 1) for i in range(n_row)]
    sent = lax.dynamic_index_in_dim(kept, 1 - odd, 0, keepdims=False)
    last, beside = lax.optimization_barrier((lax.ppermute(sent, "row", route), beside))
    return lax.dynamic_index_in_dim(kept, odd, 0, keepdims=False) + last, beside


def local(n_row, inverse_pairs, factor_rows, diag_blocks, row_lists, block_order):
    supernodes = row_lists.shape[0]
    local_rows, local_cols = inverse_pairs.shape[1:]
    per_chip = factor_rows.shape[2]
    sub = min(BLK, per_chip)
    entries = per_chip // sub
    half = n_row // 2
    cycle = list(range(0, n_row, 2)) + list(range(n_row - 1, 0, -2))
    ahead = [(cycle[i], cycle[(i + 1) % n_row]) for i in range(n_row)]
    behind = [(b, a) for a, b in ahead]
    swap = [(0, 1), (1, 0)]

    tab = make_table(n_row, entries, sub, local_cols // BLK, local_rows // BLK, row_lists, block_order)

    chunks = [[factor_rows[k]] for k in range(supernodes)]
    up = [factor_rows[k] for k in range(supernodes)]
    down = list(up)
    for d in range(1, half):
        for k in range(supernodes):
            up[k] = lax.ppermute(up[k], "row", ahead)
            down[k] = lax.ppermute(down[k], "row", behind)
            chunks[k] += [up[k], down[k]]
        if d == 1:
            up[0], tab = lax.optimization_barrier((up[0], tab))
    for k in range(supernodes):
        last = [lax.ppermute(up[k][0:1], "row", ahead), lax.ppermute(down[k][1:2], "row", behind)]
        chunks[k].append(jnp.concatenate(last, axis=0))
    early = max(1, n_row - 3)
    own = [
        jnp.stack([jnp.stack(chunks[k][:early]) for k in range(supernodes)]),
        jnp.stack([jnp.stack(chunks[k][early:]) for k in range(supernodes)]),
    ]
    stacks = own + [lax.ppermute(x, "col", swap) for x in own]

    mine, theirs = make_gram(tab, inverse_pairs, stacks, entries, sub, n_row)
    total = mine + lax.ppermute(theirs, "col", swap)
    total, tab = lax.optimization_barrier((total, tab))
    mine, theirs = make_values(tab, inverse_pairs, stacks, entries, sub)
    share, theirs = scatter_sum(total, n_row, theirs)
    values = mine + lax.ppermute(theirs, "col", swap)
    shares = lax.all_to_all(jnp.broadcast_to(share[None], total.shape), "row", 0, 0, tiled=True)
    gram = jnp.moveaxis(shares, 0, 2).reshape(diag_blocks.shape)
    return (values, diag_blocks.astype(jnp.float32) - gram)


def solution(mesh):
    in_specs = (
        P("pole", "row", "col"),
        P("pole", None, "row", "col"),
        P("pole", None, None, "col"),
        P(),
        P(),
    )
    out_specs = (P("pole", None, "row", "col"), P("pole", None, None, "col"))
    body = functools.partial(local, mesh.shape["row"])
    return jax.shard_map(body, mesh=mesh, in_specs=in_specs, out_specs=out_specs, check_vma=False)
```

```python
import functools
import math

import jax
import jax.numpy as jnp
from jax import lax
from jax.experimental import pallas as pl
from jax.experimental.pallas import tpu as pltpu
from jax.sharding import PartitionSpec as P

BLK = 128
CH = 2
DEPTH = CH * BLK
COL_ENTRY, COL_BLOCK, ROW_ENTRY, ROW_BLOCK, OFFSET, COUNTS = range(6)


def block_at(index, size=BLK):
    return pl.ds(pl.multiple_of(index * size, size), size)


def table_kernel(n_row, entries, sub, col_blocks, row_blocks, lists_ref, order_ref, tab_ref, where_ref):
    half = n_row // 2
    row, core = lax.axis_index("row"), lax.axis_index("col")
    place = jnp.where(lax.rem(row, 2) == 0, lax.div(row, 2), n_row - 1 - lax.div(row, 2))

    def invert(g, carry):
        where_ref[order_ref[g]] = g
        return carry

    lax.fori_loop(0, order_ref.shape[0], invert, 0, unroll=8)
    for k in range(tab_ref.shape[0]):

        def one(i, counts, k=k):
            listed, placed = counts
            chunk, at = lax.div(i, entries), lax.rem(i, entries)
            step = lax.div(chunk + 1, 2)
            step = jnp.where((lax.rem(chunk, 2) == 1) | (chunk == n_row - 1), step, -step)
            source = lax.rem(place - step + 2 * n_row, n_row)
            source = jnp.where(source < half, 2 * source, 2 * (n_row - 1 - source) + 1)
            first = source * (entries * sub) + at * sub
            block = where_ref[lists_ref[k, lax.div(first, BLK)]]
            tab_ref[k, OFFSET, i] = lax.rem(first, BLK)
            col, line = block - core * col_blocks, block - row * row_blocks
            is_col = (col >= 0) & (col < col_blocks)
            is_row = (line >= 0) & (line < row_blocks)

            @pl.when(is_col)
            def _():
                tab_ref[k, COL_ENTRY, listed] = i
                tab_ref[k, COL_BLOCK, listed] = col

            @pl.when(is_row)
            def _():
                tab_ref[k, ROW_ENTRY, placed] = i
                tab_ref[k, ROW_BLOCK, placed] = line

            return listed + is_col.astype(jnp.int32), placed + is_row.astype(jnp.int32)

        listed, placed = lax.fori_loop(0, n_row * entries, one, (jnp.int32(0), jnp.int32(0)), unroll=4)
        tab_ref[k, COUNTS, 0] = listed
        tab_ref[k, COUNTS, 1] = placed
        tab_ref[k, COUNTS, 2] = core


def make_table(n_row, entries, sub, col_blocks, row_blocks, row_lists, block_order):
    smem = pl.BlockSpec(memory_space=pltpu.SMEM)
    return pl.pallas_call(
        functools.partial(table_kernel, n_row, entries, sub, col_blocks, row_blocks),
        out_shape=jax.ShapeDtypeStruct((row_lists.shape[0], 6, max(n_row * entries, 3)), jnp.int32),
        in_specs=[smem] * 2,
        out_specs=smem,
        scratch_shapes=[pltpu.SMEM(block_order.shape, jnp.int32)],
        name="table",
    )(row_lists, block_order)


def start_rows(tab_ref, kind, k, to_ref, sems, halves, entries, early_count, sub):
    def one(at, carry):
        entry = tab_ref[k, kind, at]
        chunk, part = lax.div(entry, entries), lax.rem(entry, entries)
        rows = block_at(at)
        if sub < BLK:
            to_ref[k, rows, :] = jnp.zeros((BLK, to_ref.shape[2]), to_ref.dtype)
            rows = pl.ds(pl.multiple_of(at * BLK + tab_ref[k, OFFSET, entry], sub), sub)

        def copy(stack, chunk, there, p):
            here = stack.at[k, chunk, p, block_at(part, sub), :]
            pltpu.make_async_copy(here, there, sems.at[k]).start()

        for half, stacks in enumerate(halves):
            width = stacks[0].shape[4]
            for p in range(2):
                there = to_ref.at[k, rows, pl.ds((2 * half + p) * width, width)]

                @pl.when(chunk < early_count)
                def _(stacks=stacks, there=there, p=p):
                    copy(stacks[0], chunk, there, p)

                @pl.when(chunk >= early_count)
                def _(stacks=stacks, there=there, p=p):
                    copy(stacks[1], chunk - early_count, there, p)

        return carry

    return one


def wait_rows(k, to_ref, sems, width, sub, halves):
    def one(at, carry):
        there = to_ref.at[k, pl.ds(0, sub), pl.ds(0, 2 * halves * width)]
        pltpu.make_async_copy(there, there, sems.at[k]).wait()
        return carry

    return one


def product(x, w, x_rows, depth):
    width = w.shape[1] // 2
    real, imag = (
        jnp.dot(x[p, x_rows, depth], w[depth, :], preferred_element_type=jnp.float32) for p in range(2)
    )
    return imag[:, width:] - real[:, :width], -(real[:, width:] + imag[:, :width])


def values_kernel(entries, early_count, sub, tile, tab_ref, a_ref, own0, own1, sib0, sib1, *refs):
    mine_ref, theirs_ref, x_ref, w_ref, x_sems, w_sems = refs
    k, step = pl.program_id(0), pl.program_id(1)
    supernodes, tiles = pl.num_programs(0), pl.num_programs(1)
    width = mine_ref.shape[3]
    listed = tab_ref[k, COUNTS, 0]
    now = k * tiles + step

    def start(at):
        which, rows, buffer = lax.div(at, tiles), lax.rem(at, tiles), lax.rem(at, 2)

        def one(slot, carry):
            pltpu.make_async_copy(
                a_ref.at[:, block_at(rows, tile), block_at(tab_ref[which, COL_BLOCK, slot])],
                x_ref.at[buffer, :, :, block_at(slot)],
                x_sems.at[buffer],
            ).start()
            return carry

        lax.fori_loop(0, tab_ref[which, COUNTS, 0], one, 0)

    @pl.when(now == 0)
    def _():
        for which in range(w_ref.shape[0]):
            rows = start_rows(
                tab_ref, COL_ENTRY, which, w_ref, w_sems, ((own0, own1), (sib0, sib1)), entries, early_count, sub
            )
            lax.fori_loop(0, tab_ref[which, COUNTS, 0], rows, 0)
            if which == 0:
                start(now)

    @pl.when(now + 1 < supernodes * tiles)
    def _():
        start(now + 1)

    @pl.when(step == 0)
    def _():
        @pl.when(lax.rem(listed, CH) != 0)
        def _():
            w_ref[k, block_at(listed), :] = jnp.zeros((BLK, w_ref.shape[2]), w_ref.dtype)

        lax.fori_loop(0, listed, wait_rows(k, w_ref, w_sems, width, sub, 2), 0)

    buffer = lax.rem(now, 2)

    @pl.when(lax.rem(listed, CH) != 0)
    def _():
        x_ref[buffer, :, :, block_at(listed)] = jnp.zeros((2, tile, BLK), x_ref.dtype)

    def arrived(slot, carry):
        there = x_ref.at[buffer, :, :, block_at(slot)]
        pltpu.make_async_copy(there, there, x_sems.at[buffer]).wait()
        return carry

    lax.fori_loop(0, listed, arrived, 0)
    steps = lax.div(listed + (CH - 1), CH)

    @pl.when(steps == 0)
    def _():
        mine_ref[...] = jnp.zeros_like(mine_ref)
        theirs_ref[...] = jnp.zeros_like(theirs_ref)

    for count in range(1, w_ref.shape[1] // DEPTH + 1):

        @pl.when(steps == count)
        def _(count=count):
            for half, out_ref in enumerate((mine_ref, theirs_ref)):
                columns = w_ref.at[k, :, pl.ds(2 * half * width, 2 * width)]
                parts = product(x_ref.at[buffer], columns, pl.ds(0, tile), pl.ds(0, count * DEPTH))
                for q in range(2):
                    out_ref[0, q] = parts[q]


def gram_kernel(entries, early_count, sub, tab_ref, a_ref, own0, own1, sib0, sib1, *refs):
    mine_ref, theirs_ref, x_ref, w_ref, l_ref, v_ref, r_ref, acc_ref, x_sems, w_sems, l_sems = refs
    k = pl.program_id(0)
    own, sib = (own0, own1), (sib0, sib1)
    width = mine_ref.shape[4]
    chunk_rows = mine_ref.shape[3]
    listed, placed = tab_ref[k, COUNTS, 0], tab_ref[k, COUNTS, 1]

    def start_pair(which, pair):
        def one_place(place, carry):
            rows = block_at(tab_ref[which, ROW_BLOCK, place])

            def one(slot, inner):
                pltpu.make_async_copy(
                    a_ref.at[:, rows, block_at(tab_ref[which, COL_BLOCK, slot])],
                    x_ref.at[which, lax.rem(pair, 2), :, block_at(place - 2 * pair), block_at(slot)],
                    x_sems.at[which, lax.rem(pair, 2)],
                ).start()
                return inner

            return lax.fori_loop(0, tab_ref[which, COUNTS, 0], one, carry)

        lax.fori_loop(2 * pair, jnp.minimum(2 * pair + 2, tab_ref[which, COUNTS, 1]), one_place, 0)

    @pl.when(k == 0)
    def _():
        for which in range(x_ref.shape[0]):
            stacks = ((own, sib), entries, early_count, sub)
            there = tab_ref[which, COUNTS, 1]
            lax.fori_loop(0, there, start_rows(tab_ref, ROW_ENTRY, which, l_ref, l_sems, *stacks), 0)

            @pl.when(there > 0)
            def _(which=which, stacks=stacks):
                lax.fori_loop(
                    0, tab_ref[which, COUNTS, 0], start_rows(tab_ref, COL_ENTRY, which, w_ref, w_sems, *stacks), 0
                )

            start_pair(which, 0)

    acc_ref[...] = jnp.zeros_like(acc_ref)
    odd = lax.rem(listed, CH) != 0
    steps = lax.div(listed + (CH - 1), CH)
    lax.fori_loop(0, placed, wait_rows(k, l_ref, l_sems, width, sub, 2), 0)

    @pl.when(placed > 0)
    def _():
        lax.fori_loop(0, listed, wait_rows(k, w_ref, w_sems, width, sub, 2), 0)

    def one_pair(pair, carry):
        start_pair(k, pair + 1)
        buffer = lax.rem(pair, 2)

        @pl.when(odd)
        def _():
            x_ref[k, buffer, :, :, block_at(listed)] = jnp.zeros((2, 2 * BLK, BLK), x_ref.dtype)

        def one_place(place, inner):
            def arrived(slot, innermost):
                there = x_ref.at[k, buffer, :, block_at(place - 2 * pair), block_at(slot)]
                pltpu.make_async_copy(there, there, x_sems.at[k, buffer]).wait()
                return innermost

            return lax.fori_loop(0, listed, arrived, inner)

        lax.fori_loop(2 * pair, jnp.minimum(2 * pair + 2, placed), one_place, 0)
        for count in range(1, w_ref.shape[1] // DEPTH + 1):

            @pl.when(steps == count)
            def _(count=count):
                for half in range(2):
                    columns = w_ref.at[k, :, pl.ds(2 * half * width, 2 * width)]
                    parts = product(x_ref.at[k, buffer], columns, pl.ds(0, 2 * BLK), pl.ds(0, count * DEPTH))
                    for q in range(2):
                        v_ref[:, pl.ds((2 * half + q) * width, width)] = parts[q]

        @pl.when(2 * pair + 1 >= placed)
        def _():
            v_ref[pl.ds(BLK, BLK), :] = jnp.zeros((BLK, v_ref.shape[1]), v_ref.dtype)
            l_ref[k, block_at(2 * pair + 1), :] = jnp.zeros((BLK, l_ref.shape[2]), l_ref.dtype)

        left = l_ref[k, block_at(pair, 2 * BLK), :]
        rest = v_ref[...]
        for piece in range(3):
            kept = rest.astype(jnp.bfloat16)
            r_ref[pl.ds(piece * 2 * BLK, 2 * BLK), :] = kept
            rest = rest - kept.astype(jnp.float32)
        for p in range(2):
            turned = jnp.concatenate(
                [left[:, (2 * h + p) * width : (2 * h + p + 1) * width].T for h in range(2)], axis=0
            )
            turned = jnp.concatenate([turned] * 3, axis=1)
            acc_ref[p] += jnp.dot(turned, r_ref[...], preferred_element_type=jnp.float32)
        return carry

    @pl.when((listed > 0) & (placed > 0))
    def _():
        @pl.when(odd)
        def _():
            w_ref[k, block_at(listed), :] = jnp.zeros((BLK, w_ref.shape[2]), w_ref.dtype)

        lax.fori_loop(0, lax.div(placed + 1, 2), one_pair, 0)

    core = tab_ref[0, COUNTS, 2]
    per_half = width // chunk_rows
    for half in range(2):
        first = (core if half == 0 else 1 - core) * per_half
        for i in range(per_half):
            rows = pl.ds(half * width + i * chunk_rows, chunk_rows)
            for out_ref, at in ((mine_ref, 0), (theirs_ref, 2 * width)):
                real, imag = pl.ds(at, width), pl.ds(width + at, width)
                out_ref[first + i, 0, 0] = acc_ref[0, rows, real] - acc_ref[1, rows, imag]
                out_ref[first + i, 0, 1] = acc_ref[0, rows, imag] + acc_ref[1, rows, real]


def vmem_limit(scratch, blocks):
    held = [x for x in scratch if x.dtype in (jnp.bfloat16, jnp.float32)]
    size = sum(math.prod(x.shape) * jnp.dtype(x.dtype).itemsize for x in held)
    return size + 2 * sum(math.prod(shape) * 4 for shape in blocks) + 5 * 2**20


def make_values(tab, a, stacks, entries, sub):
    supernodes, early_count = stacks[0].shape[:2]
    rows, width = a.shape[1], stacks[0].shape[4]
    slots = tab.shape[2] + tab.shape[2] % CH
    tile = max(t for t in range(BLK, min(rows, 512) + 1, BLK) if rows % t == 0)
    out_spec = pl.BlockSpec((1, 2, tile, width), lambda k, m, _: (k, 0, m, 0))
    out = jax.ShapeDtypeStruct((supernodes, 2, rows, width), jnp.float32)
    scratch = [
        pltpu.VMEM((2, 2, tile, slots * BLK), jnp.bfloat16),
        pltpu.VMEM((supernodes, slots * BLK, 4 * width), jnp.bfloat16),
        pltpu.SemaphoreType.DMA((2,)),
        pltpu.SemaphoreType.DMA((supernodes,)),
    ]
    return pl.pallas_call(
        functools.partial(values_kernel, entries, early_count, sub, tile),
        out_shape=(out, out),
        grid_spec=pltpu.PrefetchScalarGridSpec(
            num_scalar_prefetch=1,
            grid=(supernodes, rows // tile),
            in_specs=[pl.BlockSpec(memory_space=pl.ANY)] * 5,
            out_specs=(out_spec, out_spec),
            scratch_shapes=scratch,
        ),
        compiler_params=pltpu.CompilerParams(vmem_limit_bytes=vmem_limit(scratch, [(2, tile, width)] * 2)),
        cost_estimate=pl.CostEstimate(
            flops=2 * supernodes * rows * slots * BLK * 4 * width, bytes_accessed=16 * 2**20, transcendentals=0
        ),
        name="values",
    )(tab, a, *stacks)


def make_gram(tab, a, stacks, entries, sub, shares):
    supernodes, early_count = stacks[0].shape[:2]
    rows, width = a.shape[1], stacks[0].shape[4]
    slots = tab.shape[2] + tab.shape[2] % CH
    places = min(slots, (rows // BLK) * (BLK // sub))
    places += places % 2
    out = jax.ShapeDtypeStruct((shares, supernodes, 2, 2 * width // shares, width), jnp.float32)
    out_spec = pl.BlockSpec((shares, 1) + out.shape[2:], lambda k, _: (0, k, 0, 0, 0))
    scratch = [
        pltpu.VMEM((supernodes, 2, 2, 2 * BLK, slots * BLK), jnp.bfloat16),
        pltpu.VMEM((supernodes, slots * BLK, 4 * width), jnp.bfloat16),
        pltpu.VMEM((supernodes, places * BLK, 4 * width), jnp.bfloat16),
        pltpu.VMEM((2 * BLK, 4 * width), jnp.float32),
        pltpu.VMEM((3 * 2 * BLK, 4 * width), jnp.bfloat16),
        pltpu.VMEM((2, 2 * width, 4 * width), jnp.float32),
        pltpu.SemaphoreType.DMA((supernodes, 2)),
        pltpu.SemaphoreType.DMA((supernodes,)),
        pltpu.SemaphoreType.DMA((supernodes,)),
    ]
    return pl.pallas_call(
        functools.partial(gram_kernel, entries, early_count, sub),
        out_shape=(out, out),
        grid_spec=pltpu.PrefetchScalarGridSpec(
            num_scalar_prefetch=1,
            grid=(supernodes,),
            in_specs=[pl.BlockSpec(memory_space=pl.ANY)] * 5,
            out_specs=(out_spec, out_spec),
            scratch_shapes=scratch,
        ),
        compiler_params=pltpu.CompilerParams(vmem_limit_bytes=vmem_limit(scratch, [out.shape] * 2)),
        cost_estimate=pl.CostEstimate(
            flops=supernodes * 2 * BLK * slots * 2 * BLK * 4 * width, bytes_accessed=8 * 2**20, transcendentals=0
        ),
        name="gram",
    )(tab, a, *stacks)


def scatter_sum(total, n_row, beside):
    half = n_row // 2
    row = lax.axis_index("row")
    level, odd = row // 2, row % 2
    pairs = total.reshape((half, 2) + total.shape[1:])
    came = []
    for d in range(1, half):
        route = [(i, (i + 2 * d) % n_row) for i in range(n_row)]
        sent = lax.dynamic_index_in_dim(pairs, (level + d) % half, 0, keepdims=False)
        came.append(lax.ppermute(sent, "row", route))
    *came, beside = lax.optimization_barrier((*came, beside))
    kept = lax.dynamic_index_in_dim(pairs, level, 0, keepdims=False)
    for x in came:
        kept = kept + x
    route = [(i, i ^ 1) for i in range(n_row)]
    sent = lax.dynamic_index_in_dim(kept, 1 - odd, 0, keepdims=False)
    last, beside = lax.optimization_barrier((lax.ppermute(sent, "row", route), beside))
    return lax.dynamic_index_in_dim(kept, odd, 0, keepdims=False) + last, beside


def place_kernel(n_row, diag_ref, *refs):
    *own, other, out_ref = refs
    half = n_row // 2
    row = lax.axis_index("row")
    level, odd = lax.div(row, 2), lax.rem(row, 2)
    size = own[0].shape[2]
    out_ref[...] = diag_ref[...].astype(jnp.float32)
    for d in range(half):
        base = 2 * lax.rem(level - d + half, half)
        out_ref[:, :, block_at(base + odd, size), :] -= own[d][...]
        out_ref[:, :, block_at(base + 1 - odd, size), :] -= other[d]


def gather_shares(diag_blocks, share, n_row, beside):
    half = n_row // 2
    own = [share]
    for d in range(1, half):
        own.append(lax.ppermute(share, "row", [(i, (i + 2 * d) % n_row) for i in range(n_row)]))
    other = lax.ppermute(jnp.stack(own), "row", [(i, i ^ 1) for i in range(n_row)])
    other, beside = lax.optimization_barrier((other, beside))
    vmem = pl.BlockSpec(memory_space=pltpu.VMEM)
    schur = pl.pallas_call(
        functools.partial(place_kernel, n_row),
        out_shape=jax.ShapeDtypeStruct(diag_blocks.shape, jnp.float32),
        in_specs=[vmem] * (half + 2),
        out_specs=vmem,
        name="place",
    )(diag_blocks, *own, other)
    return schur, beside


def local(n_row, inverse_pairs, factor_rows, diag_blocks, row_lists, block_order):
    supernodes = row_lists.shape[0]
    local_rows, local_cols = inverse_pairs.shape[1:]
    per_chip = factor_rows.shape[2]
    sub = min(BLK, per_chip)
    entries = per_chip // sub
    half = n_row // 2
    cycle = list(range(0, n_row, 2)) + list(range(n_row - 1, 0, -2))
    ahead = [(cycle[i], cycle[(i + 1) % n_row]) for i in range(n_row)]
    behind = [(b, a) for a, b in ahead]
    swap = [(0, 1), (1, 0)]

    tab = make_table(n_row, entries, sub, local_cols // BLK, local_rows // BLK, row_lists, block_order)

    chunks = [[factor_rows[k]] for k in range(supernodes)]
    up = [factor_rows[k] for k in range(supernodes)]
    down = list(up)
    for d in range(1, half):
        for k in range(supernodes):
            up[k] = lax.ppermute(up[k], "row", ahead)
            down[k] = lax.ppermute(down[k], "row", behind)
            chunks[k] += [up[k], down[k]]
        if d == 1:
            up[0], tab = lax.optimization_barrier((up[0], tab))
    for k in range(supernodes):
        last = [lax.ppermute(up[k][0:1], "row", ahead), lax.ppermute(down[k][1:2], "row", behind)]
        chunks[k].append(jnp.concatenate(last, axis=0))
    early = max(1, n_row - 3)
    own = [
        jnp.stack([jnp.stack(chunks[k][:early]) for k in range(supernodes)]),
        jnp.stack([jnp.stack(chunks[k][early:]) for k in range(supernodes)]),
    ]
    stacks = own + [lax.ppermute(x, "col", swap) for x in own]

    mine, theirs = make_gram(tab, inverse_pairs, stacks, entries, sub, n_row)
    total = mine + lax.ppermute(theirs, "col", swap)
    total, tab = lax.optimization_barrier((total, tab))
    mine, theirs = make_values(tab, inverse_pairs, stacks, entries, sub)
    share, theirs = scatter_sum(total, n_row, theirs)
    values = mine + lax.ppermute(theirs, "col", swap)
    schur, values = gather_shares(diag_blocks, share, n_row, values)
    return (values, schur)


def solution(mesh):
    in_specs = (
        P("pole", "row", "col"),
        P("pole", None, "row", "col"),
        P("pole", None, None, "col"),
        P(),
        P(),
    )
    out_specs = (P("pole", None, "row", "col"), P("pole", None, None, "col"))
    body = functools.partial(local, mesh.shape["row"])
    return jax.shard_map(body, mesh=mesh, in_specs=in_specs, out_specs=out_specs, check_vma=False)
```

```python
import functools
import math

import jax
import jax.numpy as jnp
from jax import lax
from jax.experimental import pallas as pl
from jax.experimental.pallas import tpu as pltpu
from jax.sharding import PartitionSpec as P

BLK = 128
CH = 2
DEPTH = CH * BLK
COL_ENTRY, COL_BLOCK, ROW_ENTRY, ROW_BLOCK, OFFSET, COUNTS = range(6)


def block_at(index, size=BLK):
    return pl.ds(pl.multiple_of(index * size, size), size)


def table_kernel(n_row, entries, sub, col_blocks, row_blocks, lists_ref, order_ref, tab_ref, where_ref):
    half = n_row // 2
    row, core = lax.axis_index("row"), lax.axis_index("col")
    place = jnp.where(lax.rem(row, 2) == 0, lax.div(row, 2), n_row - 1 - lax.div(row, 2))

    def invert(g, carry):
        where_ref[order_ref[g]] = g
        return carry

    lax.fori_loop(0, order_ref.shape[0], invert, 0, unroll=8)
    for k in range(tab_ref.shape[0]):

        def one(i, counts, k=k):
            listed, placed = counts
            chunk, at = lax.div(i, entries), lax.rem(i, entries)
            step = lax.div(chunk + 1, 2)
            step = jnp.where((lax.rem(chunk, 2) == 1) | (chunk == n_row - 1), step, -step)
            source = lax.rem(place - step + 2 * n_row, n_row)
            source = jnp.where(source < half, 2 * source, 2 * (n_row - 1 - source) + 1)
            first = source * (entries * sub) + at * sub
            block = where_ref[lists_ref[k, lax.div(first, BLK)]]
            tab_ref[k, OFFSET, i] = lax.rem(first, BLK)
            col, line = block - core * col_blocks, block - row * row_blocks
            is_col = (col >= 0) & (col < col_blocks)
            is_row = (line >= 0) & (line < row_blocks)

            @pl.when(is_col)
            def _():
                tab_ref[k, COL_ENTRY, listed] = i
                tab_ref[k, COL_BLOCK, listed] = col

            @pl.when(is_row)
            def _():
                tab_ref[k, ROW_ENTRY, placed] = i
                tab_ref[k, ROW_BLOCK, placed] = line

            return listed + is_col.astype(jnp.int32), placed + is_row.astype(jnp.int32)

        listed, placed = lax.fori_loop(0, n_row * entries, one, (jnp.int32(0), jnp.int32(0)), unroll=4)
        tab_ref[k, COUNTS, 0] = listed
        tab_ref[k, COUNTS, 1] = placed
        tab_ref[k, COUNTS, 2] = core


def make_table(n_row, entries, sub, col_blocks, row_blocks, row_lists, block_order):
    smem = pl.BlockSpec(memory_space=pltpu.SMEM)
    return pl.pallas_call(
        functools.partial(table_kernel, n_row, entries, sub, col_blocks, row_blocks),
        out_shape=jax.ShapeDtypeStruct((row_lists.shape[0], 6, max(n_row * entries, 3)), jnp.int32),
        in_specs=[smem] * 2,
        out_specs=smem,
        scratch_shapes=[pltpu.SMEM(block_order.shape, jnp.int32)],
        name="table",
    )(row_lists, block_order)


def start_rows(tab_ref, kind, k, to_ref, sems, halves, entries, early_count, sub):
    def one(at, carry):
        entry = tab_ref[k, kind, at]
        chunk, part = lax.div(entry, entries), lax.rem(entry, entries)
        rows = block_at(at)
        if sub < BLK:
            to_ref[k, :, rows, :] = jnp.zeros((to_ref.shape[1], BLK, to_ref.shape[3]), to_ref.dtype)
            rows = pl.ds(pl.multiple_of(at * BLK + tab_ref[k, OFFSET, entry], sub), sub)

        def copy(which, chunk):
            for half, stacks in enumerate(halves):
                here = stacks[which].at[k, chunk, :, block_at(part, sub), :]
                there = to_ref.at[k, pl.ds(2 * half, 2), rows, :]
                pltpu.make_async_copy(here, there, sems.at[k]).start()

        @pl.when(chunk < early_count)
        def _():
            copy(0, chunk)

        @pl.when(chunk >= early_count)
        def _():
            copy(1, chunk - early_count)

        return carry

    return one


def wait_rows(k, to_ref, sems, sub):
    def one(at, carry):
        there = to_ref.at[k, :, pl.ds(0, sub), :]
        pltpu.make_async_copy(there, there, sems.at[k]).wait()
        return carry

    return one


def product(x, w, half, x_rows, depth):
    width = w.shape[2]
    columns = jnp.concatenate([w[2 * half, depth, :], w[2 * half + 1, depth, :]], axis=1)
    real, imag = (jnp.dot(x[p, x_rows, depth], columns, preferred_element_type=jnp.float32) for p in range(2))
    return imag[:, width:] - real[:, :width], -(real[:, width:] + imag[:, :width])


def values_kernel(entries, early_count, sub, tile, tab_ref, a_ref, own0, own1, sib0, sib1, *refs):
    mine_ref, theirs_ref, x_ref, w_ref, x_sems, w_sems = refs
    k, step = pl.program_id(0), pl.program_id(1)
    supernodes, tiles = pl.num_programs(0), pl.num_programs(1)
    width = mine_ref.shape[3]
    listed = tab_ref[k, COUNTS, 0]
    now = k * tiles + step

    def start(at):
        which, rows, buffer = lax.div(at, tiles), lax.rem(at, tiles), lax.rem(at, 2)

        def one(slot, carry):
            pltpu.make_async_copy(
                a_ref.at[:, block_at(rows, tile), block_at(tab_ref[which, COL_BLOCK, slot])],
                x_ref.at[buffer, :, :, block_at(slot)],
                x_sems.at[buffer],
            ).start()
            return carry

        lax.fori_loop(0, tab_ref[which, COUNTS, 0], one, 0)

    def start_weights(which):
        halves = ((own0, own1), (sib0, sib1))
        rows = start_rows(tab_ref, COL_ENTRY, which, w_ref, w_sems, halves, entries, early_count, sub)
        lax.fori_loop(0, tab_ref[which, COUNTS, 0], rows, 0)

    @pl.when(now == 0)
    def _():
        start_weights(0)
        start(now)

    @pl.when(now + 1 < supernodes * tiles)
    def _():
        start(now + 1)

    for which in range(1, w_ref.shape[0]):

        @pl.when(now == which * tiles - 1)
        def _(which=which):
            start_weights(which)

    @pl.when(step == 0)
    def _():
        @pl.when(lax.rem(listed, CH) != 0)
        def _():
            w_ref[k, :, block_at(listed), :] = jnp.zeros((w_ref.shape[1], BLK, w_ref.shape[3]), w_ref.dtype)

        lax.fori_loop(0, listed, wait_rows(k, w_ref, w_sems, sub), 0)

    buffer = lax.rem(now, 2)

    @pl.when(lax.rem(listed, CH) != 0)
    def _():
        x_ref[buffer, :, :, block_at(listed)] = jnp.zeros((2, tile, BLK), x_ref.dtype)

    def arrived(slot, carry):
        there = x_ref.at[buffer, :, :, block_at(slot)]
        pltpu.make_async_copy(there, there, x_sems.at[buffer]).wait()
        return carry

    lax.fori_loop(0, listed, arrived, 0)
    steps = lax.div(listed + (CH - 1), CH)

    @pl.when(steps == 0)
    def _():
        mine_ref[...] = jnp.zeros_like(mine_ref)
        theirs_ref[...] = jnp.zeros_like(theirs_ref)

    for count in range(1, w_ref.shape[2] // DEPTH + 1):

        @pl.when(steps == count)
        def _(count=count):
            for half, out_ref in enumerate((mine_ref, theirs_ref)):
                parts = product(x_ref.at[buffer], w_ref.at[k], half, pl.ds(0, tile), pl.ds(0, count * DEPTH))
                for q in range(2):
                    out_ref[0, q] = parts[q]


def gram_kernel(entries, early_count, sub, tab_ref, a_ref, own0, own1, sib0, sib1, *refs):
    mine_ref, theirs_ref, x_ref, w_ref, l_ref, v_ref, r_ref, acc_ref, x_sems, w_sems, l_sems = refs
    k = pl.program_id(0)
    own, sib = (own0, own1), (sib0, sib1)
    width = mine_ref.shape[4]
    chunk_rows = mine_ref.shape[3]
    listed, placed = tab_ref[k, COUNTS, 0], tab_ref[k, COUNTS, 1]

    def start_pair(which, pair):
        def one_place(place, carry):
            rows = block_at(tab_ref[which, ROW_BLOCK, place])

            def one(slot, inner):
                pltpu.make_async_copy(
                    a_ref.at[:, rows, block_at(tab_ref[which, COL_BLOCK, slot])],
                    x_ref.at[which, lax.rem(pair, 2), :, block_at(place - 2 * pair), block_at(slot)],
                    x_sems.at[which, lax.rem(pair, 2)],
                ).start()
                return inner

            return lax.fori_loop(0, tab_ref[which, COUNTS, 0], one, carry)

        lax.fori_loop(2 * pair, jnp.minimum(2 * pair + 2, tab_ref[which, COUNTS, 1]), one_place, 0)

    @pl.when(k == 0)
    def _():
        for which in range(x_ref.shape[0]):
            stacks = ((own, sib), entries, early_count, sub)
            there = tab_ref[which, COUNTS, 1]
            lax.fori_loop(0, there, start_rows(tab_ref, ROW_ENTRY, which, l_ref, l_sems, *stacks), 0)

            @pl.when(there > 0)
            def _(which=which, stacks=stacks):
                lax.fori_loop(
                    0, tab_ref[which, COUNTS, 0], start_rows(tab_ref, COL_ENTRY, which, w_ref, w_sems, *stacks), 0
                )

            start_pair(which, 0)

    acc_ref[...] = jnp.zeros_like(acc_ref)
    odd = lax.rem(listed, CH) != 0
    steps = lax.div(listed + (CH - 1), CH)
    lax.fori_loop(0, placed, wait_rows(k, l_ref, l_sems, sub), 0)

    @pl.when(placed > 0)
    def _():
        lax.fori_loop(0, listed, wait_rows(k, w_ref, w_sems, sub), 0)

    def one_pair(pair, carry):
        start_pair(k, pair + 1)
        buffer = lax.rem(pair, 2)

        @pl.when(odd)
        def _():
            x_ref[k, buffer, :, :, block_at(listed)] = jnp.zeros((2, 2 * BLK, BLK), x_ref.dtype)

        def one_place(place, inner):
            def arrived(slot, innermost):
                there = x_ref.at[k, buffer, :, block_at(place - 2 * pair), block_at(slot)]
                pltpu.make_async_copy(there, there, x_sems.at[k, buffer]).wait()
                return innermost

            return lax.fori_loop(0, listed, arrived, inner)

        lax.fori_loop(2 * pair, jnp.minimum(2 * pair + 2, placed), one_place, 0)
        for count in range(1, w_ref.shape[2] // DEPTH + 1):

            @pl.when(steps == count)
            def _(count=count):
                for half in range(2):
                    parts = product(x_ref.at[k, buffer], w_ref.at[k], half, pl.ds(0, 2 * BLK), pl.ds(0, count * DEPTH))
                    for q in range(2):
                        v_ref[:, pl.ds((2 * half + q) * width, width)] = parts[q]

        @pl.when(2 * pair + 1 >= placed)
        def _():
            v_ref[pl.ds(BLK, BLK), :] = jnp.zeros((BLK, v_ref.shape[1]), v_ref.dtype)
            l_ref[k, :, block_at(2 * pair + 1), :] = jnp.zeros((l_ref.shape[1], BLK, width), l_ref.dtype)

        rest = v_ref[...]
        for piece in range(3):
            kept = rest.astype(jnp.bfloat16)
            r_ref[pl.ds(piece * 2 * BLK, 2 * BLK), :] = kept
            rest = rest - kept.astype(jnp.float32)
        for p in range(2):
            turned = jnp.concatenate(
                [l_ref[k, 2 * h + p, block_at(pair, 2 * BLK), :].T for h in range(2)], axis=0
            )
            turned = jnp.concatenate([turned] * 3, axis=1)
            acc_ref[p] += jnp.dot(turned, r_ref[...], preferred_element_type=jnp.float32)
        return carry

    @pl.when((listed > 0) & (placed > 0))
    def _():
        @pl.when(odd)
        def _():
            w_ref[k, :, block_at(listed), :] = jnp.zeros((w_ref.shape[1], BLK, w_ref.shape[3]), w_ref.dtype)

        lax.fori_loop(0, lax.div(placed + 1, 2), one_pair, 0)

    core = tab_ref[0, COUNTS, 2]
    per_half = width // chunk_rows
    for half in range(2):
        first = (core if half == 0 else 1 - core) * per_half
        for i in range(per_half):
            rows = pl.ds(half * width + i * chunk_rows, chunk_rows)
            for out_ref, at in ((mine_ref, 0), (theirs_ref, 2 * width)):
                real, imag = pl.ds(at, width), pl.ds(width + at, width)
                out_ref[first + i, 0, 0] = acc_ref[0, rows, real] - acc_ref[1, rows, imag]
                out_ref[first + i, 0, 1] = acc_ref[0, rows, imag] + acc_ref[1, rows, real]


def vmem_limit(scratch, blocks):
    held = [x for x in scratch if x.dtype in (jnp.bfloat16, jnp.float32)]
    size = sum(math.prod(x.shape) * jnp.dtype(x.dtype).itemsize for x in held)
    return size + 2 * sum(math.prod(shape) * 4 for shape in blocks) + 2 * 2**20


def make_values(tab, a, stacks, entries, sub):
    supernodes, early_count = stacks[0].shape[:2]
    rows, width = a.shape[1], stacks[0].shape[4]
    slots = tab.shape[2] + tab.shape[2] % CH
    tile = max(t for t in range(BLK, min(rows, 512) + 1, BLK) if rows % t == 0)
    out_spec = pl.BlockSpec((1, 2, tile, width), lambda k, m, _: (k, 0, m, 0))
    out = jax.ShapeDtypeStruct((supernodes, 2, rows, width), jnp.float32)
    scratch = [
        pltpu.VMEM((2, 2, tile, slots * BLK), jnp.bfloat16),
        pltpu.VMEM((supernodes, 4, slots * BLK, width), jnp.bfloat16),
        pltpu.SemaphoreType.DMA((2,)),
        pltpu.SemaphoreType.DMA((supernodes,)),
    ]
    return pl.pallas_call(
        functools.partial(values_kernel, entries, early_count, sub, tile),
        out_shape=(out, out),
        grid_spec=pltpu.PrefetchScalarGridSpec(
            num_scalar_prefetch=1,
            grid=(supernodes, rows // tile),
            in_specs=[pl.BlockSpec(memory_space=pl.ANY)] * 5,
            out_specs=(out_spec, out_spec),
            scratch_shapes=scratch,
        ),
        compiler_params=pltpu.CompilerParams(vmem_limit_bytes=vmem_limit(scratch, [(2, tile, width)] * 2)),
        cost_estimate=pl.CostEstimate(
            flops=2 * supernodes * rows * slots * BLK * 4 * width, bytes_accessed=16 * 2**20, transcendentals=0
        ),
        name="values",
    )(tab, a, *stacks)


def make_gram(tab, a, stacks, entries, sub, shares):
    supernodes, early_count = stacks[0].shape[:2]
    rows, width = a.shape[1], stacks[0].shape[4]
    slots = tab.shape[2] + tab.shape[2] % CH
    places = min(slots, (rows // BLK) * (BLK // sub))
    places += places % 2
    out = jax.ShapeDtypeStruct((shares, supernodes, 2, 2 * width // shares, width), jnp.float32)
    out_spec = pl.BlockSpec((shares, 1) + out.shape[2:], lambda k, _: (0, k, 0, 0, 0))
    scratch = [
        pltpu.VMEM((supernodes, 2, 2, 2 * BLK, slots * BLK), jnp.bfloat16),
        pltpu.VMEM((supernodes, 4, slots * BLK, width), jnp.bfloat16),
        pltpu.VMEM((supernodes, 4, places * BLK, width), jnp.bfloat16),
        pltpu.VMEM((2 * BLK, 4 * width), jnp.float32),
        pltpu.VMEM((3 * 2 * BLK, 4 * width), jnp.bfloat16),
        pltpu.VMEM((2, 2 * width, 4 * width), jnp.float32),
        pltpu.SemaphoreType.DMA((supernodes, 2)),
        pltpu.SemaphoreType.DMA((supernodes,)),
        pltpu.SemaphoreType.DMA((supernodes,)),
    ]
    return pl.pallas_call(
        functools.partial(gram_kernel, entries, early_count, sub),
        out_shape=(out, out),
        grid_spec=pltpu.PrefetchScalarGridSpec(
            num_scalar_prefetch=1,
            grid=(supernodes,),
            in_specs=[pl.BlockSpec(memory_space=pl.ANY)] * 5,
            out_specs=(out_spec, out_spec),
            scratch_shapes=scratch,
        ),
        compiler_params=pltpu.CompilerParams(vmem_limit_bytes=vmem_limit(scratch, [out.shape] * 2)),
        cost_estimate=pl.CostEstimate(
            flops=supernodes * 2 * BLK * slots * 2 * BLK * 4 * width, bytes_accessed=8 * 2**20, transcendentals=0
        ),
        name="gram",
    )(tab, a, *stacks)


def scatter_sum(total, n_row, beside):
    half = n_row // 2
    row = lax.axis_index("row")
    level, odd = row // 2, row % 2
    pairs = total.reshape((half, 2) + total.shape[1:])
    came = []
    for d in range(1, half):
        route = [(i, (i + 2 * d) % n_row) for i in range(n_row)]
        sent = lax.dynamic_index_in_dim(pairs, (level + d) % half, 0, keepdims=False)
        came.append(lax.ppermute(sent, "row", route))
    *came, beside = lax.optimization_barrier((*came, beside))
    kept = lax.dynamic_index_in_dim(pairs, level, 0, keepdims=False)
    for x in came:
        kept = kept + x
    route = [(i, i ^ 1) for i in range(n_row)]
    sent = lax.dynamic_index_in_dim(kept, 1 - odd, 0, keepdims=False)
    last, beside = lax.optimization_barrier((lax.ppermute(sent, "row", route), beside))
    return lax.dynamic_index_in_dim(kept, odd, 0, keepdims=False) + last, beside


def place_kernel(n_row, diag_ref, *refs):
    *own, other, out_ref = refs
    half = n_row // 2
    row = lax.axis_index("row")
    level, odd = lax.div(row, 2), lax.rem(row, 2)
    size = own[0].shape[2]
    out_ref[...] = diag_ref[...].astype(jnp.float32)
    for d in range(half):
        base = 2 * lax.rem(level - d + half, half)
        out_ref[:, :, block_at(base + odd, size), :] -= own[d][...]
        out_ref[:, :, block_at(base + 1 - odd, size), :] -= other[d]


def gather_shares(diag_blocks, share, n_row, beside):
    half = n_row // 2
    own = [share]
    for d in range(1, half):
        own.append(lax.ppermute(share, "row", [(i, (i + 2 * d) % n_row) for i in range(n_row)]))
    other = lax.ppermute(jnp.stack(own), "row", [(i, i ^ 1) for i in range(n_row)])
    other, beside = lax.optimization_barrier((other, beside))
    vmem = pl.BlockSpec(memory_space=pltpu.VMEM)
    schur = pl.pallas_call(
        functools.partial(place_kernel, n_row),
        out_shape=jax.ShapeDtypeStruct(diag_blocks.shape, jnp.float32),
        in_specs=[vmem] * (half + 2),
        out_specs=vmem,
        name="place",
    )(diag_blocks, *own, other)
    return schur, beside


def local(n_row, inverse_pairs, factor_rows, diag_blocks, row_lists, block_order):
    supernodes = row_lists.shape[0]
    local_rows, local_cols = inverse_pairs.shape[1:]
    per_chip = factor_rows.shape[2]
    sub = min(BLK, per_chip)
    entries = per_chip // sub
    half = n_row // 2
    cycle = list(range(0, n_row, 2)) + list(range(n_row - 1, 0, -2))
    ahead = [(cycle[i], cycle[(i + 1) % n_row]) for i in range(n_row)]
    behind = [(b, a) for a, b in ahead]
    swap = [(0, 1), (1, 0)]

    tab = make_table(n_row, entries, sub, local_cols // BLK, local_rows // BLK, row_lists, block_order)

    chunks = [[factor_rows[k]] for k in range(supernodes)]
    up = [factor_rows[k] for k in range(supernodes)]
    down = list(up)
    for d in range(1, half):
        for k in range(supernodes):
            up[k] = lax.ppermute(up[k], "row", ahead)
            down[k] = lax.ppermute(down[k], "row", behind)
            chunks[k] += [up[k], down[k]]
        if d == 1:
            up[0], tab = lax.optimization_barrier((up[0], tab))
    for k in range(supernodes):
        last = [lax.ppermute(up[k][0:1], "row", ahead), lax.ppermute(down[k][1:2], "row", behind)]
        chunks[k].append(jnp.concatenate(last, axis=0))
    early = n_row - 1
    own = [
        jnp.stack([jnp.stack(chunks[k][:early]) for k in range(supernodes)]),
        jnp.stack([jnp.stack(chunks[k][early:]) for k in range(supernodes)]),
    ]
    stacks = own + [lax.ppermute(x, "col", swap) for x in own]

    mine, theirs = make_gram(tab, inverse_pairs, stacks, entries, sub, n_row)
    total = mine + lax.ppermute(theirs, "col", swap)
    total, tab = lax.optimization_barrier((total, tab))
    mine, theirs = make_values(tab, inverse_pairs, stacks, entries, sub)
    share, theirs = scatter_sum(total, n_row, theirs)
    values = mine + lax.ppermute(theirs, "col", swap)
    schur, values = gather_shares(diag_blocks, share, n_row, values)
    return (values, schur)


def solution(mesh):
    in_specs = (
        P("pole", "row", "col"),
        P("pole", None, "row", "col"),
        P("pole", None, None, "col"),
        P(),
        P(),
    )
    out_specs = (P("pole", None, "row", "col"), P("pole", None, None, "col"))
    body = functools.partial(local, mesh.shape["row"])
    return jax.shard_map(body, mesh=mesh, in_specs=in_specs, out_specs=out_specs, check_vma=False)
```

```python
import functools
import math

import jax
import jax.numpy as jnp
from jax import lax
from jax.experimental import pallas as pl
from jax.experimental.pallas import tpu as pltpu
from jax.sharding import PartitionSpec as P

BLK = 128
CH = 2
DEPTH = CH * BLK
COL_ENTRY, COL_BLOCK, ROW_ENTRY, ROW_BLOCK, OFFSET, COUNTS = range(6)


def block_at(index, size=BLK):
    return pl.ds(pl.multiple_of(index * size, size), size)


def table_kernel(n_row, entries, sub, col_blocks, row_blocks, lists_ref, order_ref, tab_ref, where_ref):
    half = n_row // 2
    row, core = lax.axis_index("row"), lax.axis_index("col")
    place = jnp.where(lax.rem(row, 2) == 0, lax.div(row, 2), n_row - 1 - lax.div(row, 2))

    def invert(g, carry):
        where_ref[order_ref[g]] = g
        return carry

    lax.fori_loop(0, order_ref.shape[0], invert, 0, unroll=8)
    for k in range(tab_ref.shape[0]):

        def one(i, counts, k=k):
            listed, placed = counts
            chunk, at = lax.div(i, entries), lax.rem(i, entries)
            step = lax.div(chunk + 1, 2)
            step = jnp.where((lax.rem(chunk, 2) == 1) | (chunk == n_row - 1), step, -step)
            source = lax.rem(place - step + 2 * n_row, n_row)
            source = jnp.where(source < half, 2 * source, 2 * (n_row - 1 - source) + 1)
            first = source * (entries * sub) + at * sub
            block = where_ref[lists_ref[k, lax.div(first, BLK)]]
            tab_ref[k, OFFSET, i] = lax.rem(first, BLK)
            col, line = block - core * col_blocks, block - row * row_blocks
            is_col = (col >= 0) & (col < col_blocks)
            is_row = (line >= 0) & (line < row_blocks)

            @pl.when(is_col)
            def _():
                tab_ref[k, COL_ENTRY, listed] = i
                tab_ref[k, COL_BLOCK, listed] = col

            @pl.when(is_row)
            def _():
                tab_ref[k, ROW_ENTRY, placed] = i
                tab_ref[k, ROW_BLOCK, placed] = line

            return listed + is_col.astype(jnp.int32), placed + is_row.astype(jnp.int32)

        listed, placed = lax.fori_loop(0, n_row * entries, one, (jnp.int32(0), jnp.int32(0)), unroll=4)
        tab_ref[k, COUNTS, 0] = listed
        tab_ref[k, COUNTS, 1] = placed
        tab_ref[k, COUNTS, 2] = core


def make_table(n_row, entries, sub, col_blocks, row_blocks, row_lists, block_order):
    smem = pl.BlockSpec(memory_space=pltpu.SMEM)
    return pl.pallas_call(
        functools.partial(table_kernel, n_row, entries, sub, col_blocks, row_blocks),
        out_shape=jax.ShapeDtypeStruct((row_lists.shape[0], 6, max(n_row * entries, 3)), jnp.int32),
        in_specs=[smem] * 2,
        out_specs=smem,
        scratch_shapes=[pltpu.SMEM(block_order.shape, jnp.int32)],
        name="table",
    )(row_lists, block_order)


def start_rows(tab_ref, kind, k, to_ref, sems, halves, entries, early_count, sub):
    def one(at, carry):
        entry = tab_ref[k, kind, at]
        chunk, part = lax.div(entry, entries), lax.rem(entry, entries)
        rows = block_at(at)
        if sub < BLK:
            to_ref[k, :, rows, :] = jnp.zeros((to_ref.shape[1], BLK, to_ref.shape[3]), to_ref.dtype)
            rows = pl.ds(pl.multiple_of(at * BLK + tab_ref[k, OFFSET, entry], sub), sub)

        def copy(which, chunk):
            for half, stacks in enumerate(halves):
                here = stacks[which].at[k, chunk, :, block_at(part, sub), :]
                there = to_ref.at[k, pl.ds(2 * half, 2), rows, :]
                pltpu.make_async_copy(here, there, sems.at[k]).start()

        @pl.when(chunk < early_count)
        def _():
            copy(0, chunk)

        @pl.when(chunk >= early_count)
        def _():
            copy(1, chunk - early_count)

        return carry

    return one


def wait_rows(k, to_ref, sems, sub):
    def one(at, carry):
        there = to_ref.at[k, :, pl.ds(0, sub), :]
        pltpu.make_async_copy(there, there, sems.at[k]).wait()
        return carry

    return one


def product(x, w, half, x_rows, depth):
    width = w.shape[2]
    columns = jnp.concatenate([w[2 * half, depth, :], w[2 * half + 1, depth, :]], axis=1)
    real, imag = (jnp.dot(x[p, x_rows, depth], columns, preferred_element_type=jnp.float32) for p in range(2))
    return imag[:, width:] - real[:, :width], -(real[:, width:] + imag[:, :width])


def values_kernel(entries, early_count, sub, tile, tab_ref, a_ref, own0, own1, sib0, sib1, *refs):
    mine_ref, theirs_ref, x_ref, w_ref, x_sems, w_sems = refs
    k, step = pl.program_id(0), pl.program_id(1)
    supernodes, tiles = pl.num_programs(0), pl.num_programs(1)
    width = mine_ref.shape[3]
    listed = tab_ref[k, COUNTS, 0]
    now = k * tiles + step

    def start(at):
        which, rows, buffer = lax.div(at, tiles), lax.rem(at, tiles), lax.rem(at, 2)

        def one(slot, carry):
            pltpu.make_async_copy(
                a_ref.at[:, block_at(rows, tile), block_at(tab_ref[which, COL_BLOCK, slot])],
                x_ref.at[buffer, :, :, block_at(slot)],
                x_sems.at[buffer],
            ).start()
            return carry

        lax.fori_loop(0, tab_ref[which, COUNTS, 0], one, 0)

    def start_weights(which):
        halves = ((own0, own1), (sib0, sib1))
        rows = start_rows(tab_ref, COL_ENTRY, which, w_ref, w_sems, halves, entries, early_count, sub)
        lax.fori_loop(0, tab_ref[which, COUNTS, 0], rows, 0)

    @pl.when(now == 0)
    def _():
        start_weights(0)
        start(now)

    @pl.when(now + 1 < supernodes * tiles)
    def _():
        start(now + 1)

    for which in range(1, w_ref.shape[0]):

        @pl.when(now == which * tiles - 1)
        def _(which=which):
            start_weights(which)

    @pl.when(step == 0)
    def _():
        @pl.when(lax.rem(listed, CH) != 0)
        def _():
            w_ref[k, :, block_at(listed), :] = jnp.zeros((w_ref.shape[1], BLK, w_ref.shape[3]), w_ref.dtype)

        lax.fori_loop(0, listed, wait_rows(k, w_ref, w_sems, sub), 0)

    buffer = lax.rem(now, 2)

    @pl.when(lax.rem(listed, CH) != 0)
    def _():
        x_ref[buffer, :, :, block_at(listed)] = jnp.zeros((2, tile, BLK), x_ref.dtype)

    def arrived(slot, carry):
        there = x_ref.at[buffer, :, :, block_at(slot)]
        pltpu.make_async_copy(there, there, x_sems.at[buffer]).wait()
        return carry

    lax.fori_loop(0, listed, arrived, 0)
    steps = lax.div(listed + (CH - 1), CH)

    @pl.when(steps == 0)
    def _():
        mine_ref[...] = jnp.zeros_like(mine_ref)
        theirs_ref[...] = jnp.zeros_like(theirs_ref)

    for count in range(1, w_ref.shape[2] // DEPTH + 1):

        @pl.when(steps == count)
        def _(count=count):
            for half, out_ref in enumerate((mine_ref, theirs_ref)):
                parts = product(x_ref.at[buffer], w_ref.at[k], half, pl.ds(0, tile), pl.ds(0, count * DEPTH))
                for q in range(2):
                    out_ref[0, q] = parts[q]


def gram_kernel(entries, early_count, sub, tab_ref, a_ref, own0, own1, sib0, sib1, *refs):
    mine_ref, theirs_ref, x_ref, w_ref, l_ref, v_ref, r_ref, acc_ref, x_sems, w_sems, l_sems = refs
    k = pl.program_id(0)
    own, sib = (own0, own1), (sib0, sib1)
    width = mine_ref.shape[4]
    chunk_rows = mine_ref.shape[3]
    listed, placed = tab_ref[k, COUNTS, 0], tab_ref[k, COUNTS, 1]

    def start_pair(which, pair):
        def one_place(place, carry):
            rows = block_at(tab_ref[which, ROW_BLOCK, place])

            def one(slot, inner):
                pltpu.make_async_copy(
                    a_ref.at[:, rows, block_at(tab_ref[which, COL_BLOCK, slot])],
                    x_ref.at[which, lax.rem(pair, 2), :, block_at(place - 2 * pair), block_at(slot)],
                    x_sems.at[which, lax.rem(pair, 2)],
                ).start()
                return inner

            return lax.fori_loop(0, tab_ref[which, COUNTS, 0], one, carry)

        lax.fori_loop(2 * pair, jnp.minimum(2 * pair + 2, tab_ref[which, COUNTS, 1]), one_place, 0)

    @pl.when(k == 0)
    def _():
        for which in range(x_ref.shape[0]):
            stacks = ((own, sib), entries, early_count, sub)
            there = tab_ref[which, COUNTS, 1]
            lax.fori_loop(0, there, start_rows(tab_ref, ROW_ENTRY, which, l_ref, l_sems, *stacks), 0)

            @pl.when(there > 0)
            def _(which=which, stacks=stacks):
                lax.fori_loop(
                    0, tab_ref[which, COUNTS, 0], start_rows(tab_ref, COL_ENTRY, which, w_ref, w_sems, *stacks), 0
                )

            start_pair(which, 0)

    acc_ref[...] = jnp.zeros_like(acc_ref)
    odd = lax.rem(listed, CH) != 0
    steps = lax.div(listed + (CH - 1), CH)
    lax.fori_loop(0, placed, wait_rows(k, l_ref, l_sems, sub), 0)

    @pl.when(placed > 0)
    def _():
        lax.fori_loop(0, listed, wait_rows(k, w_ref, w_sems, sub), 0)

    def one_pair(pair, carry):
        start_pair(k, pair + 1)
        buffer = lax.rem(pair, 2)

        @pl.when(odd)
        def _():
            x_ref[k, buffer, :, :, block_at(listed)] = jnp.zeros((2, 2 * BLK, BLK), x_ref.dtype)

        def one_place(place, inner):
            def arrived(slot, innermost):
                there = x_ref.at[k, buffer, :, block_at(place - 2 * pair), block_at(slot)]
                pltpu.make_async_copy(there, there, x_sems.at[k, buffer]).wait()
                return innermost

            return lax.fori_loop(0, listed, arrived, inner)

        lax.fori_loop(2 * pair, jnp.minimum(2 * pair + 2, placed), one_place, 0)
        for count in range(1, w_ref.shape[2] // DEPTH + 1):

            @pl.when(steps == count)
            def _(count=count):
                for half in range(2):
                    parts = product(x_ref.at[k, buffer], w_ref.at[k], half, pl.ds(0, 2 * BLK), pl.ds(0, count * DEPTH))
                    for q in range(2):
                        v_ref[:, pl.ds((2 * half + q) * width, width)] = parts[q]

        @pl.when(2 * pair + 1 >= placed)
        def _():
            v_ref[pl.ds(BLK, BLK), :] = jnp.zeros((BLK, v_ref.shape[1]), v_ref.dtype)
            l_ref[k, :, block_at(2 * pair + 1), :] = jnp.zeros((l_ref.shape[1], BLK, width), l_ref.dtype)

        rest = v_ref[...]
        for piece in range(3):
            kept = rest.astype(jnp.bfloat16)
            r_ref[pl.ds(piece * 2 * BLK, 2 * BLK), :] = kept
            rest = rest - kept.astype(jnp.float32)
        for p in range(2):
            turned = jnp.concatenate(
                [l_ref[k, 2 * h + p, block_at(pair, 2 * BLK), :].T for h in range(2)], axis=0
            )
            turned = jnp.concatenate([turned] * 3, axis=1)
            acc_ref[p] += jnp.dot(turned, r_ref[...], preferred_element_type=jnp.float32)
        return carry

    @pl.when((listed > 0) & (placed > 0))
    def _():
        @pl.when(odd)
        def _():
            w_ref[k, :, block_at(listed), :] = jnp.zeros((w_ref.shape[1], BLK, w_ref.shape[3]), w_ref.dtype)

        lax.fori_loop(0, lax.div(placed + 1, 2), one_pair, 0)

    core = tab_ref[0, COUNTS, 2]
    per_half = width // chunk_rows
    for half in range(2):
        first = (core if half == 0 else 1 - core) * per_half
        for i in range(per_half):
            rows = pl.ds(half * width + i * chunk_rows, chunk_rows)
            for out_ref, at in ((mine_ref, 0), (theirs_ref, 2 * width)):
                real, imag = pl.ds(at, width), pl.ds(width + at, width)
                out_ref[first + i, 0, 0] = acc_ref[0, rows, real] - acc_ref[1, rows, imag]
                out_ref[first + i, 0, 1] = acc_ref[0, rows, imag] + acc_ref[1, rows, real]


def vmem_limit(scratch, blocks):
    held = [x for x in scratch if x.dtype in (jnp.bfloat16, jnp.float32)]
    size = sum(math.prod(x.shape) * jnp.dtype(x.dtype).itemsize for x in held)
    return size + 2 * sum(math.prod(shape) * 4 for shape in blocks) + 2 * 2**20


def make_values(tab, a, stacks, entries, sub):
    supernodes, early_count = stacks[0].shape[:2]
    rows, width = a.shape[1], stacks[0].shape[4]
    slots = tab.shape[2] + tab.shape[2] % CH
    tile = max(t for t in range(BLK, min(rows, 512) + 1, BLK) if rows % t == 0)
    out_spec = pl.BlockSpec((1, 2, tile, width), lambda k, m, _: (k, 0, m, 0))
    out = pltpu.HBM((supernodes, 2, rows, width), jnp.float32)
    scratch = [
        pltpu.VMEM((2, 2, tile, slots * BLK), jnp.bfloat16),
        pltpu.VMEM((supernodes, 4, slots * BLK, width), jnp.bfloat16),
        pltpu.SemaphoreType.DMA((2,)),
        pltpu.SemaphoreType.DMA((supernodes,)),
    ]
    return pl.pallas_call(
        functools.partial(values_kernel, entries, early_count, sub, tile),
        out_shape=(out, out),
        grid_spec=pltpu.PrefetchScalarGridSpec(
            num_scalar_prefetch=1,
            grid=(supernodes, rows // tile),
            in_specs=[pl.BlockSpec(memory_space=pl.ANY)] * 5,
            out_specs=(out_spec, out_spec),
            scratch_shapes=scratch,
        ),
        compiler_params=pltpu.CompilerParams(vmem_limit_bytes=vmem_limit(scratch, [(2, tile, width)] * 2)),
        cost_estimate=pl.CostEstimate(
            flops=2 * supernodes * rows * slots * BLK * 4 * width, bytes_accessed=16 * 2**20, transcendentals=0
        ),
        name="values",
    )(tab, a, *stacks)


def make_gram(tab, a, stacks, entries, sub, shares):
    supernodes, early_count = stacks[0].shape[:2]
    rows, width = a.shape[1], stacks[0].shape[4]
    slots = tab.shape[2] + tab.shape[2] % CH
    places = min(slots, (rows // BLK) * (BLK // sub))
    places += places % 2
    out = jax.ShapeDtypeStruct((shares, supernodes, 2, 2 * width // shares, width), jnp.float32)
    out_spec = pl.BlockSpec((shares, 1) + out.shape[2:], lambda k, _: (0, k, 0, 0, 0))
    scratch = [
        pltpu.VMEM((supernodes, 2, 2, 2 * BLK, slots * BLK), jnp.bfloat16),
        pltpu.VMEM((supernodes, 4, slots * BLK, width), jnp.bfloat16),
        pltpu.VMEM((supernodes, 4, places * BLK, width), jnp.bfloat16),
        pltpu.VMEM((2 * BLK, 4 * width), jnp.float32),
        pltpu.VMEM((3 * 2 * BLK, 4 * width), jnp.bfloat16),
        pltpu.VMEM((2, 2 * width, 4 * width), jnp.float32),
        pltpu.SemaphoreType.DMA((supernodes, 2)),
        pltpu.SemaphoreType.DMA((supernodes,)),
        pltpu.SemaphoreType.DMA((supernodes,)),
    ]
    return pl.pallas_call(
        functools.partial(gram_kernel, entries, early_count, sub),
        out_shape=(out, out),
        grid_spec=pltpu.PrefetchScalarGridSpec(
            num_scalar_prefetch=1,
            grid=(supernodes,),
            in_specs=[pl.BlockSpec(memory_space=pl.ANY)] * 5,
            out_specs=(out_spec, out_spec),
            scratch_shapes=scratch,
        ),
        compiler_params=pltpu.CompilerParams(vmem_limit_bytes=vmem_limit(scratch, [out.shape] * 2)),
        cost_estimate=pl.CostEstimate(
            flops=supernodes * 2 * BLK * slots * 2 * BLK * 4 * width, bytes_accessed=8 * 2**20, transcendentals=0
        ),
        name="gram",
    )(tab, a, *stacks)


def scatter_sum(total, n_row, beside):
    half = n_row // 2
    row = lax.axis_index("row")
    level, odd = row // 2, row % 2
    pairs = total.reshape((half, 2) + total.shape[1:])
    came = []
    for d in range(1, half):
        route = [(i, (i + 2 * d) % n_row) for i in range(n_row)]
        sent = lax.dynamic_index_in_dim(pairs, (level + d) % half, 0, keepdims=False)
        came.append(lax.ppermute(sent, "row", route))
    *came, beside = lax.optimization_barrier((*came, beside))
    kept = lax.dynamic_index_in_dim(pairs, level, 0, keepdims=False)
    for x in came:
        kept = kept + x
    route = [(i, i ^ 1) for i in range(n_row)]
    sent = lax.dynamic_index_in_dim(kept, 1 - odd, 0, keepdims=False)
    last, beside = lax.optimization_barrier((lax.ppermute(sent, "row", route), beside))
    return lax.dynamic_index_in_dim(kept, odd, 0, keepdims=False) + last, beside


def place_kernel(n_row, diag_ref, *refs):
    half = n_row // 2
    parts, (out_ref, held_ref, sems) = refs[: half + 1], refs[half + 1 :]
    row = lax.axis_index("row")
    level, odd = lax.div(row, 2), lax.rem(row, 2)
    size = held_ref.shape[3]
    copies = [pltpu.make_async_copy(part, held_ref.at[d], sems.at[d]) for d, part in enumerate(parts[:half])]
    copies.append(pltpu.make_async_copy(parts[half], held_ref.at[pl.ds(half, half)], sems.at[half]))
    for copy in copies:
        copy.start()
    out_ref[...] = diag_ref[...].astype(jnp.float32)
    for copy in copies:
        copy.wait()
    for d in range(half):
        base = 2 * lax.rem(level - d + half, half)
        out_ref[:, :, block_at(base + odd, size), :] -= held_ref[d]
        out_ref[:, :, block_at(base + 1 - odd, size), :] -= held_ref[half + d]


def gather_shares(diag_blocks, share, n_row, beside):
    half = n_row // 2
    own = [share]
    for d in range(1, half):
        own.append(lax.ppermute(share, "row", [(i, (i + 2 * d) % n_row) for i in range(n_row)]))
    other = lax.ppermute(jnp.stack(own), "row", [(i, i ^ 1) for i in range(n_row)])
    other, beside = lax.optimization_barrier((other, beside))
    vmem = pl.BlockSpec(memory_space=pltpu.VMEM)
    schur = pl.pallas_call(
        functools.partial(place_kernel, n_row),
        out_shape=jax.ShapeDtypeStruct(diag_blocks.shape, jnp.float32),
        in_specs=[vmem] + [pl.BlockSpec(memory_space=pl.ANY)] * (half + 1),
        out_specs=vmem,
        scratch_shapes=[
            pltpu.VMEM((n_row,) + share.shape, jnp.float32),
            pltpu.SemaphoreType.DMA((half + 1,)),
        ],
        name="place",
    )(diag_blocks, *own, other)
    return schur, beside


def local(n_row, inverse_pairs, factor_rows, diag_blocks, row_lists, block_order):
    supernodes = row_lists.shape[0]
    local_rows, local_cols = inverse_pairs.shape[1:]
    per_chip = factor_rows.shape[2]
    sub = min(BLK, per_chip)
    entries = per_chip // sub
    half = n_row // 2
    cycle = list(range(0, n_row, 2)) + list(range(n_row - 1, 0, -2))
    ahead = [(cycle[i], cycle[(i + 1) % n_row]) for i in range(n_row)]
    behind = [(b, a) for a, b in ahead]
    swap = [(0, 1), (1, 0)]

    tab = make_table(n_row, entries, sub, local_cols // BLK, local_rows // BLK, row_lists, block_order)

    chunks = [[factor_rows[k]] for k in range(supernodes)]
    up = [factor_rows[k] for k in range(supernodes)]
    down = list(up)
    for d in range(1, half):
        for k in range(supernodes):
            up[k] = lax.ppermute(up[k], "row", ahead)
            down[k] = lax.ppermute(down[k], "row", behind)
            chunks[k] += [up[k], down[k]]
        if d == 1:
            up[0], tab = lax.optimization_barrier((up[0], tab))
    for k in range(supernodes):
        last = [lax.ppermute(up[k][0:1], "row", ahead), lax.ppermute(down[k][1:2], "row", behind)]
        chunks[k].append(jnp.concatenate(last, axis=0))
    early = max(1, n_row - 3)
    own = [
        jnp.stack([jnp.stack(chunks[k][:early]) for k in range(supernodes)]),
        jnp.stack([jnp.stack(chunks[k][early:]) for k in range(supernodes)]),
    ]
    stacks = own + [lax.ppermute(x, "col", swap) for x in own]

    mine, theirs = make_gram(tab, inverse_pairs, stacks, entries, sub, n_row)
    total = mine + lax.ppermute(theirs, "col", swap)
    total, tab = lax.optimization_barrier((total, tab))
    mine, theirs = make_values(tab, inverse_pairs, stacks, entries, sub)
    share, theirs = scatter_sum(total, n_row, theirs)
    values = mine + lax.ppermute(theirs, "col", swap)
    schur, values = gather_shares(diag_blocks, share, n_row, values)
    return (values, schur)


def solution(mesh):
    in_specs = (
        P("pole", "row", "col"),
        P("pole", None, "row", "col"),
        P("pole", None, None, "col"),
        P(),
        P(),
    )
    out_specs = (P("pole", None, "row", "col"), P("pole", None, None, "col"))
    body = functools.partial(local, mesh.shape["row"])
    return jax.shard_map(body, mesh=mesh, in_specs=in_specs, out_specs=out_specs, check_vma=False)
```

```python
import functools
import math

import jax
import jax.numpy as jnp
from jax import lax
from jax.experimental import pallas as pl
from jax.experimental.pallas import tpu as pltpu
from jax.sharding import PartitionSpec as P

BLK = 128
CH = 2
DEPTH = CH * BLK
COL_ENTRY, COL_BLOCK, ROW_ENTRY, ROW_BLOCK, OFFSET, COUNTS = range(6)


def block_at(index, size=BLK):
    return pl.ds(pl.multiple_of(index * size, size), size)


def table_kernel(n_row, entries, sub, col_blocks, row_blocks, lists_ref, order_ref, tab_ref, where_ref):
    half = n_row // 2
    row, core = lax.axis_index("row"), lax.axis_index("col")
    place = jnp.where(lax.rem(row, 2) == 0, lax.div(row, 2), n_row - 1 - lax.div(row, 2))

    def invert(g, carry):
        where_ref[order_ref[g]] = g
        return carry

    lax.fori_loop(0, order_ref.shape[0], invert, 0, unroll=8)
    for k in range(tab_ref.shape[0]):

        def one(i, counts, k=k):
            listed, placed = counts
            chunk, at = lax.div(i, entries), lax.rem(i, entries)
            step = lax.div(chunk + 1, 2)
            step = jnp.where((lax.rem(chunk, 2) == 1) | (chunk == n_row - 1), step, -step)
            source = lax.rem(place - step + 2 * n_row, n_row)
            source = jnp.where(source < half, 2 * source, 2 * (n_row - 1 - source) + 1)
            first = source * (entries * sub) + at * sub
            block = where_ref[lists_ref[k, lax.div(first, BLK)]]
            tab_ref[k, OFFSET, i] = lax.rem(first, BLK)
            col, line = block - core * col_blocks, block - row * row_blocks
            is_col = (col >= 0) & (col < col_blocks)
            is_row = (line >= 0) & (line < row_blocks)

            @pl.when(is_col)
            def _():
                tab_ref[k, COL_ENTRY, listed] = i
                tab_ref[k, COL_BLOCK, listed] = col

            @pl.when(is_row)
            def _():
                tab_ref[k, ROW_ENTRY, placed] = i
                tab_ref[k, ROW_BLOCK, placed] = line

            return listed + is_col.astype(jnp.int32), placed + is_row.astype(jnp.int32)

        listed, placed = lax.fori_loop(0, n_row * entries, one, (jnp.int32(0), jnp.int32(0)), unroll=4)
        tab_ref[k, COUNTS, 0] = listed
        tab_ref[k, COUNTS, 1] = placed
        tab_ref[k, COUNTS, 2] = core


def make_table(n_row, entries, sub, col_blocks, row_blocks, row_lists, block_order):
    smem = pl.BlockSpec(memory_space=pltpu.SMEM)
    return pl.pallas_call(
        functools.partial(table_kernel, n_row, entries, sub, col_blocks, row_blocks),
        out_shape=jax.ShapeDtypeStruct((row_lists.shape[0], 6, max(n_row * entries, 3)), jnp.int32),
        in_specs=[smem] * 2,
        out_specs=smem,
        scratch_shapes=[pltpu.SMEM(block_order.shape, jnp.int32)],
        name="table",
    )(row_lists, block_order)


def start_rows(tab_ref, kind, k, to_ref, sems, halves, entries, early_count, sub, to=None):
    to = k if to is None else to

    def one(at, carry):
        entry = tab_ref[k, kind, at]
        chunk, part = lax.div(entry, entries), lax.rem(entry, entries)
        rows = block_at(at)
        if sub < BLK:
            to_ref[to, rows, :] = jnp.zeros((BLK, to_ref.shape[2]), to_ref.dtype)
            rows = pl.ds(pl.multiple_of(at * BLK + tab_ref[k, OFFSET, entry], sub), sub)

        def copy(stack, chunk, there, p):
            here = stack.at[k, chunk, p, block_at(part, sub), :]
            pltpu.make_async_copy(here, there, sems.at[to]).start()

        for half, stacks in enumerate(halves):
            width = stacks[0].shape[4]
            for p in range(2):
                there = to_ref.at[to, rows, pl.ds((2 * half + p) * width, width)]

                @pl.when(chunk < early_count)
                def _(stacks=stacks, there=there, p=p):
                    copy(stacks[0], chunk, there, p)

                @pl.when(chunk >= early_count)
                def _(stacks=stacks, there=there, p=p):
                    copy(stacks[1], chunk - early_count, there, p)

        return carry

    return one


def wait_rows(k, to_ref, sems, width, sub, halves):
    def one(at, carry):
        there = to_ref.at[k, pl.ds(0, sub), pl.ds(0, 2 * halves * width)]
        pltpu.make_async_copy(there, there, sems.at[k]).wait()
        return carry

    return one


def product(x, w, x_rows, depth):
    width = w.shape[1] // 2
    real, imag = (
        jnp.dot(x[p, x_rows, depth], w[depth, :], preferred_element_type=jnp.float32) for p in range(2)
    )
    return imag[:, width:] - real[:, :width], -(real[:, width:] + imag[:, :width])


def values_kernel(k, entries, early_count, sub, tile, tab_ref, a_ref, own0, own1, sib0, sib1, *refs):
    mine_ref, theirs_ref, x_ref, w_ref, x_sems, w_sems = refs[-6:]
    step, tiles = pl.program_id(0), pl.num_programs(0)
    width = mine_ref.shape[3]
    listed = tab_ref[k, COUNTS, 0]

    def start(at):
        def one(slot, carry):
            pltpu.make_async_copy(
                a_ref.at[:, block_at(at, tile), block_at(tab_ref[k, COL_BLOCK, slot])],
                x_ref.at[lax.rem(at, 2), :, :, block_at(slot)],
                x_sems.at[lax.rem(at, 2)],
            ).start()
            return carry

        lax.fori_loop(0, listed, one, 0)

    @pl.when(step == 0)
    def _():
        halves = ((own0, own1), (sib0, sib1))
        rows = start_rows(tab_ref, COL_ENTRY, k, w_ref, w_sems, halves, entries, early_count, sub, 0)
        lax.fori_loop(0, listed, rows, 0)
        start(step)

    @pl.when(step + 1 < tiles)
    def _():
        start(step + 1)

    buffer = lax.rem(step, 2)

    @pl.when(step == 0)
    def _():
        @pl.when(lax.rem(listed, CH) != 0)
        def _():
            w_ref[0, block_at(listed), :] = jnp.zeros((BLK, w_ref.shape[2]), w_ref.dtype)

        lax.fori_loop(0, listed, wait_rows(0, w_ref, w_sems, width, sub, 2), 0)

    @pl.when(lax.rem(listed, CH) != 0)
    def _():
        x_ref[buffer, :, :, block_at(listed)] = jnp.zeros((2, tile, BLK), x_ref.dtype)

    def arrived(slot, carry):
        there = x_ref.at[buffer, :, :, block_at(slot)]
        pltpu.make_async_copy(there, there, x_sems.at[buffer]).wait()
        return carry

    lax.fori_loop(0, listed, arrived, 0)
    steps = lax.div(listed + (CH - 1), CH)

    @pl.when(steps == 0)
    def _():
        mine_ref[...] = jnp.zeros_like(mine_ref)
        theirs_ref[...] = jnp.zeros_like(theirs_ref)

    for count in range(1, w_ref.shape[1] // DEPTH + 1):

        @pl.when(steps == count)
        def _(count=count):
            for half, out_ref in enumerate((mine_ref, theirs_ref)):
                columns = w_ref.at[0, :, pl.ds(2 * half * width, 2 * width)]
                parts = product(x_ref.at[buffer], columns, pl.ds(0, tile), pl.ds(0, count * DEPTH))
                for q in range(2):
                    out_ref[0, q] = parts[q]


def gram_kernel(entries, early_count, sub, tab_ref, a_ref, own0, own1, sib0, sib1, *refs):
    mine_ref, theirs_ref, x_ref, w_ref, l_ref, v_ref, r_ref, acc_ref, x_sems, w_sems, l_sems = refs
    k = pl.program_id(0)
    own, sib = (own0, own1), (sib0, sib1)
    width = mine_ref.shape[4]
    chunk_rows = mine_ref.shape[3]
    listed, placed = tab_ref[k, COUNTS, 0], tab_ref[k, COUNTS, 1]

    def start_pair(which, pair):
        def one_place(place, carry):
            rows = block_at(tab_ref[which, ROW_BLOCK, place])

            def one(slot, inner):
                pltpu.make_async_copy(
                    a_ref.at[:, rows, block_at(tab_ref[which, COL_BLOCK, slot])],
                    x_ref.at[which, lax.rem(pair, 2), :, block_at(place - 2 * pair), block_at(slot)],
                    x_sems.at[which, lax.rem(pair, 2)],
                ).start()
                return inner

            return lax.fori_loop(0, tab_ref[which, COUNTS, 0], one, carry)

        lax.fori_loop(2 * pair, jnp.minimum(2 * pair + 2, tab_ref[which, COUNTS, 1]), one_place, 0)

    @pl.when(k == 0)
    def _():
        for which in range(x_ref.shape[0]):
            stacks = ((own, sib), entries, early_count, sub)
            there = tab_ref[which, COUNTS, 1]
            lax.fori_loop(0, there, start_rows(tab_ref, ROW_ENTRY, which, l_ref, l_sems, *stacks), 0)

            @pl.when(there > 0)
            def _(which=which, stacks=stacks):
                lax.fori_loop(
                    0, tab_ref[which, COUNTS, 0], start_rows(tab_ref, COL_ENTRY, which, w_ref, w_sems, *stacks), 0
                )

            start_pair(which, 0)

    acc_ref[...] = jnp.zeros_like(acc_ref)
    odd = lax.rem(listed, CH) != 0
    steps = lax.div(listed + (CH - 1), CH)
    lax.fori_loop(0, placed, wait_rows(k, l_ref, l_sems, width, sub, 2), 0)

    @pl.when(placed > 0)
    def _():
        lax.fori_loop(0, listed, wait_rows(k, w_ref, w_sems, width, sub, 2), 0)

    def one_pair(pair, carry):
        start_pair(k, pair + 1)
        buffer = lax.rem(pair, 2)

        @pl.when(odd)
        def _():
            x_ref[k, buffer, :, :, block_at(listed)] = jnp.zeros((2, 2 * BLK, BLK), x_ref.dtype)

        def one_place(place, inner):
            def arrived(slot, innermost):
                there = x_ref.at[k, buffer, :, block_at(place - 2 * pair), block_at(slot)]
                pltpu.make_async_copy(there, there, x_sems.at[k, buffer]).wait()
                return innermost

            return lax.fori_loop(0, listed, arrived, inner)

        lax.fori_loop(2 * pair, jnp.minimum(2 * pair + 2, placed), one_place, 0)
        for count in range(1, w_ref.shape[1] // DEPTH + 1):

            @pl.when(steps == count)
            def _(count=count):
                for half in range(2):
                    columns = w_ref.at[k, :, pl.ds(2 * half * width, 2 * width)]
                    parts = product(x_ref.at[k, buffer], columns, pl.ds(0, 2 * BLK), pl.ds(0, count * DEPTH))
                    for q in range(2):
                        v_ref[:, pl.ds((2 * half + q) * width, width)] = parts[q]

        @pl.when(2 * pair + 1 >= placed)
        def _():
            v_ref[pl.ds(BLK, BLK), :] = jnp.zeros((BLK, v_ref.shape[1]), v_ref.dtype)
            l_ref[k, block_at(2 * pair + 1), :] = jnp.zeros((BLK, l_ref.shape[2]), l_ref.dtype)

        left = l_ref[k, block_at(pair, 2 * BLK), :]
        rest = v_ref[...]
        for piece in range(3):
            kept = rest.astype(jnp.bfloat16)
            r_ref[pl.ds(piece * 2 * BLK, 2 * BLK), :] = kept
            rest = rest - kept.astype(jnp.float32)
        for p in range(2):
            turned = jnp.concatenate(
                [left[:, (2 * h + p) * width : (2 * h + p + 1) * width].T for h in range(2)], axis=0
            )
            turned = jnp.concatenate([turned] * 3, axis=1)
            acc_ref[p] += jnp.dot(turned, r_ref[...], preferred_element_type=jnp.float32)
        return carry

    @pl.when((listed > 0) & (placed > 0))
    def _():
        @pl.when(odd)
        def _():
            w_ref[k, block_at(listed), :] = jnp.zeros((BLK, w_ref.shape[2]), w_ref.dtype)

        lax.fori_loop(0, lax.div(placed + 1, 2), one_pair, 0)

    core = tab_ref[0, COUNTS, 2]
    per_half = width // chunk_rows
    for half in range(2):
        first = (core if half == 0 else 1 - core) * per_half
        for i in range(per_half):
            rows = pl.ds(half * width + i * chunk_rows, chunk_rows)
            for out_ref, at in ((mine_ref, 0), (theirs_ref, 2 * width)):
                real, imag = pl.ds(at, width), pl.ds(width + at, width)
                out_ref[first + i, 0, 0] = acc_ref[0, rows, real] - acc_ref[1, rows, imag]
                out_ref[first + i, 0, 1] = acc_ref[0, rows, imag] + acc_ref[1, rows, real]


def vmem_limit(scratch, blocks):
    held = [x for x in scratch if x.dtype in (jnp.bfloat16, jnp.float32)]
    size = sum(math.prod(x.shape) * jnp.dtype(x.dtype).itemsize for x in held)
    return size + 2 * sum(math.prod(shape) * 4 for shape in blocks) + 2 * 2**20


def make_values(k, tab, a, stacks, entries, sub, before=()):
    supernodes, early_count = stacks[0].shape[:2]
    rows, width = a.shape[1], stacks[0].shape[4]
    slots = tab.shape[2] + tab.shape[2] % CH
    tile = max(t for t in range(BLK, min(rows, 768) + 1, BLK) if rows % t == 0)
    out_spec = pl.BlockSpec((1, 2, tile, width), lambda m, _: (k, 0, m, 0))
    out = pltpu.HBM((supernodes, 2, rows, width), jnp.float32)
    scratch = [
        pltpu.VMEM((2, 2, tile, slots * BLK), jnp.bfloat16),
        pltpu.VMEM((1, slots * BLK, 4 * width), jnp.bfloat16),
        pltpu.SemaphoreType.DMA((2,)),
        pltpu.SemaphoreType.DMA((1,)),
    ]
    return pl.pallas_call(
        functools.partial(values_kernel, k, entries, early_count, sub, tile),
        out_shape=(out, out),
        grid_spec=pltpu.PrefetchScalarGridSpec(
            num_scalar_prefetch=1,
            grid=(rows // tile,),
            in_specs=[pl.BlockSpec(memory_space=pl.ANY)] * (5 + len(before)),
            out_specs=(out_spec, out_spec),
            scratch_shapes=scratch,
        ),
        input_output_aliases={6 + i: i for i in range(len(before))},
        compiler_params=pltpu.CompilerParams(vmem_limit_bytes=vmem_limit(scratch, [(2, tile, width)] * 2)),
        cost_estimate=pl.CostEstimate(
            flops=2 * rows * slots * BLK * 4 * width, bytes_accessed=8 * 2**20, transcendentals=0
        ),
        name="values",
    )(tab, a, *stacks, *before)


def make_gram(tab, a, stacks, entries, sub, shares):
    supernodes, early_count = stacks[0].shape[:2]
    rows, width = a.shape[1], stacks[0].shape[4]
    slots = tab.shape[2] + tab.shape[2] % CH
    places = min(slots, (rows // BLK) * (BLK // sub))
    places += places % 2
    out = jax.ShapeDtypeStruct((shares, supernodes, 2, 2 * width // shares, width), jnp.float32)
    out_spec = pl.BlockSpec((shares, 1) + out.shape[2:], lambda k, _: (0, k, 0, 0, 0))
    scratch = [
        pltpu.VMEM((supernodes, 2, 2, 2 * BLK, slots * BLK), jnp.bfloat16),
        pltpu.VMEM((supernodes, slots * BLK, 4 * width), jnp.bfloat16),
        pltpu.VMEM((supernodes, places * BLK, 4 * width), jnp.bfloat16),
        pltpu.VMEM((2 * BLK, 4 * width), jnp.float32),
        pltpu.VMEM((3 * 2 * BLK, 4 * width), jnp.bfloat16),
        pltpu.VMEM((2, 2 * width, 4 * width), jnp.float32),
        pltpu.SemaphoreType.DMA((supernodes, 2)),
        pltpu.SemaphoreType.DMA((supernodes,)),
        pltpu.SemaphoreType.DMA((supernodes,)),
    ]
    return pl.pallas_call(
        functools.partial(gram_kernel, entries, early_count, sub),
        out_shape=(out, out),
        grid_spec=pltpu.PrefetchScalarGridSpec(
            num_scalar_prefetch=1,
            grid=(supernodes,),
            in_specs=[pl.BlockSpec(memory_space=pl.ANY)] * 5,
            out_specs=(out_spec, out_spec),
            scratch_shapes=scratch,
        ),
        compiler_params=pltpu.CompilerParams(vmem_limit_bytes=vmem_limit(scratch, [out.shape] * 2)),
        cost_estimate=pl.CostEstimate(
            flops=supernodes * 2 * BLK * slots * 2 * BLK * 4 * width, bytes_accessed=8 * 2**20, transcendentals=0
        ),
        name="gram",
    )(tab, a, *stacks)


def scatter_sum(total, n_row, first, second):
    half = n_row // 2
    row = lax.axis_index("row")
    level, odd = row // 2, row % 2
    pairs = total.reshape((half, 2) + total.shape[1:])
    came = []
    for d in range(1, half):
        route = [(i, (i + 2 * d) % n_row) for i in range(n_row)]
        sent = lax.dynamic_index_in_dim(pairs, (level + d) % half, 0, keepdims=False)
        came.append(lax.ppermute(sent, "row", route))
    came, first = lax.optimization_barrier((came, first))
    kept = lax.dynamic_index_in_dim(pairs, level, 0, keepdims=False)
    for x in came:
        kept = kept + x
    route = [(i, i ^ 1) for i in range(n_row)]
    sent, first = lax.optimization_barrier((lax.dynamic_index_in_dim(kept, 1 - odd, 0, keepdims=False), first))
    last, both = lax.optimization_barrier((lax.ppermute(sent, "row", route), second(first)))
    return lax.dynamic_index_in_dim(kept, odd, 0, keepdims=False) + last, both


def place_kernel(n_row, diag_ref, *refs):
    *own, other, out_ref = refs
    half = n_row // 2
    row = lax.axis_index("row")
    level, odd = lax.div(row, 2), lax.rem(row, 2)
    size = own[0].shape[2]
    out_ref[...] = diag_ref[...].astype(jnp.float32)
    for d in range(half):
        base = 2 * lax.rem(level - d + half, half)
        out_ref[:, :, block_at(base + odd, size), :] -= own[d][...]
        out_ref[:, :, block_at(base + 1 - odd, size), :] -= other[d]


def gather_shares(diag_blocks, share, n_row, beside):
    half = n_row // 2
    own = [share]
    for d in range(1, half):
        own.append(lax.ppermute(share, "row", [(i, (i + 2 * d) % n_row) for i in range(n_row)]))
    other = lax.ppermute(jnp.stack(own), "row", [(i, i ^ 1) for i in range(n_row)])
    other, beside = lax.optimization_barrier((other, beside))
    vmem = pl.BlockSpec(memory_space=pltpu.VMEM)
    schur = pl.pallas_call(
        functools.partial(place_kernel, n_row),
        out_shape=jax.ShapeDtypeStruct(diag_blocks.shape, jnp.float32),
        in_specs=[vmem] * (half + 2),
        out_specs=vmem,
        name="place",
    )(diag_blocks, *own, other)
    return schur, beside


def local(n_row, inverse_pairs, factor_rows, diag_blocks, row_lists, block_order):
    supernodes = row_lists.shape[0]
    local_rows, local_cols = inverse_pairs.shape[1:]
    per_chip = factor_rows.shape[2]
    sub = min(BLK, per_chip)
    entries = per_chip // sub
    half = n_row // 2
    cycle = list(range(0, n_row, 2)) + list(range(n_row - 1, 0, -2))
    ahead = [(cycle[i], cycle[(i + 1) % n_row]) for i in range(n_row)]
    behind = [(b, a) for a, b in ahead]
    swap = [(0, 1), (1, 0)]

    tab = make_table(n_row, entries, sub, local_cols // BLK, local_rows // BLK, row_lists, block_order)

    chunks = [[factor_rows[k]] for k in range(supernodes)]
    up = [factor_rows[k] for k in range(supernodes)]
    down = list(up)
    for d in range(1, half):
        for k in range(supernodes):
            up[k] = lax.ppermute(up[k], "row", ahead)
            down[k] = lax.ppermute(down[k], "row", behind)
            chunks[k] += [up[k], down[k]]
        if d == 1:
            up[0], tab = lax.optimization_barrier((up[0], tab))
    for k in range(supernodes):
        last = [lax.ppermute(up[k][0:1], "row", ahead), lax.ppermute(down[k][1:2], "row", behind)]
        chunks[k].append(jnp.concatenate(last, axis=0))
    early = max(1, n_row - 3)
    own = [
        jnp.stack([jnp.stack(chunks[k][:early]) for k in range(supernodes)]),
        jnp.stack([jnp.stack(chunks[k][early:]) for k in range(supernodes)]),
    ]
    stacks = own + [lax.ppermute(x, "col", swap) for x in own]

    mine, theirs = make_gram(tab, inverse_pairs, stacks, entries, sub, n_row)
    total = mine + lax.ppermute(theirs, "col", swap)
    total, tab = lax.optimization_barrier((total, tab))
    def rest(made):
        for k in range(1, supernodes):
            made = make_values(k, tab, inverse_pairs, stacks, entries, sub, made)
        return made

    made = make_values(0, tab, inverse_pairs, stacks, entries, sub)
    share, (mine, theirs) = scatter_sum(total, n_row, made, rest)
    values = mine + lax.ppermute(theirs, "col", swap)
    schur, values = gather_shares(diag_blocks, share, n_row, values)
    return (values, schur)


def solution(mesh):
    in_specs = (
        P("pole", "row", "col"),
        P("pole", None, "row", "col"),
        P("pole", None, None, "col"),
        P(),
        P(),
    )
    out_specs = (P("pole", None, "row", "col"), P("pole", None, None, "col"))
    body = functools.partial(local, mesh.shape["row"])
    return jax.shard_map(body, mesh=mesh, in_specs=in_specs, out_specs=out_specs, check_vma=False)
```

```python
import functools
import math

import jax
import jax.numpy as jnp
from jax import lax
from jax.experimental import pallas as pl
from jax.experimental.pallas import tpu as pltpu
from jax.sharding import PartitionSpec as P

BLK = 128
CH = 2
DEPTH = CH * BLK
COL_ENTRY, COL_BLOCK, ROW_ENTRY, ROW_BLOCK, OFFSET, COUNTS = range(6)


def block_at(index, size=BLK):
    return pl.ds(pl.multiple_of(index * size, size), size)


def table_kernel(n_row, entries, sub, col_blocks, row_blocks, lists_ref, order_ref, tab_ref, where_ref):
    half = n_row // 2
    row, core = lax.axis_index("row"), lax.axis_index("col")
    place = jnp.where(lax.rem(row, 2) == 0, lax.div(row, 2), n_row - 1 - lax.div(row, 2))

    def invert(g, carry):
        where_ref[order_ref[g]] = g
        return carry

    lax.fori_loop(0, order_ref.shape[0], invert, 0, unroll=8)
    for k in range(tab_ref.shape[0]):

        def one(i, counts, k=k):
            listed, placed = counts
            chunk, at = lax.div(i, entries), lax.rem(i, entries)
            step = lax.div(chunk + 1, 2)
            step = jnp.where((lax.rem(chunk, 2) == 1) | (chunk == n_row - 1), step, -step)
            source = lax.rem(place - step + 2 * n_row, n_row)
            source = jnp.where(source < half, 2 * source, 2 * (n_row - 1 - source) + 1)
            first = source * (entries * sub) + at * sub
            block = where_ref[lists_ref[k, lax.div(first, BLK)]]
            tab_ref[k, OFFSET, i] = lax.rem(first, BLK)
            col, line = block - core * col_blocks, block - row * row_blocks
            is_col = (col >= 0) & (col < col_blocks)
            is_row = (line >= 0) & (line < row_blocks)

            @pl.when(is_col)
            def _():
                tab_ref[k, COL_ENTRY, listed] = i
                tab_ref[k, COL_BLOCK, listed] = col

            @pl.when(is_row)
            def _():
                tab_ref[k, ROW_ENTRY, placed] = i
                tab_ref[k, ROW_BLOCK, placed] = line

            return listed + is_col.astype(jnp.int32), placed + is_row.astype(jnp.int32)

        listed, placed = lax.fori_loop(0, n_row * entries, one, (jnp.int32(0), jnp.int32(0)), unroll=4)
        tab_ref[k, COUNTS, 0] = listed
        tab_ref[k, COUNTS, 1] = placed
        tab_ref[k, COUNTS, 2] = core


def make_table(n_row, entries, sub, col_blocks, row_blocks, row_lists, block_order):
    smem = pl.BlockSpec(memory_space=pltpu.SMEM)
    return pl.pallas_call(
        functools.partial(table_kernel, n_row, entries, sub, col_blocks, row_blocks),
        out_shape=jax.ShapeDtypeStruct((row_lists.shape[0], 6, max(n_row * entries, 3)), jnp.int32),
        in_specs=[smem] * 2,
        out_specs=smem,
        scratch_shapes=[pltpu.SMEM(block_order.shape, jnp.int32)],
        name="table",
    )(row_lists, block_order)


def start_rows(tab_ref, kind, k, to_ref, sems, halves, entries, early_count, sub):
    def one(at, carry):
        entry = tab_ref[k, kind, at]
        chunk, part = lax.div(entry, entries), lax.rem(entry, entries)
        rows = block_at(at)
        if sub < BLK:
            to_ref[k, rows, :] = jnp.zeros((BLK, to_ref.shape[2]), to_ref.dtype)
            rows = pl.ds(pl.multiple_of(at * BLK + tab_ref[k, OFFSET, entry], sub), sub)

        def copy(stack, chunk, there, p):
            here = stack.at[k, chunk, p, block_at(part, sub), :]
            pltpu.make_async_copy(here, there, sems.at[k]).start()

        for half, stacks in enumerate(halves):
            width = stacks[0].shape[4]
            for p in range(2):
                there = to_ref.at[k, rows, pl.ds((2 * half + p) * width, width)]

                @pl.when(chunk < early_count)
                def _(stacks=stacks, there=there, p=p):
                    copy(stacks[0], chunk, there, p)

                @pl.when(chunk >= early_count)
                def _(stacks=stacks, there=there, p=p):
                    copy(stacks[1], chunk - early_count, there, p)

        return carry

    return one


def wait_rows(k, to_ref, sems, width, sub, halves):
    def one(at, carry):
        there = to_ref.at[k, pl.ds(0, sub), pl.ds(0, 2 * halves * width)]
        pltpu.make_async_copy(there, there, sems.at[k]).wait()
        return carry

    return one


def product(x, w, x_rows, depth):
    width = w.shape[1] // 2
    real, imag = (
        jnp.dot(x[p, x_rows, depth], w[depth, :], preferred_element_type=jnp.float32) for p in range(2)
    )
    return imag[:, width:] - real[:, :width], -(real[:, width:] + imag[:, :width])


def values_kernel(entries, early_count, sub, tile, tab_ref, a_ref, own0, own1, sib0, sib1, *refs):
    mine_ref, theirs_ref, x_ref, w_ref, x_sems, w_sems = refs
    k, step = pl.program_id(0), pl.program_id(1)
    supernodes, tiles = pl.num_programs(0), pl.num_programs(1)
    width = mine_ref.shape[3]
    listed = tab_ref[k, COUNTS, 0]
    now = k * tiles + step

    def start(at):
        which, rows, buffer = lax.div(at, tiles), lax.rem(at, tiles), lax.rem(at, 2)

        def one(slot, carry):
            pltpu.make_async_copy(
                a_ref.at[:, block_at(rows, tile), block_at(tab_ref[which, COL_BLOCK, slot])],
                x_ref.at[buffer, :, :, block_at(slot)],
                x_sems.at[buffer],
            ).start()
            return carry

        lax.fori_loop(0, tab_ref[which, COUNTS, 0], one, 0)

    def start_weights(which):
        halves = ((own0, own1), (sib0, sib1))
        rows = start_rows(tab_ref, COL_ENTRY, which, w_ref, w_sems, halves, entries, early_count, sub)
        lax.fori_loop(0, tab_ref[which, COUNTS, 0], rows, 0)

    @pl.when(now == 0)
    def _():
        start(now)
        start_weights(0)

    @pl.when(now + 1 < supernodes * tiles)
    def _():
        start(now + 1)

    for which in range(1, w_ref.shape[0]):

        @pl.when(now == which * tiles - 1)
        def _(which=which):
            start_weights(which)

    @pl.when(step == 0)
    def _():
        @pl.when(lax.rem(listed, CH) != 0)
        def _():
            w_ref[k, block_at(listed), :] = jnp.zeros((BLK, w_ref.shape[2]), w_ref.dtype)

        lax.fori_loop(0, listed, wait_rows(k, w_ref, w_sems, width, sub, 2), 0)

    buffer = lax.rem(now, 2)

    @pl.when(lax.rem(listed, CH) != 0)
    def _():
        x_ref[buffer, :, :, block_at(listed)] = jnp.zeros((2, tile, BLK), x_ref.dtype)

    def arrived(slot, carry):
        there = x_ref.at[buffer, :, :, block_at(slot)]
        pltpu.make_async_copy(there, there, x_sems.at[buffer]).wait()
        return carry

    lax.fori_loop(0, listed, arrived, 0)
    steps = lax.div(listed + (CH - 1), CH)

    @pl.when(steps == 0)
    def _():
        mine_ref[...] = jnp.zeros_like(mine_ref)
        theirs_ref[...] = jnp.zeros_like(theirs_ref)

    for count in range(1, w_ref.shape[1] // DEPTH + 1):

        @pl.when(steps == count)
        def _(count=count):
            for half, out_ref in enumerate((mine_ref, theirs_ref)):
                columns = w_ref.at[k, :, pl.ds(2 * half * width, 2 * width)]
                parts = product(x_ref.at[buffer], columns, pl.ds(0, tile), pl.ds(0, count * DEPTH))
                for q in range(2):
                    out_ref[0, q] = parts[q]


def gram_kernel(entries, early_count, sub, tab_ref, a_ref, own0, own1, sib0, sib1, *refs):
    mine_ref, theirs_ref, x_ref, w_ref, l_ref, v_ref, r_ref, acc_ref, x_sems, w_sems, l_sems = refs
    k = pl.program_id(0)
    own, sib = (own0, own1), (sib0, sib1)
    width = mine_ref.shape[4]
    chunk_rows = mine_ref.shape[3]
    listed, placed = tab_ref[k, COUNTS, 0], tab_ref[k, COUNTS, 1]

    def start_pair(which, pair):
        def one_place(place, carry):
            rows = block_at(tab_ref[which, ROW_BLOCK, place])

            def one(slot, inner):
                pltpu.make_async_copy(
                    a_ref.at[:, rows, block_at(tab_ref[which, COL_BLOCK, slot])],
                    x_ref.at[which, lax.rem(pair, 2), :, block_at(place - 2 * pair), block_at(slot)],
                    x_sems.at[which, lax.rem(pair, 2)],
                ).start()
                return inner

            return lax.fori_loop(0, tab_ref[which, COUNTS, 0], one, carry)

        lax.fori_loop(2 * pair, jnp.minimum(2 * pair + 2, tab_ref[which, COUNTS, 1]), one_place, 0)

    @pl.when(k == 0)
    def _():
        for which in range(x_ref.shape[0]):
            stacks = ((own, sib), entries, early_count, sub)
            there = tab_ref[which, COUNTS, 1]
            start_pair(which, 0)

            @pl.when(there > 0)
            def _(which=which, stacks=stacks):
                lax.fori_loop(
                    0, tab_ref[which, COUNTS, 0], start_rows(tab_ref, COL_ENTRY, which, w_ref, w_sems, *stacks), 0
                )

            lax.fori_loop(0, there, start_rows(tab_ref, ROW_ENTRY, which, l_ref, l_sems, *stacks), 0)

    acc_ref[...] = jnp.zeros_like(acc_ref)
    odd = lax.rem(listed, CH) != 0
    steps = lax.div(listed + (CH - 1), CH)
    lax.fori_loop(0, placed, wait_rows(k, l_ref, l_sems, width, sub, 2), 0)

    @pl.when(placed > 0)
    def _():
        lax.fori_loop(0, listed, wait_rows(k, w_ref, w_sems, width, sub, 2), 0)

    def one_group(places, pair, carry):
        start_pair(k, pair + 1)
        buffer, rows = lax.rem(pair, 2), places * BLK

        @pl.when(odd)
        def _():
            x_ref[k, buffer, :, pl.ds(0, rows), block_at(listed)] = jnp.zeros((2, rows, BLK), x_ref.dtype)

        def arrived(slot, inner):
            for place in range(places):
                there = x_ref.at[k, buffer, :, pl.ds(place * BLK, BLK), block_at(slot)]
                pltpu.make_async_copy(there, there, x_sems.at[k, buffer]).wait()
            return inner

        lax.fori_loop(0, listed, arrived, 0)
        for count in range(1, w_ref.shape[1] // DEPTH + 1):

            @pl.when(steps == count)
            def _(count=count):
                for half in range(2):
                    columns = w_ref.at[k, :, pl.ds(2 * half * width, 2 * width)]
                    parts = product(x_ref.at[k, buffer], columns, pl.ds(0, rows), pl.ds(0, count * DEPTH))
                    for q in range(2):
                        v_ref[pl.ds(0, rows), pl.ds((2 * half + q) * width, width)] = parts[q]

        rest = v_ref[pl.ds(0, rows), :]
        for piece in range(3):
            kept = rest.astype(jnp.bfloat16)
            r_ref[pl.ds(piece * rows, rows), :] = kept
            rest = rest - kept.astype(jnp.float32)
        left = l_ref[k, pl.ds(pl.multiple_of(pair * 2 * BLK, 2 * BLK), rows), :]
        for p in range(2):
            turned = jnp.concatenate(
                [left[:, (2 * h + p) * width : (2 * h + p + 1) * width].T for h in range(2)], axis=0
            )
            turned = jnp.concatenate([turned] * 3, axis=1)
            acc_ref[p] += jnp.dot(turned, r_ref[pl.ds(0, 3 * rows), :], preferred_element_type=jnp.float32)
        return carry

    @pl.when((listed > 0) & (placed > 0))
    def _():
        @pl.when(odd)
        def _():
            w_ref[k, block_at(listed), :] = jnp.zeros((BLK, w_ref.shape[2]), w_ref.dtype)

        pairs = lax.div(placed, 2)
        lax.fori_loop(0, pairs, functools.partial(one_group, 2), 0)

        @pl.when(lax.rem(placed, 2) != 0)
        def _():
            one_group(1, pairs, 0)

    core = tab_ref[0, COUNTS, 2]
    per_half = width // chunk_rows
    for half in range(2):
        first = (core if half == 0 else 1 - core) * per_half
        for i in range(per_half):
            rows = pl.ds(half * width + i * chunk_rows, chunk_rows)
            for out_ref, at in ((mine_ref, 0), (theirs_ref, 2 * width)):
                real, imag = pl.ds(at, width), pl.ds(width + at, width)
                out_ref[first + i, 0, 0] = acc_ref[0, rows, real] - acc_ref[1, rows, imag]
                out_ref[first + i, 0, 1] = acc_ref[0, rows, imag] + acc_ref[1, rows, real]


def vmem_limit(scratch, blocks):
    held = [x for x in scratch if x.dtype in (jnp.bfloat16, jnp.float32)]
    size = sum(math.prod(x.shape) * jnp.dtype(x.dtype).itemsize for x in held)
    return size + 2 * sum(math.prod(shape) * 4 for shape in blocks) + 2 * 2**20


def make_values(tab, a, stacks, entries, sub):
    supernodes, early_count = stacks[0].shape[:2]
    rows, width = a.shape[1], stacks[0].shape[4]
    slots = tab.shape[2] + tab.shape[2] % CH
    tile = max(t for t in range(BLK, min(rows, 768) + 1, BLK) if rows % t == 0)
    out_spec = pl.BlockSpec((1, 2, tile, width), lambda k, m, _: (k, 0, m, 0))
    out = pltpu.HBM((supernodes, 2, rows, width), jnp.float32)
    scratch = [
        pltpu.VMEM((2, 2, tile, slots * BLK), jnp.bfloat16),
        pltpu.VMEM((supernodes, slots * BLK, 4 * width), jnp.bfloat16),
        pltpu.SemaphoreType.DMA((2,)),
        pltpu.SemaphoreType.DMA((supernodes,)),
    ]
    return pl.pallas_call(
        functools.partial(values_kernel, entries, early_count, sub, tile),
        out_shape=(out, out),
        grid_spec=pltpu.PrefetchScalarGridSpec(
            num_scalar_prefetch=1,
            grid=(supernodes, rows // tile),
            in_specs=[pl.BlockSpec(memory_space=pl.ANY)] * 5,
            out_specs=(out_spec, out_spec),
            scratch_shapes=scratch,
        ),
        compiler_params=pltpu.CompilerParams(vmem_limit_bytes=vmem_limit(scratch, [(2, tile, width)] * 2)),
        cost_estimate=pl.CostEstimate(
            flops=2 * supernodes * rows * slots * BLK * 4 * width, bytes_accessed=16 * 2**20, transcendentals=0
        ),
        name="values",
    )(tab, a, *stacks)


def make_gram(tab, a, stacks, entries, sub, shares):
    supernodes, early_count = stacks[0].shape[:2]
    rows, width = a.shape[1], stacks[0].shape[4]
    slots = tab.shape[2] + tab.shape[2] % CH
    places = min(slots, (rows // BLK) * (BLK // sub))
    places += places % 2
    out = jax.ShapeDtypeStruct((shares, supernodes, 2, 2 * width // shares, width), jnp.float32)
    out_spec = pl.BlockSpec((shares, 1) + out.shape[2:], lambda k, _: (0, k, 0, 0, 0))
    scratch = [
        pltpu.VMEM((supernodes, 2, 2, 2 * BLK, slots * BLK), jnp.bfloat16),
        pltpu.VMEM((supernodes, slots * BLK, 4 * width), jnp.bfloat16),
        pltpu.VMEM((supernodes, places * BLK, 4 * width), jnp.bfloat16),
        pltpu.VMEM((2 * BLK, 4 * width), jnp.float32),
        pltpu.VMEM((3 * 2 * BLK, 4 * width), jnp.bfloat16),
        pltpu.VMEM((2, 2 * width, 4 * width), jnp.float32),
        pltpu.SemaphoreType.DMA((supernodes, 2)),
        pltpu.SemaphoreType.DMA((supernodes,)),
        pltpu.SemaphoreType.DMA((supernodes,)),
    ]
    return pl.pallas_call(
        functools.partial(gram_kernel, entries, early_count, sub),
        out_shape=(out, out),
        grid_spec=pltpu.PrefetchScalarGridSpec(
            num_scalar_prefetch=1,
            grid=(supernodes,),
            in_specs=[pl.BlockSpec(memory_space=pl.ANY)] * 5,
            out_specs=(out_spec, out_spec),
            scratch_shapes=scratch,
        ),
        compiler_params=pltpu.CompilerParams(vmem_limit_bytes=vmem_limit(scratch, [out.shape] * 2)),
        cost_estimate=pl.CostEstimate(
            flops=supernodes * 2 * BLK * slots * 2 * BLK * 4 * width, bytes_accessed=8 * 2**20, transcendentals=0
        ),
        name="gram",
    )(tab, a, *stacks)


def scatter_sum(total, n_row, beside):
    half = n_row // 2
    row = lax.axis_index("row")
    level, odd = row // 2, row % 2
    pairs = total.reshape((half, 2) + total.shape[1:])
    came = []
    for d in range(1, half):
        route = [(i, (i + 2 * d) % n_row) for i in range(n_row)]
        sent = lax.dynamic_index_in_dim(pairs, (level + d) % half, 0, keepdims=False)
        came.append(lax.ppermute(sent, "row", route))
    *came, beside = lax.optimization_barrier((*came, beside))
    kept = lax.dynamic_index_in_dim(pairs, level, 0, keepdims=False)
    for x in came:
        kept = kept + x
    route = [(i, i ^ 1) for i in range(n_row)]
    sent = lax.dynamic_index_in_dim(kept, 1 - odd, 0, keepdims=False)
    last, beside = lax.optimization_barrier((lax.ppermute(sent, "row", route), beside))
    return lax.dynamic_index_in_dim(kept, odd, 0, keepdims=False) + last, beside


def place_kernel(n_row, diag_ref, *refs):
    *own, other, out_ref = refs
    half = n_row // 2
    row = lax.axis_index("row")
    level, odd = lax.div(row, 2), lax.rem(row, 2)
    size = own[0].shape[2]
    out_ref[...] = diag_ref[...].astype(jnp.float32)
    for d in range(half):
        base = 2 * lax.rem(level - d + half, half)
        out_ref[:, :, block_at(base + odd, size), :] -= own[d][...]
        out_ref[:, :, block_at(base + 1 - odd, size), :] -= other[d]


def gather_shares(diag_blocks, share, n_row, beside):
    half = n_row // 2
    own = [share]
    for d in range(1, half):
        own.append(lax.ppermute(share, "row", [(i, (i + 2 * d) % n_row) for i in range(n_row)]))
    other = lax.ppermute(jnp.stack(own), "row", [(i, i ^ 1) for i in range(n_row)])
    other, beside = lax.optimization_barrier((other, beside))
    vmem = pl.BlockSpec(memory_space=pltpu.VMEM)
    schur = pl.pallas_call(
        functools.partial(place_kernel, n_row),
        out_shape=jax.ShapeDtypeStruct(diag_blocks.shape, jnp.float32),
        in_specs=[vmem] * (half + 2),
        out_specs=vmem,
        name="place",
    )(diag_blocks, *own, other)
    return schur, beside


def local(n_row, inverse_pairs, factor_rows, diag_blocks, row_lists, block_order):
    supernodes = row_lists.shape[0]
    local_rows, local_cols = inverse_pairs.shape[1:]
    per_chip = factor_rows.shape[2]
    sub = min(BLK, per_chip)
    entries = per_chip // sub
    half = n_row // 2
    cycle = list(range(0, n_row, 2)) + list(range(n_row - 1, 0, -2))
    ahead = [(cycle[i], cycle[(i + 1) % n_row]) for i in range(n_row)]
    behind = [(b, a) for a, b in ahead]
    swap = [(0, 1), (1, 0)]

    tab = make_table(n_row, entries, sub, local_cols // BLK, local_rows // BLK, row_lists, block_order)

    chunks = [[factor_rows[k]] for k in range(supernodes)]
    up = [factor_rows[k] for k in range(supernodes)]
    down = list(up)
    for d in range(1, half):
        for k in range(supernodes):
            up[k] = lax.ppermute(up[k], "row", ahead)
            down[k] = lax.ppermute(down[k], "row", behind)
            chunks[k] += [up[k], down[k]]
        if d == 1:
            up[0], tab = lax.optimization_barrier((up[0], tab))
    for k in range(supernodes):
        last = [lax.ppermute(up[k][0:1], "row", ahead), lax.ppermute(down[k][1:2], "row", behind)]
        chunks[k].append(jnp.concatenate(last, axis=0))
    early = max(1, n_row - 3)
    own = [
        jnp.stack([jnp.stack(chunks[k][:early]) for k in range(supernodes)]),
        jnp.stack([jnp.stack(chunks[k][early:]) for k in range(supernodes)]),
    ]
    stacks = own + [lax.ppermute(x, "col", swap) for x in own]

    mine, theirs = make_gram(tab, inverse_pairs, stacks, entries, sub, n_row)
    total = mine + lax.ppermute(theirs, "col", swap)
    total, tab = lax.optimization_barrier((total, tab))
    mine, theirs = make_values(tab, inverse_pairs, stacks, entries, sub)
    share, theirs = scatter_sum(total, n_row, theirs)
    values = mine + lax.ppermute(theirs, "col", swap)
    schur, values = gather_shares(diag_blocks, share, n_row, values)
    return (values, schur)


def solution(mesh):
    in_specs = (
        P("pole", "row", "col"),
        P("pole", None, "row", "col"),
        P("pole", None, None, "col"),
        P(),
        P(),
    )
    out_specs = (P("pole", None, "row", "col"), P("pole", None, None, "col"))
    body = functools.partial(local, mesh.shape["row"])
    return jax.shard_map(body, mesh=mesh, in_specs=in_specs, out_specs=out_specs, check_vma=False)
```

```python
import functools
import math

import jax
import jax.numpy as jnp
from jax import lax
from jax.experimental import pallas as pl
from jax.experimental.pallas import tpu as pltpu
from jax.sharding import PartitionSpec as P

BLK = 128
CH = 2
DEPTH = CH * BLK
COL_ENTRY, COL_BLOCK, ROW_ENTRY, ROW_BLOCK, OFFSET, COUNTS = range(6)


def block_at(index, size=BLK):
    return pl.ds(pl.multiple_of(index * size, size), size)


def table_kernel(n_row, entries, sub, col_blocks, row_blocks, lists_ref, order_ref, tab_ref, where_ref):
    half = n_row // 2
    row, core = lax.axis_index("row"), lax.axis_index("col")
    place = jnp.where(lax.rem(row, 2) == 0, lax.div(row, 2), n_row - 1 - lax.div(row, 2))

    def invert(g, carry):
        where_ref[order_ref[g]] = g
        return carry

    lax.fori_loop(0, order_ref.shape[0], invert, 0, unroll=8)
    for k in range(tab_ref.shape[0]):

        def one(i, counts, k=k):
            listed, placed = counts
            chunk, at = lax.div(i, entries), lax.rem(i, entries)
            step = lax.div(chunk + 1, 2)
            step = jnp.where((lax.rem(chunk, 2) == 1) | (chunk == n_row - 1), step, -step)
            source = lax.rem(place - step + 2 * n_row, n_row)
            source = jnp.where(source < half, 2 * source, 2 * (n_row - 1 - source) + 1)
            first = source * (entries * sub) + at * sub
            block = where_ref[lists_ref[k, lax.div(first, BLK)]]
            tab_ref[k, OFFSET, i] = lax.rem(first, BLK)
            col, line = block - core * col_blocks, block - row * row_blocks
            is_col = (col >= 0) & (col < col_blocks)
            is_row = (line >= 0) & (line < row_blocks)

            @pl.when(is_col)
            def _():
                tab_ref[k, COL_ENTRY, listed] = i
                tab_ref[k, COL_BLOCK, listed] = col

            @pl.when(is_row)
            def _():
                tab_ref[k, ROW_ENTRY, placed] = i
                tab_ref[k, ROW_BLOCK, placed] = line

            return listed + is_col.astype(jnp.int32), placed + is_row.astype(jnp.int32)

        listed, placed = lax.fori_loop(0, n_row * entries, one, (jnp.int32(0), jnp.int32(0)), unroll=4)
        tab_ref[k, COUNTS, 0] = listed
        tab_ref[k, COUNTS, 1] = placed
        tab_ref[k, COUNTS, 2] = core


def make_table(n_row, entries, sub, col_blocks, row_blocks, row_lists, block_order):
    smem = pl.BlockSpec(memory_space=pltpu.SMEM)
    return pl.pallas_call(
        functools.partial(table_kernel, n_row, entries, sub, col_blocks, row_blocks),
        out_shape=jax.ShapeDtypeStruct((row_lists.shape[0], 6, max(n_row * entries, 3)), jnp.int32),
        in_specs=[smem] * 2,
        out_specs=smem,
        scratch_shapes=[pltpu.SMEM(block_order.shape, jnp.int32)],
        name="table",
    )(row_lists, block_order)


def start_rows(tab_ref, kind, k, to_ref, sems, halves, entries, early_count, sub):
    def one(at, carry):
        entry = tab_ref[k, kind, at]
        chunk, part = lax.div(entry, entries), lax.rem(entry, entries)
        rows = block_at(at)
        if sub < BLK:
            to_ref[k, rows, :] = jnp.zeros((BLK, to_ref.shape[2]), to_ref.dtype)
            rows = pl.ds(pl.multiple_of(at * BLK + tab_ref[k, OFFSET, entry], sub), sub)

        def copy(stack, chunk, there, p):
            here = stack.at[k, chunk, p, block_at(part, sub), :]
            pltpu.make_async_copy(here, there, sems.at[k]).start()

        for half, stacks in enumerate(halves):
            width = stacks[0].shape[4]
            for p in range(2):
                there = to_ref.at[k, rows, pl.ds((2 * half + p) * width, width)]

                @pl.when(chunk < early_count)
                def _(stacks=stacks, there=there, p=p):
                    copy(stacks[0], chunk, there, p)

                @pl.when(chunk >= early_count)
                def _(stacks=stacks, there=there, p=p):
                    copy(stacks[1], chunk - early_count, there, p)

        return carry

    return one


def wait_rows(k, to_ref, sems, width, sub, halves):
    def one(at, carry):
        there = to_ref.at[k, pl.ds(0, sub), pl.ds(0, 2 * halves * width)]
        pltpu.make_async_copy(there, there, sems.at[k]).wait()
        return carry

    return one


def product(x, w, x_rows, depth):
    width = w.shape[1] // 2
    real, imag = (
        jnp.dot(x[p, x_rows, depth], w[depth, :], preferred_element_type=jnp.float32) for p in range(2)
    )
    return imag[:, width:] - real[:, :width], -(real[:, width:] + imag[:, :width])


def values_kernel(tile, tab_ref, a_ref, rows_ref, mine_ref, theirs_ref, x_ref, w_ref, x_sems, w_sems):
    k, step = pl.program_id(0), pl.program_id(1)
    supernodes, tiles = pl.num_programs(0), pl.num_programs(1)
    width = mine_ref.shape[3]
    listed = tab_ref[k, COUNTS, 0]
    now = k * tiles + step

    def start(at):
        which, rows, buffer = lax.div(at, tiles), lax.rem(at, tiles), lax.rem(at, 2)

        def one(slot, carry):
            pltpu.make_async_copy(
                a_ref.at[:, block_at(rows, tile), block_at(tab_ref[which, COL_BLOCK, slot])],
                x_ref.at[buffer, :, :, block_at(slot)],
                x_sems.at[buffer],
            ).start()
            return carry

        lax.fori_loop(0, tab_ref[which, COUNTS, 0], one, 0)

    def weights(which):
        return pltpu.make_async_copy(rows_ref.at[which], w_ref.at[which], w_sems.at[which])

    @pl.when(now == 0)
    def _():
        start(now)
        for which in range(w_ref.shape[0]):
            weights(which).start()

    @pl.when(now + 1 < supernodes * tiles)
    def _():
        start(now + 1)

    @pl.when(step == 0)
    def _():
        weights(k).wait()

    buffer = lax.rem(now, 2)

    @pl.when(lax.rem(listed, CH) != 0)
    def _():
        x_ref[buffer, :, :, block_at(listed)] = jnp.zeros((2, tile, BLK), x_ref.dtype)

    def arrived(slot, carry):
        there = x_ref.at[buffer, :, :, block_at(slot)]
        pltpu.make_async_copy(there, there, x_sems.at[buffer]).wait()
        return carry

    lax.fori_loop(0, listed, arrived, 0)
    steps = lax.div(listed + (CH - 1), CH)

    @pl.when(steps == 0)
    def _():
        mine_ref[...] = jnp.zeros_like(mine_ref)
        theirs_ref[...] = jnp.zeros_like(theirs_ref)

    for count in range(1, w_ref.shape[1] // DEPTH + 1):

        @pl.when(steps == count)
        def _(count=count):
            for half, out_ref in enumerate((mine_ref, theirs_ref)):
                columns = w_ref.at[k, :, pl.ds(2 * half * width, 2 * width)]
                parts = product(x_ref.at[buffer], columns, pl.ds(0, tile), pl.ds(0, count * DEPTH))
                for q in range(2):
                    out_ref[0, q] = parts[q]


def gram_kernel(entries, early_count, sub, tab_ref, a_ref, own0, own1, sib0, sib1, *refs):
    mine_ref, theirs_ref, rows_ref, x_ref, w_ref, l_ref, v_ref, r_ref, acc_ref, x_sems, w_sems, l_sems, out_sem = refs
    k = pl.program_id(0)
    own, sib = (own0, own1), (sib0, sib1)
    width = mine_ref.shape[4]
    chunk_rows = mine_ref.shape[3]
    listed, placed = tab_ref[k, COUNTS, 0], tab_ref[k, COUNTS, 1]

    def start_pair(which, pair):
        def one_place(place, carry):
            rows = block_at(tab_ref[which, ROW_BLOCK, place])

            def one(slot, inner):
                pltpu.make_async_copy(
                    a_ref.at[:, rows, block_at(tab_ref[which, COL_BLOCK, slot])],
                    x_ref.at[which, lax.rem(pair, 2), :, block_at(place - 2 * pair), block_at(slot)],
                    x_sems.at[which, lax.rem(pair, 2)],
                ).start()
                return inner

            return lax.fori_loop(0, tab_ref[which, COUNTS, 0], one, carry)

        lax.fori_loop(2 * pair, jnp.minimum(2 * pair + 2, tab_ref[which, COUNTS, 1]), one_place, 0)

    @pl.when(k == 0)
    def _():
        for which in range(x_ref.shape[0]):
            stacks = ((own, sib), entries, early_count, sub)
            there = tab_ref[which, COUNTS, 1]
            start_pair(which, 0)
            lax.fori_loop(
                0, tab_ref[which, COUNTS, 0], start_rows(tab_ref, COL_ENTRY, which, w_ref, w_sems, *stacks), 0
            )
            lax.fori_loop(0, there, start_rows(tab_ref, ROW_ENTRY, which, l_ref, l_sems, *stacks), 0)

    acc_ref[...] = jnp.zeros_like(acc_ref)
    odd = lax.rem(listed, CH) != 0
    steps = lax.div(listed + (CH - 1), CH)
    lax.fori_loop(0, listed, wait_rows(k, w_ref, w_sems, width, sub, 2), 0)

    @pl.when(odd)
    def _():
        w_ref[k, block_at(listed), :] = jnp.zeros((BLK, w_ref.shape[2]), w_ref.dtype)

    handed = pltpu.make_async_copy(w_ref.at[k], rows_ref.at[k], out_sem)
    handed.start()
    lax.fori_loop(0, placed, wait_rows(k, l_ref, l_sems, width, sub, 2), 0)

    def one_group(places, pair, carry):
        start_pair(k, pair + 1)
        buffer, rows = lax.rem(pair, 2), places * BLK

        @pl.when(odd)
        def _():
            x_ref[k, buffer, :, pl.ds(0, rows), block_at(listed)] = jnp.zeros((2, rows, BLK), x_ref.dtype)

        def arrived(slot, inner):
            for place in range(places):
                there = x_ref.at[k, buffer, :, pl.ds(place * BLK, BLK), block_at(slot)]
                pltpu.make_async_copy(there, there, x_sems.at[k, buffer]).wait()
            return inner

        lax.fori_loop(0, listed, arrived, 0)
        for count in range(1, w_ref.shape[1] // DEPTH + 1):

            @pl.when(steps == count)
            def _(count=count):
                for half in range(2):
                    columns = w_ref.at[k, :, pl.ds(2 * half * width, 2 * width)]
                    parts = product(x_ref.at[k, buffer], columns, pl.ds(0, rows), pl.ds(0, count * DEPTH))
                    for q in range(2):
                        v_ref[pl.ds(0, rows), pl.ds((2 * half + q) * width, width)] = parts[q]

        rest = v_ref[pl.ds(0, rows), :]
        for piece in range(3):
            kept = rest.astype(jnp.bfloat16)
            r_ref[pl.ds(piece * rows, rows), :] = kept
            rest = rest - kept.astype(jnp.float32)
        left = l_ref[k, pl.ds(pl.multiple_of(pair * 2 * BLK, 2 * BLK), rows), :]
        for p in range(2):
            turned = jnp.concatenate(
                [left[:, (2 * h + p) * width : (2 * h + p + 1) * width].T for h in range(2)], axis=0
            )
            turned = jnp.concatenate([turned] * 3, axis=1)
            acc_ref[p] += jnp.dot(turned, r_ref[pl.ds(0, 3 * rows), :], preferred_element_type=jnp.float32)
        return carry

    @pl.when((listed > 0) & (placed > 0))
    def _():
        pairs = lax.div(placed, 2)
        lax.fori_loop(0, pairs, functools.partial(one_group, 2), 0)

        @pl.when(lax.rem(placed, 2) != 0)
        def _():
            one_group(1, pairs, 0)

    core = tab_ref[0, COUNTS, 2]
    per_half = width // chunk_rows
    for half in range(2):
        first = (core if half == 0 else 1 - core) * per_half
        for i in range(per_half):
            rows = pl.ds(half * width + i * chunk_rows, chunk_rows)
            for out_ref, at in ((mine_ref, 0), (theirs_ref, 2 * width)):
                real, imag = pl.ds(at, width), pl.ds(width + at, width)
                out_ref[first + i, 0, 0] = acc_ref[0, rows, real] - acc_ref[1, rows, imag]
                out_ref[first + i, 0, 1] = acc_ref[0, rows, imag] + acc_ref[1, rows, real]
    handed.wait()


def vmem_limit(scratch, blocks):
    held = [x for x in scratch if x.dtype in (jnp.bfloat16, jnp.float32)]
    size = sum(math.prod(x.shape) * jnp.dtype(x.dtype).itemsize for x in held)
    return size + 2 * sum(math.prod(shape) * 4 for shape in blocks) + 2 * 2**20


def make_values(tab, a, gathered):
    supernodes, rows, width = gathered.shape[0], a.shape[1], gathered.shape[2] // 4
    slots = tab.shape[2] + tab.shape[2] % CH
    tile = max(t for t in range(BLK, min(rows, 768) + 1, BLK) if rows % t == 0)
    out_spec = pl.BlockSpec((1, 2, tile, width), lambda k, m, _: (k, 0, m, 0))
    out = pltpu.HBM((supernodes, 2, rows, width), jnp.float32)
    scratch = [
        pltpu.VMEM((2, 2, tile, slots * BLK), jnp.bfloat16),
        pltpu.VMEM(gathered.shape, jnp.bfloat16),
        pltpu.SemaphoreType.DMA((2,)),
        pltpu.SemaphoreType.DMA((supernodes,)),
    ]
    return pl.pallas_call(
        functools.partial(values_kernel, tile),
        out_shape=(out, out),
        grid_spec=pltpu.PrefetchScalarGridSpec(
            num_scalar_prefetch=1,
            grid=(supernodes, rows // tile),
            in_specs=[pl.BlockSpec(memory_space=pl.ANY)] * 2,
            out_specs=(out_spec, out_spec),
            scratch_shapes=scratch,
        ),
        compiler_params=pltpu.CompilerParams(vmem_limit_bytes=vmem_limit(scratch, [(2, tile, width)] * 2)),
        cost_estimate=pl.CostEstimate(
            flops=2 * supernodes * rows * slots * BLK * 4 * width, bytes_accessed=16 * 2**20, transcendentals=0
        ),
        name="values",
    )(tab, a, gathered)


def make_gram(tab, a, stacks, entries, sub, shares):
    supernodes, early_count = stacks[0].shape[:2]
    rows, width = a.shape[1], stacks[0].shape[4]
    slots = tab.shape[2] + tab.shape[2] % CH
    places = min(slots, (rows // BLK) * (BLK // sub))
    places += places % 2
    out = jax.ShapeDtypeStruct((shares, supernodes, 2, 2 * width // shares, width), jnp.float32)
    out_spec = pl.BlockSpec((shares, 1) + out.shape[2:], lambda k, _: (0, k, 0, 0, 0))
    scratch = [
        pltpu.VMEM((supernodes, 2, 2, 2 * BLK, slots * BLK), jnp.bfloat16),
        pltpu.VMEM((supernodes, slots * BLK, 4 * width), jnp.bfloat16),
        pltpu.VMEM((supernodes, places * BLK, 4 * width), jnp.bfloat16),
        pltpu.VMEM((2 * BLK, 4 * width), jnp.float32),
        pltpu.VMEM((3 * 2 * BLK, 4 * width), jnp.bfloat16),
        pltpu.VMEM((2, 2 * width, 4 * width), jnp.float32),
        pltpu.SemaphoreType.DMA((supernodes, 2)),
        pltpu.SemaphoreType.DMA((supernodes,)),
        pltpu.SemaphoreType.DMA((supernodes,)),
        pltpu.SemaphoreType.DMA,
    ]
    return pl.pallas_call(
        functools.partial(gram_kernel, entries, early_count, sub),
        out_shape=(out, out, pltpu.HBM((supernodes, slots * BLK, 4 * width), jnp.bfloat16)),
        grid_spec=pltpu.PrefetchScalarGridSpec(
            num_scalar_prefetch=1,
            grid=(supernodes,),
            in_specs=[pl.BlockSpec(memory_space=pl.ANY)] * 5,
            out_specs=(out_spec, out_spec, pl.BlockSpec(memory_space=pl.ANY)),
            scratch_shapes=scratch,
        ),
        compiler_params=pltpu.CompilerParams(vmem_limit_bytes=vmem_limit(scratch, [out.shape] * 2)),
        cost_estimate=pl.CostEstimate(
            flops=supernodes * 2 * BLK * slots * 2 * BLK * 4 * width, bytes_accessed=8 * 2**20, transcendentals=0
        ),
        name="gram",
    )(tab, a, *stacks)


def scatter_sum(total, n_row, beside):
    half = n_row // 2
    row = lax.axis_index("row")
    level, odd = row // 2, row % 2
    pairs = total.reshape((half, 2) + total.shape[1:])
    came = []
    for d in range(1, half):
        route = [(i, (i + 2 * d) % n_row) for i in range(n_row)]
        sent = lax.dynamic_index_in_dim(pairs, (level + d) % half, 0, keepdims=False)
        came.append(lax.ppermute(sent, "row", route))
    *came, beside = lax.optimization_barrier((*came, beside))
    kept = lax.dynamic_index_in_dim(pairs, level, 0, keepdims=False)
    for x in came:
        kept = kept + x
    route = [(i, i ^ 1) for i in range(n_row)]
    sent = lax.dynamic_index_in_dim(kept, 1 - odd, 0, keepdims=False)
    last, beside = lax.optimization_barrier((lax.ppermute(sent, "row", route), beside))
    return lax.dynamic_index_in_dim(kept, odd, 0, keepdims=False) + last, beside


def place_kernel(n_row, diag_ref, *refs):
    *own, other, out_ref = refs
    half = n_row // 2
    row = lax.axis_index("row")
    level, odd = lax.div(row, 2), lax.rem(row, 2)
    size = own[0].shape[2]
    out_ref[...] = diag_ref[...].astype(jnp.float32)
    for d in range(half):
        base = 2 * lax.rem(level - d + half, half)
        out_ref[:, :, block_at(base + odd, size), :] -= own[d][...]
        out_ref[:, :, block_at(base + 1 - odd, size), :] -= other[d]


def gather_shares(diag_blocks, share, n_row, beside):
    half = n_row // 2
    own = [share]
    for d in range(1, half):
        own.append(lax.ppermute(share, "row", [(i, (i + 2 * d) % n_row) for i in range(n_row)]))
    other = lax.ppermute(jnp.stack(own), "row", [(i, i ^ 1) for i in range(n_row)])
    other, beside = lax.optimization_barrier((other, beside))
    vmem = pl.BlockSpec(memory_space=pltpu.VMEM)
    schur = pl.pallas_call(
        functools.partial(place_kernel, n_row),
        out_shape=jax.ShapeDtypeStruct(diag_blocks.shape, jnp.float32),
        in_specs=[vmem] * (half + 2),
        out_specs=vmem,
        name="place",
    )(diag_blocks, *own, other)
    return schur, beside


def local(n_row, inverse_pairs, factor_rows, diag_blocks, row_lists, block_order):
    supernodes = row_lists.shape[0]
    local_rows, local_cols = inverse_pairs.shape[1:]
    per_chip = factor_rows.shape[2]
    sub = min(BLK, per_chip)
    entries = per_chip // sub
    half = n_row // 2
    cycle = list(range(0, n_row, 2)) + list(range(n_row - 1, 0, -2))
    ahead = [(cycle[i], cycle[(i + 1) % n_row]) for i in range(n_row)]
    behind = [(b, a) for a, b in ahead]
    swap = [(0, 1), (1, 0)]

    tab = make_table(n_row, entries, sub, local_cols // BLK, local_rows // BLK, row_lists, block_order)

    chunks = [[factor_rows[k]] for k in range(supernodes)]
    up = [factor_rows[k] for k in range(supernodes)]
    down = list(up)
    for d in range(1, half):
        for k in range(supernodes):
            up[k] = lax.ppermute(up[k], "row", ahead)
            down[k] = lax.ppermute(down[k], "row", behind)
            chunks[k] += [up[k], down[k]]
        if d == 1:
            up[0], tab = lax.optimization_barrier((up[0], tab))
    for k in range(supernodes):
        last = [lax.ppermute(up[k][0:1], "row", ahead), lax.ppermute(down[k][1:2], "row", behind)]
        chunks[k].append(jnp.concatenate(last, axis=0))
    early = max(1, n_row - 3)
    own = [
        jnp.stack([jnp.stack(chunks[k][:early]) for k in range(supernodes)]),
        jnp.stack([jnp.stack(chunks[k][early:]) for k in range(supernodes)]),
    ]
    stacks = own + [lax.ppermute(x, "col", swap) for x in own]

    mine, theirs, gathered = make_gram(tab, inverse_pairs, stacks, entries, sub, n_row)
    total = mine + lax.ppermute(theirs, "col", swap)
    total, tab = lax.optimization_barrier((total, tab))
    mine, theirs = make_values(tab, inverse_pairs, gathered)
    share, theirs = scatter_sum(total, n_row, theirs)
    values = mine + lax.ppermute(theirs, "col", swap)
    schur, values = gather_shares(diag_blocks, share, n_row, values)
    return (values, schur)


def solution(mesh):
    in_specs = (
        P("pole", "row", "col"),
        P("pole", None, "row", "col"),
        P("pole", None, None, "col"),
        P(),
        P(),
    )
    out_specs = (P("pole", None, "row", "col"), P("pole", None, None, "col"))
    body = functools.partial(local, mesh.shape["row"])
    return jax.shard_map(body, mesh=mesh, in_specs=in_specs, out_specs=out_specs, check_vma=False)
```

```python
import functools
import math

import jax
import jax.numpy as jnp
from jax import lax
from jax.experimental import pallas as pl
from jax.experimental.pallas import tpu as pltpu
from jax.sharding import PartitionSpec as P

BLK = 128
CH = 2
DEPTH = CH * BLK
COL_ENTRY, COL_BLOCK, ROW_ENTRY, ROW_BLOCK, OFFSET, COUNTS = range(6)


def block_at(index, size=BLK):
    return pl.ds(pl.multiple_of(index * size, size), size)


def table_kernel(n_row, entries, sub, col_blocks, row_blocks, lists_ref, order_ref, tab_ref, where_ref):
    half = n_row // 2
    row, core = lax.axis_index("row"), lax.axis_index("col")
    place = jnp.where(lax.rem(row, 2) == 0, lax.div(row, 2), n_row - 1 - lax.div(row, 2))

    def invert(g, carry):
        where_ref[order_ref[g]] = g
        return carry

    lax.fori_loop(0, order_ref.shape[0], invert, 0, unroll=8)
    for k in range(tab_ref.shape[0]):

        def one(i, counts, k=k):
            listed, placed = counts
            chunk, at = lax.div(i, entries), lax.rem(i, entries)
            step = lax.div(chunk + 1, 2)
            step = jnp.where((lax.rem(chunk, 2) == 1) | (chunk == n_row - 1), step, -step)
            source = lax.rem(place - step + 2 * n_row, n_row)
            source = jnp.where(source < half, 2 * source, 2 * (n_row - 1 - source) + 1)
            first = source * (entries * sub) + at * sub
            block = where_ref[lists_ref[k, lax.div(first, BLK)]]
            tab_ref[k, OFFSET, i] = lax.rem(first, BLK)
            col, line = block - core * col_blocks, block - row * row_blocks
            is_col = (col >= 0) & (col < col_blocks)
            is_row = (line >= 0) & (line < row_blocks)

            @pl.when(is_col)
            def _():
                tab_ref[k, COL_ENTRY, listed] = i
                tab_ref[k, COL_BLOCK, listed] = col

            @pl.when(is_row)
            def _():
                tab_ref[k, ROW_ENTRY, placed] = i
                tab_ref[k, ROW_BLOCK, placed] = line

            return listed + is_col.astype(jnp.int32), placed + is_row.astype(jnp.int32)

        listed, placed = lax.fori_loop(0, n_row * entries, one, (jnp.int32(0), jnp.int32(0)), unroll=4)
        tab_ref[k, COUNTS, 0] = listed
        tab_ref[k, COUNTS, 1] = placed
        tab_ref[k, COUNTS, 2] = core


def make_table(n_row, entries, sub, col_blocks, row_blocks, row_lists, block_order):
    smem = pl.BlockSpec(memory_space=pltpu.SMEM)
    return pl.pallas_call(
        functools.partial(table_kernel, n_row, entries, sub, col_blocks, row_blocks),
        out_shape=jax.ShapeDtypeStruct((row_lists.shape[0], 6, max(n_row * entries, 3)), jnp.int32),
        in_specs=[smem] * 2,
        out_specs=smem,
        scratch_shapes=[pltpu.SMEM(block_order.shape, jnp.int32)],
        name="table",
    )(row_lists, block_order)


def start_rows(tab_ref, kind, k, to_ref, sems, halves, entries, early_count, sub):
    def one(at, carry):
        entry = tab_ref[k, kind, at]
        chunk, part = lax.div(entry, entries), lax.rem(entry, entries)
        rows = block_at(at)
        if sub < BLK:
            to_ref[k, rows, :] = jnp.zeros((BLK, to_ref.shape[2]), to_ref.dtype)
            rows = pl.ds(pl.multiple_of(at * BLK + tab_ref[k, OFFSET, entry], sub), sub)

        def copy(stack, chunk, there, p):
            here = stack.at[k, chunk, p, block_at(part, sub), :]
            pltpu.make_async_copy(here, there, sems.at[k]).start()

        for half, stacks in enumerate(halves):
            width = stacks[0].shape[4]
            for p in range(2):
                there = to_ref.at[k, rows, pl.ds((2 * half + p) * width, width)]

                @pl.when(chunk < early_count)
                def _(stacks=stacks, there=there, p=p):
                    copy(stacks[0], chunk, there, p)

                @pl.when(chunk >= early_count)
                def _(stacks=stacks, there=there, p=p):
                    copy(stacks[1], chunk - early_count, there, p)

        return carry

    return one


def wait_rows(k, to_ref, sems, width, sub, halves):
    def one(at, carry):
        there = to_ref.at[k, pl.ds(0, sub), pl.ds(0, 2 * halves * width)]
        pltpu.make_async_copy(there, there, sems.at[k]).wait()
        return carry

    return one


def product(x, w, x_rows, depth):
    width = w.shape[1] // 2
    real, imag = (
        jnp.dot(x[p, x_rows, depth], w[depth, :], preferred_element_type=jnp.float32) for p in range(2)
    )
    return imag[:, width:] - real[:, :width], -(real[:, width:] + imag[:, :width])


def values_kernel(tile, tab_ref, a_ref, rows_ref, mine_ref, theirs_ref, x_ref, w_ref, x_sems, w_sems):
    k, step = pl.program_id(0), pl.program_id(1)
    supernodes, tiles = pl.num_programs(0), pl.num_programs(1)
    width = mine_ref.shape[3]
    listed = tab_ref[k, COUNTS, 0]
    now = k * tiles + step

    def start(at):
        which, rows, buffer = lax.div(at, tiles), lax.rem(at, tiles), lax.rem(at, 2)

        def one(slot, carry):
            pltpu.make_async_copy(
                a_ref.at[:, block_at(rows, tile), block_at(tab_ref[which, COL_BLOCK, slot])],
                x_ref.at[buffer, :, :, block_at(slot)],
                x_sems.at[buffer],
            ).start()
            return carry

        lax.fori_loop(0, tab_ref[which, COUNTS, 0], one, 0)

    def weights(which):
        return pltpu.make_async_copy(rows_ref.at[which], w_ref.at[which], w_sems.at[which])

    @pl.when(now == 0)
    def _():
        start(now)
        for which in range(w_ref.shape[0]):
            weights(which).start()

    @pl.when(now + 1 < supernodes * tiles)
    def _():
        start(now + 1)

    @pl.when(step == 0)
    def _():
        weights(k).wait()

    buffer = lax.rem(now, 2)

    @pl.when(lax.rem(listed, CH) != 0)
    def _():
        x_ref[buffer, :, :, block_at(listed)] = jnp.zeros((2, tile, BLK), x_ref.dtype)

    def arrived(slot, carry):
        there = x_ref.at[buffer, :, :, block_at(slot)]
        pltpu.make_async_copy(there, there, x_sems.at[buffer]).wait()
        return carry

    lax.fori_loop(0, listed, arrived, 0)
    steps = lax.div(listed + (CH - 1), CH)

    @pl.when(steps == 0)
    def _():
        mine_ref[...] = jnp.zeros_like(mine_ref)
        theirs_ref[...] = jnp.zeros_like(theirs_ref)

    for count in range(1, w_ref.shape[1] // DEPTH + 1):

        @pl.when(steps == count)
        def _(count=count):
            for half, out_ref in enumerate((mine_ref, theirs_ref)):
                columns = w_ref.at[k, :, pl.ds(2 * half * width, 2 * width)]
                parts = product(x_ref.at[buffer], columns, pl.ds(0, tile), pl.ds(0, count * DEPTH))
                for q in range(2):
                    out_ref[0, q] = parts[q]


def gram_kernel(entries, early_count, sub, tab_ref, a_ref, own0, own1, sib0, sib1, *refs):
    mine_ref, theirs_ref, rows_ref, x_ref, w_ref, l_ref, v_ref, r_ref, acc_ref, x_sems, w_sems, l_sems, out_sem = refs
    k = pl.program_id(0)
    own, sib = (own0, own1), (sib0, sib1)
    width = mine_ref.shape[4]
    chunk_rows = mine_ref.shape[3]
    listed, placed = tab_ref[k, COUNTS, 0], tab_ref[k, COUNTS, 1]

    def start_pair(which, pair):
        def one_place(place, carry):
            rows = block_at(tab_ref[which, ROW_BLOCK, place])

            def one(slot, inner):
                pltpu.make_async_copy(
                    a_ref.at[:, rows, block_at(tab_ref[which, COL_BLOCK, slot])],
                    x_ref.at[which, lax.rem(pair, 2), :, block_at(place - 2 * pair), block_at(slot)],
                    x_sems.at[which, lax.rem(pair, 2)],
                ).start()
                return inner

            return lax.fori_loop(0, tab_ref[which, COUNTS, 0], one, carry)

        lax.fori_loop(2 * pair, jnp.minimum(2 * pair + 2, tab_ref[which, COUNTS, 1]), one_place, 0)

    @pl.when(k == 0)
    def _():
        for which in range(x_ref.shape[0]):
            stacks = ((own, sib), entries, early_count, sub)
            there = tab_ref[which, COUNTS, 1]
            start_pair(which, 0)
            lax.fori_loop(
                0, tab_ref[which, COUNTS, 0], start_rows(tab_ref, COL_ENTRY, which, w_ref, w_sems, *stacks), 0
            )
            lax.fori_loop(0, there, start_rows(tab_ref, ROW_ENTRY, which, l_ref, l_sems, *stacks), 0)

    acc_ref[...] = jnp.zeros_like(acc_ref)
    odd = lax.rem(listed, CH) != 0
    steps = lax.div(listed + (CH - 1), CH)
    lax.fori_loop(0, listed, wait_rows(k, w_ref, w_sems, width, sub, 2), 0)

    @pl.when(odd)
    def _():
        w_ref[k, block_at(listed), :] = jnp.zeros((BLK, w_ref.shape[2]), w_ref.dtype)

    handed = pltpu.make_async_copy(w_ref.at[k], rows_ref.at[k], out_sem)
    handed.start()
    lax.fori_loop(0, placed, wait_rows(k, l_ref, l_sems, width, sub, 2), 0)

    def one_group(places, pair, carry):
        start_pair(k, pair + 1)
        buffer, rows = lax.rem(pair, 2), places * BLK

        @pl.when(odd)
        def _():
            x_ref[k, buffer, :, pl.ds(0, rows), block_at(listed)] = jnp.zeros((2, rows, BLK), x_ref.dtype)

        def arrived(slot, inner):
            for place in range(places):
                there = x_ref.at[k, buffer, :, pl.ds(place * BLK, BLK), block_at(slot)]
                pltpu.make_async_copy(there, there, x_sems.at[k, buffer]).wait()
            return inner

        lax.fori_loop(0, listed, arrived, 0)
        for count in range(1, w_ref.shape[1] // DEPTH + 1):

            @pl.when(steps == count)
            def _(count=count):
                for half in range(2):
                    columns = w_ref.at[k, :, pl.ds(2 * half * width, 2 * width)]
                    parts = product(x_ref.at[k, buffer], columns, pl.ds(0, rows), pl.ds(0, count * DEPTH))
                    for q in range(2):
                        v_ref[pl.ds(0, rows), pl.ds((2 * half + q) * width, width)] = parts[q]

        rest = v_ref[pl.ds(0, rows), :]
        for piece in range(3):
            kept = rest.astype(jnp.bfloat16)
            r_ref[pl.ds(piece * rows, rows), :] = kept
            rest = rest - kept.astype(jnp.float32)
        left = l_ref[k, pl.ds(pl.multiple_of(pair * 2 * BLK, 2 * BLK), rows), :]
        for p in range(2):
            turned = jnp.concatenate(
                [left[:, (2 * h + p) * width : (2 * h + p + 1) * width].T for h in range(2)], axis=0
            )
            turned = jnp.concatenate([turned] * 3, axis=1)
            acc_ref[p] += jnp.dot(turned, r_ref[pl.ds(0, 3 * rows), :], preferred_element_type=jnp.float32)
        return carry

    @pl.when((listed > 0) & (placed > 0))
    def _():
        pairs = lax.div(placed, 2)
        lax.fori_loop(0, pairs, functools.partial(one_group, 2), 0)

        @pl.when(lax.rem(placed, 2) != 0)
        def _():
            one_group(1, pairs, 0)

    core = tab_ref[0, COUNTS, 2]
    per_half = width // chunk_rows
    for half in range(2):
        first = (core if half == 0 else 1 - core) * per_half
        for i in range(per_half):
            rows = pl.ds(half * width + i * chunk_rows, chunk_rows)
            for out_ref, at in ((mine_ref, 0), (theirs_ref, 2 * width)):
                real, imag = pl.ds(at, width), pl.ds(width + at, width)
                out_ref[first + i, 0, 0] = acc_ref[0, rows, real] - acc_ref[1, rows, imag]
                out_ref[first + i, 0, 1] = acc_ref[0, rows, imag] + acc_ref[1, rows, real]
    handed.wait()


def vmem_limit(scratch, blocks):
    held = [x for x in scratch if x.dtype in (jnp.bfloat16, jnp.float32)]
    size = sum(math.prod(x.shape) * jnp.dtype(x.dtype).itemsize for x in held)
    return size + 2 * sum(math.prod(shape) * 4 for shape in blocks) + 2 * 2**20


def make_values(tab, a, gathered):
    supernodes, rows, width = gathered.shape[0], a.shape[1], gathered.shape[2] // 4
    slots = tab.shape[2] + tab.shape[2] % CH
    tile = max(t for t in range(BLK, min(rows, 768) + 1, BLK) if rows % t == 0)
    out_spec = pl.BlockSpec((1, 2, tile, width), lambda k, m, _: (k, 0, m, 0))
    out = pltpu.HBM((supernodes, 2, rows, width), jnp.float32)
    scratch = [
        pltpu.VMEM((2, 2, tile, slots * BLK), jnp.bfloat16),
        pltpu.VMEM(gathered.shape, jnp.bfloat16),
        pltpu.SemaphoreType.DMA((2,)),
        pltpu.SemaphoreType.DMA((supernodes,)),
    ]
    return pl.pallas_call(
        functools.partial(values_kernel, tile),
        out_shape=(out, out),
        grid_spec=pltpu.PrefetchScalarGridSpec(
            num_scalar_prefetch=1,
            grid=(supernodes, rows // tile),
            in_specs=[pl.BlockSpec(memory_space=pl.ANY)] * 2,
            out_specs=(out_spec, out_spec),
            scratch_shapes=scratch,
        ),
        compiler_params=pltpu.CompilerParams(vmem_limit_bytes=60 * 2**20),
        cost_estimate=pl.CostEstimate(
            flops=2 * supernodes * rows * slots * BLK * 4 * width, bytes_accessed=16 * 2**20, transcendentals=0
        ),
        name="values",
    )(tab, a, gathered)


def make_gram(tab, a, stacks, entries, sub, shares):
    supernodes, early_count = stacks[0].shape[:2]
    rows, width = a.shape[1], stacks[0].shape[4]
    slots = tab.shape[2] + tab.shape[2] % CH
    places = min(slots, (rows // BLK) * (BLK // sub))
    places += places % 2
    out = jax.ShapeDtypeStruct((shares, supernodes, 2, 2 * width // shares, width), jnp.float32)
    out_spec = pl.BlockSpec((shares, 1) + out.shape[2:], lambda k, _: (0, k, 0, 0, 0))
    scratch = [
        pltpu.VMEM((supernodes, 2, 2, 2 * BLK, slots * BLK), jnp.bfloat16),
        pltpu.VMEM((supernodes, slots * BLK, 4 * width), jnp.bfloat16),
        pltpu.VMEM((supernodes, places * BLK, 4 * width), jnp.bfloat16),
        pltpu.VMEM((2 * BLK, 4 * width), jnp.float32),
        pltpu.VMEM((3 * 2 * BLK, 4 * width), jnp.bfloat16),
        pltpu.VMEM((2, 2 * width, 4 * width), jnp.float32),
        pltpu.SemaphoreType.DMA((supernodes, 2)),
        pltpu.SemaphoreType.DMA((supernodes,)),
        pltpu.SemaphoreType.DMA((supernodes,)),
        pltpu.SemaphoreType.DMA,
    ]
    return pl.pallas_call(
        functools.partial(gram_kernel, entries, early_count, sub),
        out_shape=(out, out, pltpu.HBM((supernodes, slots * BLK, 4 * width), jnp.bfloat16)),
        grid_spec=pltpu.PrefetchScalarGridSpec(
            num_scalar_prefetch=1,
            grid=(supernodes,),
            in_specs=[pl.BlockSpec(memory_space=pl.ANY)] * 5,
            out_specs=(out_spec, out_spec, pl.BlockSpec(memory_space=pl.ANY)),
            scratch_shapes=scratch,
        ),
        compiler_params=pltpu.CompilerParams(vmem_limit_bytes=vmem_limit(scratch, [out.shape] * 2)),
        cost_estimate=pl.CostEstimate(
            flops=supernodes * 2 * BLK * slots * 2 * BLK * 4 * width, bytes_accessed=8 * 2**20, transcendentals=0
        ),
        name="gram",
    )(tab, a, *stacks)


def scatter_sum(total, n_row, beside):
    half = n_row // 2
    row = lax.axis_index("row")
    level, odd = row // 2, row % 2
    pairs = total.reshape((half, 2) + total.shape[1:])
    came = []
    for d in range(1, half):
        route = [(i, (i + 2 * d) % n_row) for i in range(n_row)]
        sent = lax.dynamic_index_in_dim(pairs, (level + d) % half, 0, keepdims=False)
        came.append(lax.ppermute(sent, "row", route))
    *came, beside = lax.optimization_barrier((*came, beside))
    kept = lax.dynamic_index_in_dim(pairs, level, 0, keepdims=False)
    for x in came:
        kept = kept + x
    route = [(i, i ^ 1) for i in range(n_row)]
    sent = lax.dynamic_index_in_dim(kept, 1 - odd, 0, keepdims=False)
    last, beside = lax.optimization_barrier((lax.ppermute(sent, "row", route), beside))
    return lax.dynamic_index_in_dim(kept, odd, 0, keepdims=False) + last, beside


def place_kernel(n_row, diag_ref, *refs):
    *own, other, out_ref = refs
    half = n_row // 2
    row = lax.axis_index("row")
    level, odd = lax.div(row, 2), lax.rem(row, 2)
    size = own[0].shape[2]
    out_ref[...] = diag_ref[...].astype(jnp.float32)
    for d in range(half):
        base = 2 * lax.rem(level - d + half, half)
        out_ref[:, :, block_at(base + odd, size), :] -= own[d][...]
        out_ref[:, :, block_at(base + 1 - odd, size), :] -= other[d]


def gather_shares(diag_blocks, share, n_row, beside):
    half = n_row // 2
    own = [share]
    for d in range(1, half):
        own.append(lax.ppermute(share, "row", [(i, (i + 2 * d) % n_row) for i in range(n_row)]))
    other = lax.ppermute(jnp.stack(own), "row", [(i, i ^ 1) for i in range(n_row)])
    other, beside = lax.optimization_barrier((other, beside))
    vmem = pl.BlockSpec(memory_space=pltpu.VMEM)
    schur = pl.pallas_call(
        functools.partial(place_kernel, n_row),
        out_shape=jax.ShapeDtypeStruct(diag_blocks.shape, jnp.float32),
        in_specs=[vmem] * (half + 2),
        out_specs=vmem,
        compiler_params=pltpu.CompilerParams(vmem_limit_bytes=6 * 2**20),
        name="place",
    )(diag_blocks, *own, other)
    return schur, beside


def local(n_row, inverse_pairs, factor_rows, diag_blocks, row_lists, block_order):
    supernodes = row_lists.shape[0]
    local_rows, local_cols = inverse_pairs.shape[1:]
    per_chip = factor_rows.shape[2]
    sub = min(BLK, per_chip)
    entries = per_chip // sub
    half = n_row // 2
    cycle = list(range(0, n_row, 2)) + list(range(n_row - 1, 0, -2))
    ahead = [(cycle[i], cycle[(i + 1) % n_row]) for i in range(n_row)]
    behind = [(b, a) for a, b in ahead]
    swap = [(0, 1), (1, 0)]

    tab = make_table(n_row, entries, sub, local_cols // BLK, local_rows // BLK, row_lists, block_order)

    chunks = [[factor_rows[k]] for k in range(supernodes)]
    up = [factor_rows[k] for k in range(supernodes)]
    down = list(up)
    for d in range(1, half):
        for k in range(supernodes):
            up[k] = lax.ppermute(up[k], "row", ahead)
            down[k] = lax.ppermute(down[k], "row", behind)
            chunks[k] += [up[k], down[k]]
        if d == 1:
            up[0], tab = lax.optimization_barrier((up[0], tab))
    for k in range(supernodes):
        last = [lax.ppermute(up[k][0:1], "row", ahead), lax.ppermute(down[k][1:2], "row", behind)]
        chunks[k].append(jnp.concatenate(last, axis=0))
    early = max(1, n_row - 3)
    own = [
        jnp.stack([jnp.stack(chunks[k][:early]) for k in range(supernodes)]),
        jnp.stack([jnp.stack(chunks[k][early:]) for k in range(supernodes)]),
    ]
    stacks = own + [lax.ppermute(x, "col", swap) for x in own]

    mine, theirs, gathered = make_gram(tab, inverse_pairs, stacks, entries, sub, n_row)
    total = mine + lax.ppermute(theirs, "col", swap)
    total, tab = lax.optimization_barrier((total, tab))
    mine, theirs = make_values(tab, inverse_pairs, gathered)
    share, theirs = scatter_sum(total, n_row, theirs)
    values = mine + lax.ppermute(theirs, "col", swap)
    schur, values = gather_shares(diag_blocks, share, n_row, values)
    return (values, schur)


def solution(mesh):
    in_specs = (
        P("pole", "row", "col"),
        P("pole", None, "row", "col"),
        P("pole", None, None, "col"),
        P(),
        P(),
    )
    out_specs = (P("pole", None, "row", "col"), P("pole", None, None, "col"))
    body = functools.partial(local, mesh.shape["row"])
    return jax.shard_map(body, mesh=mesh, in_specs=in_specs, out_specs=out_specs, check_vma=False)
```
